32 devices in a mesh: adjust: 2 (over y), hid: 16 (over z, x, core).
Axes of the slice: x: 2, y: 2, z: 4, core: 2. Of those that a mesh axis runs over, the one named last changes fastest.
Arguments:
- tokens: bfloat16 [1024, 4096], P(('adjust', 'hid')), parts along dimension 0, may hold values from -6 to 6
- grad_out: bfloat16 [1024, 4096], P(('adjust', 'hid')), parts along dimension 0, may hold values from -3 to 3
- gate_weight: bfloat16 [8192, 28672], P('adjust', 'hid'), parts along dimension 0, may hold values from -0.09375 to 0.09375
- up_weight: bfloat16 [8192, 28672], P('adjust', 'hid'), parts along dimension 0, may hold values from -0.09375 to 0.09375
- down_weight: bfloat16 [57344, 4096], P(('adjust', 'hid')), parts along dimension 0, may hold values from -0.03125 to 0.03125
Outputs:
- fisher_gate: bfloat16 [8192, 28672], P('adjust', 'hid'), parts along dimension 0
- fisher_up: bfloat16 [8192, 28672], P('adjust', 'hid'), parts along dimension 0
- input_grad: bfloat16 [1024, 4096], P(('adjust', 'hid')), parts along dimension 0
The draws below stay inside these ranges and needn't reach their ends.
There are 2 independent parts, one for each index of `adjust`. The reference program is written for one: setup_inputs(seed, part) draws one part's arguments, and reference() takes and returns one part's arrays. A program takes and returns all parts, laid end to end along the dimension named above; each array names one. Nothing has to cross between parts.
All inputs are finite; a program needn't handle non-finite values.
Results may differ from the reference program's by a relative error of at most 0.0058.
Values may be sent and summed in bfloat16 or wider, within the bound.
No kernel may reach another device: no remote copies, remote signals or barrier semaphores. Data moves between devices by JAX's collectives and lax.ppermute only.
A program may use at most 192 MiB of HBM per device.

```python
import jax
import jax.numpy as jnp
from jax import lax

D = 4096
FF = 28672
SEQS = 2
SEQ_LEN = 256
TOKENS = 512


def block_scale(rng, shape, pieces, least, high):
    def one(dim, parts):
        draws = jax.random.uniform(jax.random.fold_in(jax.random.fold_in(rng, 6), dim), (parts,), jnp.float32, least / len(pieces), high / len(pieces))
        return jnp.repeat(jnp.exp(draws), shape[dim] // parts).reshape((-1,) + (1,) * (len(shape) - dim - 1))

    gain = one(*pieces[0])
    for cut in pieces[1:]:
        gain = gain * one(*cut)
    return gain


def scatter_about(key, extent, scale, most, split=(), kind=jnp.bfloat16):
    gain = block_scale(key, extent, split, -0.22, 0.18) if split else 1.0
    entries = jax.random.normal(key, extent, jnp.float32) * scale * gain
    return jnp.minimum(jnp.maximum(entries, -most), most).astype(kind)


def setup_inputs(seed: int = 0, part: int = 0) -> dict:
    key_list = jax.random.split(jax.random.key(seed), 6)
    part_keys = jax.random.split(jax.random.fold_in(key_list[5], part), 6)
    tokens = scatter_about(part_keys[0], (TOKENS, D), 1.0, 6.0, ((0, 16),))
    grad_out = scatter_about(part_keys[1], (TOKENS, D), 0.5, 3.0, ((0, 16),))
    gate_weight = scatter_about(part_keys[2], (D, FF), D ** -0.5, 0.09375, ((1, 16),))
    up_weight = scatter_about(part_keys[3], (D, FF), D ** -0.5, 0.09375, ((1, 16),))
    down_weight = scatter_about(part_keys[4], (FF, D), FF ** -0.5, 0.03125, ((0, 16),))
    return {"tokens": tokens, "grad_out": grad_out, "gate_weight": gate_weight, "up_weight": up_weight, "down_weight": down_weight}


def reference(tokens, grad_out, gate_weight, up_weight, down_weight):
    gate = jnp.dot(tokens, gate_weight, preferred_element_type=jnp.float32)
    up = jnp.dot(tokens, up_weight, preferred_element_type=jnp.float32)
    hidden_grad = lax.dot_general(grad_out, down_weight, (((1,), (1,)), ((), ())), preferred_element_type=jnp.float32)
    sigma = jax.nn.sigmoid(gate)
    grad_gate = (hidden_grad * up * sigma * (1.0 + gate * (1.0 - sigma))).astype(jnp.bfloat16)
    grad_up = (hidden_grad * gate * sigma).astype(jnp.bfloat16)
    fisher_gate = jnp.zeros(gate_weight.shape, jnp.bfloat16)
    fisher_up = jnp.zeros(up_weight.shape, jnp.bfloat16)
    for index in range(SEQS):
        rows = tokens[index * SEQ_LEN:(index + 1) * SEQ_LEN]
        seq_gate = lax.dot_general(rows, grad_gate[index * SEQ_LEN:(index + 1) * SEQ_LEN], (((0,), (0,)), ((), ())), preferred_element_type=jnp.float32)
        seq_up = lax.dot_general(rows, grad_up[index * SEQ_LEN:(index + 1) * SEQ_LEN], (((0,), (0,)), ((), ())), preferred_element_type=jnp.float32)
        fisher_gate = (fisher_gate.astype(jnp.float32) + seq_gate * seq_gate * (1.0 / SEQS)).astype(jnp.bfloat16)
        fisher_up = (fisher_up.astype(jnp.float32) + seq_up * seq_up * (1.0 / SEQS)).astype(jnp.bfloat16)
    total = lax.dot_general(grad_gate, gate_weight, (((1,), (1,)), ((), ())), preferred_element_type=jnp.float32)
    total = total + lax.dot_general(grad_up, up_weight, (((1,), (1,)), ((), ())), preferred_element_type=jnp.float32)
    return fisher_gate, fisher_up, total.astype(jnp.bfloat16)
```

```python
import functools

import jax
import jax.numpy as jnp
from jax import lax
from jax.experimental import pallas as pl
from jax.experimental.pallas import tpu as pltpu
from jax.sharding import PartitionSpec as P

SEQS = 2
MIB = 1 << 20
NT = (((1,), (1,)), ((), ()))
TN = (((0,), (0,)), ((), ()))


def tile(size, want):
    return want if size % want == 0 else size


def params(mib):
    return pltpu.CompilerParams(vmem_limit_bytes=mib * MIB)


def cost(flops, read):
    return pl.CostEstimate(flops=flops, bytes_accessed=read, transcendentals=0)


def forward_kernel(x_ref, wg_ref, wu_ref, gate_ref, up_ref):
    x = x_ref[...]
    gate_ref[...] = jnp.dot(x, wg_ref[...], preferred_element_type=jnp.float32)
    up_ref[...] = jnp.dot(x, wu_ref[...], preferred_element_type=jnp.float32)


def forward(x, wg, wu):
    rows, depth = x.shape
    width = wg.shape[1]
    step = tile(width, 256)
    return pl.pallas_call(
        forward_kernel,
        grid=(width // step,),
        in_specs=[
            pl.BlockSpec((rows, depth), lambda j: (0, 0)),
            pl.BlockSpec((depth, step), lambda j: (0, j)),
            pl.BlockSpec((depth, step), lambda j: (0, j)),
        ],
        out_specs=[pl.BlockSpec((rows, step), lambda j: (0, j))] * 2,
        out_shape=[jax.ShapeDtypeStruct((rows, width), jnp.float32)] * 2,
        compiler_params=params(40),
        cost_estimate=cost(4 * rows * depth * width, 4 * depth * width),
        name="gate_up",
    )(x, wg, wu)


def back_kernel(parts, dy_ref, wd_ref, gate_ref, up_ref, gg_ref, gu_ref):
    rows = dy_ref.shape[0] // parts
    for p in range(parts):
        at = pl.ds(p * rows, rows)
        hidden = lax.dot_general(dy_ref[at, :], wd_ref[...], NT, preferred_element_type=jnp.float32)
        gate = gate_ref[at, :]
        sigma = jax.nn.sigmoid(gate)
        both = hidden * sigma
        gg_ref[at, :] = (both * up_ref[at, :] * (1.0 + gate * (1.0 - sigma))).astype(jnp.bfloat16)
        gu_ref[at, :] = (both * gate).astype(jnp.bfloat16)


def back(dy, wd, gate, up):
    rows, depth = dy.shape
    width = wd.shape[0]
    step = tile(width, 256)
    column = pl.BlockSpec((rows, step), lambda j: (0, j))
    return pl.pallas_call(
        functools.partial(back_kernel, 2),
        grid=(width // step,),
        in_specs=[
            pl.BlockSpec((rows, depth), lambda j: (0, 0)),
            pl.BlockSpec((step, depth), lambda j: (j, 0)),
            column,
            column,
        ],
        out_specs=[column, column],
        out_shape=[jax.ShapeDtypeStruct((rows, width), jnp.bfloat16)] * 2,
        compiler_params=params(40),
        cost_estimate=cost(2 * rows * depth * width, 2 * depth * width),
        name="hidden_back",
    )(dy, wd, gate, up)


def input_kernel(gg_ref, gu_ref, wg_ref, wu_ref, out_ref):
    total = lax.dot_general(gg_ref[...], wg_ref[...], NT, preferred_element_type=jnp.float32)
    total += lax.dot_general(gu_ref[...], wu_ref[...], NT, preferred_element_type=jnp.float32)
    out_ref[...] = total.astype(jnp.bfloat16)


def input_terms(gg, gu, wg, wu):
    rows, width = gg.shape
    depth = wg.shape[0]
    step = 512
    held = pl.BlockSpec((rows, width), lambda j: (0, 0))
    return pl.pallas_call(
        input_kernel,
        grid=(depth // step,),
        in_specs=[
            held,
            held,
            pl.BlockSpec((step, width), lambda j: (j, 0)),
            pl.BlockSpec((step, width), lambda j: (j, 0)),
        ],
        out_specs=pl.BlockSpec((rows, step), lambda j: (0, j)),
        out_shape=jax.ShapeDtypeStruct((rows, depth), jnp.bfloat16),
        compiler_params=params(40),
        cost_estimate=cost(4 * rows * depth * width, 4 * depth * width),
        name="input_terms",
    )(gg, gu, wg, wu)


def fisher_kernel(step, x_ref, gg_ref, gu_ref, fg_ref, fu_ref):
    half = x_ref.shape[0] // 2
    span = half // SEQS
    width = gg_ref.shape[1]

    def rows(ref, q, at):
        near = ref[pl.ds(q * span, span), at]
        far = ref[pl.ds(half + q * span, span), at]
        return jnp.concatenate([near, far], axis=0)

    xs = [rows(x_ref, q, slice(None)).T for q in range(SEQS)]
    for g_ref, f_ref in ((gg_ref, fg_ref), (gu_ref, fu_ref)):
        for c in range(width // step):
            at = pl.ds(c * step, step)
            total = None
            for q in range(SEQS):
                seq = jnp.dot(xs[q], rows(g_ref, q, at), preferred_element_type=jnp.float32)
                total = seq * seq if total is None else total + seq * seq
            f_ref[:, at] = (total * (1.0 / SEQS)).astype(jnp.bfloat16)


def fisher(x, gg, gu):
    rows, depth = x.shape
    width = gg.shape[1]
    step = 512
    held = pl.BlockSpec((rows, width), lambda j: (0, 0))
    block = pl.BlockSpec((step, width), lambda j: (j, 0))
    return pl.pallas_call(
        functools.partial(fisher_kernel, tile(width, 256)),
        grid=(depth // step,),
        in_specs=[pl.BlockSpec((rows, step), lambda j: (0, j)), held, held],
        out_specs=[block, block],
        out_shape=[jax.ShapeDtypeStruct((depth, width), jnp.bfloat16)] * 2,
        compiler_params=params(40),
        cost_estimate=cost(4 * rows * depth * width, 4 * depth * width),
        name="fisher",
    )(x, gg, gu)


def per_device(size, tokens, grad_out, wg, wu, wd):
    chips = size // 2
    across = [[2 * i + c for i in range(chips)] for c in range(2)]
    pairs = [[2 * i, 2 * i + 1] for i in range(chips)]
    block, depth = tokens.shape

    def gather(rows):
        near = lax.all_gather(rows, "hid", axis=0, tiled=True, axis_index_groups=across)
        return lax.all_gather(near, "hid", axis=0, tiled=False, axis_index_groups=pairs)

    x = gather(tokens).reshape(-1, depth)
    dy = gather(grad_out).reshape(-1, depth)
    gate, up = forward(x, wg, wu)
    gg, gu = back(dy, wd, gate, up)
    terms = input_terms(gg, gu, wg, wu).reshape(2, -1, depth)
    mine = lax.psum_scatter(
        terms, "hid", scatter_dimension=0, tiled=False, axis_index_groups=pairs
    )
    mine = lax.psum_scatter(
        mine, "hid", scatter_dimension=0, tiled=True, axis_index_groups=across
    )
    fg, fu = fisher(x, gg, gu)
    return fg, fu, mine


def solution(mesh):
    rows = P(("adjust", "hid"), None)
    weights = P("adjust", "hid")
    return jax.shard_map(
        functools.partial(per_device, mesh.shape["hid"]),
        mesh=mesh,
        in_specs=(rows, rows, weights, weights, rows),
        out_specs=(weights, weights, rows),
        check_vma=False,
    )
```

```python
import functools

import jax
import jax.numpy as jnp
from jax import lax
from jax.experimental import pallas as pl
from jax.experimental.pallas import tpu as pltpu
from jax.sharding import PartitionSpec as P

SEQS = 2
MIB = 1 << 20
CYCLE = (0, 2, 4, 6, 7, 5, 3, 1)
NT = (((1,), (1,)), ((), ()))
BF16 = jnp.bfloat16
F32 = jnp.float32


def tile(size, want):
    return want if size % want == 0 else size


def params(mib):
    return pltpu.CompilerParams(vmem_limit_bytes=mib * MIB)


def cost(flops, read):
    return pl.CostEstimate(flops=flops, bytes_accessed=read, transcendentals=0)


def silu_grads(hidden, gate, up):
    sigma = jax.nn.sigmoid(gate)
    both = hidden * sigma
    gg = both * up * (1.0 + gate * (1.0 - sigma))
    return gg.astype(BF16), (both * gate).astype(BF16)


def forward_kernel(near_ref, far_ref, wg_ref, wu_ref, wd_ref, *rest):
    gg_ref, gu_ref = rest[-2:]
    half = near_ref.shape[0] // 2
    x = jnp.concatenate([near_ref[:half, :], far_ref[:half, :]], axis=0)
    dy = jnp.concatenate([near_ref[half:, :], far_ref[half:, :]], axis=0)
    gate = jnp.dot(x, wg_ref[...], preferred_element_type=F32)
    up = jnp.dot(x, wu_ref[...], preferred_element_type=F32)
    hidden = lax.dot_general(dy, wd_ref[...], NT, preferred_element_type=F32)
    gg_ref[...], gu_ref[...] = silu_grads(hidden, gate, up)


def forward(near, far, wg, wu, wd, first, count, step, held=(), after=()):
    rows, depth = near.shape
    width = wg.shape[1]
    whole = pl.BlockSpec((rows, depth), lambda j: (0, 0))
    column = pl.BlockSpec((depth, step), lambda j: (0, first + j))
    out = pl.BlockSpec((rows, step), lambda j: (0, first + j))
    return pl.pallas_call(
        forward_kernel,
        grid=(count,),
        in_specs=[
            whole,
            whole,
            column,
            column,
            pl.BlockSpec((step, depth), lambda j: (first + j, 0)),
        ]
        + [pl.BlockSpec(memory_space=pl.ANY)] * len((*held, *after)),
        out_specs=[out, out],
        out_shape=[jax.ShapeDtypeStruct((rows, width), BF16)] * 2,
        input_output_aliases={5 + i: i for i in range(len(held))},
        compiler_params=params(56),
        cost_estimate=cost(6 * rows * depth * count * step, 6 * depth * count * step),
        name="forward",
    )(near, far, wg, wu, wd, *held, *after)


def input_kernel(gg_ref, gu_ref, wg_ref, wu_ref, *rest):
    own_ref, far_ref = rest[-2:]
    total = lax.dot_general(gg_ref[...], wg_ref[...], NT, preferred_element_type=F32)
    total += lax.dot_general(gu_ref[...], wu_ref[...], NT, preferred_element_type=F32)
    half = own_ref.shape[0]
    own_ref[...] = total[:half, :]
    far_ref[...] = total[half:, :].astype(BF16)


def input_terms(gg, gu, wg, wu, first, count, step, held=(), after=()):
    rows, width = gg.shape
    depth = wg.shape[0]
    whole = pl.BlockSpec((rows, width), lambda j: (0, 0))
    weight = pl.BlockSpec((step, width), lambda j: (first + j, 0))
    out = pl.BlockSpec((rows // 2, step), lambda j: (0, first + j))
    return pl.pallas_call(
        input_kernel,
        grid=(count,),
        in_specs=[whole, whole, weight, weight]
        + [pl.BlockSpec(memory_space=pl.ANY)] * len((*held, *after)),
        out_specs=[out, out],
        out_shape=[
            jax.ShapeDtypeStruct((rows // 2, depth), F32),
            jax.ShapeDtypeStruct((rows // 2, depth), BF16),
        ],
        input_output_aliases={4 + i: i for i in range(len(held))},
        compiler_params=params(56),
        cost_estimate=cost(4 * rows * width * count * step, 4 * width * count * step),
        name="input_terms",
    )(gg, gu, wg, wu, *held, *after)


def fisher_kernel(step, row, at_ref, *refs):
    xs, gates, ups = refs[:4], refs[4:6], refs[6:8]
    fg_ref, fu_ref = refs[-2:]
    spots = at_ref.shape[0] // SEQS
    width = fg_ref.shape[1]

    def pick(pieces, q, at):
        blocks = []
        for ref, base in pieces:
            for i in range(spots):
                start = pl.multiple_of(base + at_ref[q * spots + i] * row, row)
                blocks.append(ref[pl.ds(start, row), at])
        return jnp.concatenate(blocks, axis=0)

    lots = [[(x, 0) for x in xs]]
    for chunks in (gates, ups):
        lots.append([(g, h * g.shape[0] // 2) for g in chunks for h in range(2)])
    cols = [pick(lots[0], q, slice(None)).T for q in range(SEQS)]
    for lot, f_ref in ((lots[1], fg_ref), (lots[2], fu_ref)):
        for c in range(width // step):
            at = pl.ds(c * step, step)
            total = None
            for q in range(SEQS):
                seq = jnp.dot(cols[q], pick(lot, q, at), preferred_element_type=F32)
                total = seq * seq if total is None else total + seq * seq
            f_ref[:, at] = (total * (1.0 / SEQS)).astype(BF16)


def fisher(at, xs, gates, ups, row, first, count, step, held=(), after=()):
    rows, depth = xs[0].shape
    held_rows, width = gates[0].shape
    x_spec = pl.BlockSpec((rows // 2, step), lambda j, _: (0, first + j))
    g_spec = pl.BlockSpec((held_rows, width), lambda j, _: (0, 0))
    out = pl.BlockSpec((step, width), lambda j, _: (first + j, 0))
    flops = 8 * held_rows * width * count * step
    return pl.pallas_call(
        functools.partial(fisher_kernel, tile(width, 256), row),
        grid_spec=pltpu.PrefetchScalarGridSpec(
            num_scalar_prefetch=1,
            grid=(count,),
            in_specs=[x_spec] * 4
            + [g_spec] * 4
            + [pl.BlockSpec(memory_space=pl.ANY)] * len((*held, *after)),
            out_specs=[out, out],
        ),
        out_shape=[jax.ShapeDtypeStruct((depth, width), BF16)] * 2,
        input_output_aliases={9 + i: i for i in range(len(held))},
        compiler_params=params(56),
        cost_estimate=cost(flops, 4 * width * count * step),
        name="fisher",
    )(at, *xs, *gates, *ups, *held, *after)


def split_kernel(row, at, tokens_ref, grad_ref, *rest):
    x_ref, dy_ref = rest[-2:]
    x_ref[...] = tokens_ref[pl.ds(at, row), :]
    dy_ref[...] = grad_ref[pl.ds(at, row), :]


def split(tokens, grad_out, row, at, after=()):
    whole = pl.BlockSpec(memory_space=pltpu.VMEM)
    return pl.pallas_call(
        functools.partial(split_kernel, row, at),
        in_specs=[whole, whole] + [pl.BlockSpec(memory_space=pl.ANY)] * len(after),
        out_specs=[whole, whole],
        out_shape=[jax.ShapeDtypeStruct((row, tokens.shape[1]), BF16)] * 2,
        compiler_params=params(32),
        cost_estimate=cost(0, 4 * row * tokens.shape[1]),
        name="split",
    )(tokens, grad_out, *after)


def pack_kernel(*refs):
    pieces, out_ref, sems = refs[:-2], refs[-2], refs[-1]
    row = pieces[0].shape[0]
    copies = [
        pltpu.make_async_copy(piece, out_ref.at[pl.ds(i * row, row), :], sems.at[i])
        for i, piece in enumerate(pieces)
    ]
    for copy in copies:
        copy.start()
    for copy in copies:
        copy.wait()


def pack(pieces):
    row, depth = pieces[0].shape
    whole = pl.BlockSpec(memory_space=pl.ANY)
    return pl.pallas_call(
        pack_kernel,
        in_specs=[whole] * len(pieces),
        out_specs=whole,
        out_shape=jax.ShapeDtypeStruct((row * len(pieces), depth), BF16),
        scratch_shapes=[pltpu.SemaphoreType.DMA((len(pieces),))],
        compiler_params=params(56),
        cost_estimate=cost(0, 4 * row * len(pieces) * depth),
        name="pack",
    )(*pieces)


def ring_part(tokens, grad_out, wg, wu, wd):
    chips = len(CYCLE)
    far = chips // 2
    block, depth = tokens.shape
    width = wg.shape[1]
    row = block // 2
    links = [(CYCLE[i], CYCLE[(i + 1) % chips]) for i in range(chips)]
    to_right = [(2 * a + c, 2 * b + c) for a, b in links for c in range(2)]
    to_left = [(b, a) for a, b in to_right]
    across = [(2 * i + c, 2 * i + 1 - c) for i in range(chips) for c in range(2)]

    def right(value):
        return lax.ppermute(value, "hid", to_right)

    def left(value):
        return lax.ppermute(value, "hid", to_left)

    def swap(value):
        return lax.ppermute(value, "hid", across)

    def gather(x, dy):
        by = [[x] + [None] * (chips - 1), [dy] + [None] * (chips - 1)]
        rounds = []
        for k in range(1, far + 1):
            got = []
            for s in range(2):
                if k < far or s == 0:
                    by[s][k] = right(by[s][k - 1])
                    got.append(by[s][k])
                if k < far or s == 1:
                    by[s][chips - k] = left(by[s][(chips - k + 1) % chips])
                    got.append(by[s][chips - k])
            rounds.append(got)
        return by[0] + by[1], rounds

    def scatter(own, near, right_far):
        def base(p):
            at = slice(p * row, (p + 1) * row)
            return own[at] + near[at].astype(F32)

        def plus(p, got):
            return base(p) if got is None else base(p) + got.astype(F32)

        rounds = []
        r = l = None
        for k in range(far, 0, -1):
            got = []
            if k < far or right_far:
                r = right(plus(chips - k, r).astype(BF16))
                got.append(r)
            if k < far or not right_far:
                l = left(plus(k, l).astype(BF16))
                got.append(l)
            rounds.append(got)
        return plus(0, r) + l.astype(F32), rounds

    step = tile(width, 256)
    tiles = width // step
    cuts = [0, tiles // 3, 2 * (tiles // 3), tiles] if tiles > 2 else [0, tiles]
    lots = list(zip(cuts, cuts[1:]))
    deep = depth // 512

    def compute(near, away, waits):
        waits = list(waits) + [()] * (len(lots) + 2 - len(waits))
        held = ()
        for a, b in lots:
            held = forward(near, away, wg, wu, wd, a, b - a, step, held, waits.pop(0))
        gg, gu = held
        held = input_terms(gg, gu, wg, wu, 0, deep // 2, 512, (), waits.pop(0))
        own, sent = input_terms(gg, gu, wg, wu, deep // 2, deep // 2, 512, held, waits.pop(0))
        return gg, gu, own, swap(sent)

    pieces, rounds = gather(*split(tokens, grad_out, row, 0))
    near_a = pack(pieces)
    pieces, waits = gather(*split(tokens, grad_out, row, row, rounds[far - 2]))
    near_b = pack(pieces)
    away_a = swap(near_a)
    away_b = swap(near_b)
    gg_a, gu_a, own, got = compute(near_a, away_a, [()] + waits[:-1] + [(near_b,)])
    mine_a, waits = scatter(own, got, True)
    gg_b, gu_b, own, got_b = compute(near_b, away_b, [(), (got,)] + waits[:-1])
    mine_b, more = scatter(own, got_b, False)

    spot = [0] * chips
    for i, c in enumerate(CYCLE):
        spot[c] = i
    me = jnp.array(spot, jnp.int32)[lax.axis_index("hid") // 2]
    at = (me - jnp.array(spot, jnp.int32)) % chips
    xs = [near_a, away_a, near_b, away_b]
    waits = [waits[-1], (got_b,)] + more[:-1]
    held = ()
    first = 0
    for i, wait in enumerate(waits):
        count = (deep - first) // (len(waits) - i)
        held = fisher(at, xs, (gg_a, gg_b), (gu_a, gu_b), row, first, count, 512, held, wait)
        first += count
    mine = jnp.concatenate([mine_a, mine_b], axis=0).astype(BF16)
    return held[0], held[1], mine


def plain_forward_kernel(x_ref, wg_ref, wu_ref, gate_ref, up_ref):
    x = x_ref[...]
    gate_ref[...] = jnp.dot(x, wg_ref[...], preferred_element_type=jnp.float32)
    up_ref[...] = jnp.dot(x, wu_ref[...], preferred_element_type=jnp.float32)


def plain_forward(x, wg, wu):
    rows, depth = x.shape
    width = wg.shape[1]
    step = tile(width, 256)
    return pl.pallas_call(
        plain_forward_kernel,
        grid=(width // step,),
        in_specs=[
            pl.BlockSpec((rows, depth), lambda j: (0, 0)),
            pl.BlockSpec((depth, step), lambda j: (0, j)),
            pl.BlockSpec((depth, step), lambda j: (0, j)),
        ],
        out_specs=[pl.BlockSpec((rows, step), lambda j: (0, j))] * 2,
        out_shape=[jax.ShapeDtypeStruct((rows, width), jnp.float32)] * 2,
        compiler_params=params(40),
        cost_estimate=cost(4 * rows * depth * width, 4 * depth * width),
        name="gate_up",
    )(x, wg, wu)


def plain_back_kernel(parts, dy_ref, wd_ref, gate_ref, up_ref, gg_ref, gu_ref):
    rows = dy_ref.shape[0] // parts
    for p in range(parts):
        at = pl.ds(p * rows, rows)
        hidden = lax.dot_general(dy_ref[at, :], wd_ref[...], NT, preferred_element_type=jnp.float32)
        gate = gate_ref[at, :]
        sigma = jax.nn.sigmoid(gate)
        both = hidden * sigma
        gg_ref[at, :] = (both * up_ref[at, :] * (1.0 + gate * (1.0 - sigma))).astype(jnp.bfloat16)
        gu_ref[at, :] = (both * gate).astype(jnp.bfloat16)


def plain_back(dy, wd, gate, up):
    rows, depth = dy.shape
    width = wd.shape[0]
    step = tile(width, 256)
    column = pl.BlockSpec((rows, step), lambda j: (0, j))
    return pl.pallas_call(
        functools.partial(plain_back_kernel, 2),
        grid=(width // step,),
        in_specs=[
            pl.BlockSpec((rows, depth), lambda j: (0, 0)),
            pl.BlockSpec((step, depth), lambda j: (j, 0)),
            column,
            column,
        ],
        out_specs=[column, column],
        out_shape=[jax.ShapeDtypeStruct((rows, width), jnp.bfloat16)] * 2,
        compiler_params=params(40),
        cost_estimate=cost(2 * rows * depth * width, 2 * depth * width),
        name="hidden_back",
    )(dy, wd, gate, up)


def plain_input_kernel(gg_ref, gu_ref, wg_ref, wu_ref, out_ref):
    total = lax.dot_general(gg_ref[...], wg_ref[...], NT, preferred_element_type=jnp.float32)
    total += lax.dot_general(gu_ref[...], wu_ref[...], NT, preferred_element_type=jnp.float32)
    out_ref[...] = total.astype(jnp.bfloat16)


def plain_input_terms(gg, gu, wg, wu):
    rows, width = gg.shape
    depth = wg.shape[0]
    step = 512
    held = pl.BlockSpec((rows, width), lambda j: (0, 0))
    return pl.pallas_call(
        plain_input_kernel,
        grid=(depth // step,),
        in_specs=[
            held,
            held,
            pl.BlockSpec((step, width), lambda j: (j, 0)),
            pl.BlockSpec((step, width), lambda j: (j, 0)),
        ],
        out_specs=pl.BlockSpec((rows, step), lambda j: (0, j)),
        out_shape=jax.ShapeDtypeStruct((rows, depth), jnp.bfloat16),
        compiler_params=params(40),
        cost_estimate=cost(4 * rows * depth * width, 4 * depth * width),
        name="input_terms",
    )(gg, gu, wg, wu)


def plain_fisher_kernel(step, x_ref, gg_ref, gu_ref, fg_ref, fu_ref):
    half = x_ref.shape[0] // 2
    span = half // SEQS
    width = gg_ref.shape[1]

    def rows(ref, q, at):
        near = ref[pl.ds(q * span, span), at]
        far = ref[pl.ds(half + q * span, span), at]
        return jnp.concatenate([near, far], axis=0)

    xs = [rows(x_ref, q, slice(None)).T for q in range(SEQS)]
    for g_ref, f_ref in ((gg_ref, fg_ref), (gu_ref, fu_ref)):
        for c in range(width // step):
            at = pl.ds(c * step, step)
            total = None
            for q in range(SEQS):
                seq = jnp.dot(xs[q], rows(g_ref, q, at), preferred_element_type=jnp.float32)
                total = seq * seq if total is None else total + seq * seq
            f_ref[:, at] = (total * (1.0 / SEQS)).astype(jnp.bfloat16)


def plain_fisher(x, gg, gu):
    rows, depth = x.shape
    width = gg.shape[1]
    step = 512
    held = pl.BlockSpec((rows, width), lambda j: (0, 0))
    block = pl.BlockSpec((step, width), lambda j: (j, 0))
    return pl.pallas_call(
        functools.partial(plain_fisher_kernel, tile(width, 256)),
        grid=(depth // step,),
        in_specs=[pl.BlockSpec((rows, step), lambda j: (0, j)), held, held],
        out_specs=[block, block],
        out_shape=[jax.ShapeDtypeStruct((depth, width), jnp.bfloat16)] * 2,
        compiler_params=params(40),
        cost_estimate=cost(4 * rows * depth * width, 4 * depth * width),
        name="fisher",
    )(x, gg, gu)


def plain_part(size, tokens, grad_out, wg, wu, wd):
    chips = size // 2
    across = [[2 * i + c for i in range(chips)] for c in range(2)]
    pairs = [[2 * i, 2 * i + 1] for i in range(chips)]
    block, depth = tokens.shape

    def gather(rows):
        near = lax.all_gather(rows, "hid", axis=0, tiled=True, axis_index_groups=across)
        return lax.all_gather(near, "hid", axis=0, tiled=False, axis_index_groups=pairs)

    x = gather(tokens).reshape(-1, depth)
    dy = gather(grad_out).reshape(-1, depth)
    gate, up = plain_forward(x, wg, wu)
    gg, gu = plain_back(dy, wd, gate, up)
    terms = plain_input_terms(gg, gu, wg, wu).reshape(2, -1, depth)
    mine = lax.psum_scatter(
        terms, "hid", scatter_dimension=0, tiled=False, axis_index_groups=pairs
    )
    mine = lax.psum_scatter(
        mine, "hid", scatter_dimension=0, tiled=True, axis_index_groups=across
    )
    fg, fu = plain_fisher(x, gg, gu)
    return fg, fu, mine


def per_device(size, tokens, grad_out, wg, wu, wd):
    if size == 2 * len(CYCLE) and tokens.shape[0] % 32 == 0:
        return ring_part(tokens, grad_out, wg, wu, wd)
    return plain_part(size, tokens, grad_out, wg, wu, wd)


def solution(mesh):
    rows = P(("adjust", "hid"), None)
    weights = P("adjust", "hid")
    return jax.shard_map(
        functools.partial(per_device, mesh.shape["hid"]),
        mesh=mesh,
        in_specs=(rows, rows, weights, weights, rows),
        out_specs=(weights, weights, rows),
        check_vma=False,
    )
```

```python
import functools

import jax
import jax.numpy as jnp
from jax import lax
from jax.experimental import pallas as pl
from jax.experimental.pallas import tpu as pltpu
from jax.sharding import PartitionSpec as P

SEQS = 2
MIB = 1 << 20
CYCLE = (0, 2, 4, 6, 7, 5, 3, 1)
NT = (((1,), (1,)), ((), ()))
BF16 = jnp.bfloat16
F32 = jnp.float32


def tile(size, want):
    return want if size % want == 0 else size


def params(mib):
    return pltpu.CompilerParams(vmem_limit_bytes=mib * MIB)


def cost(flops, read):
    return pl.CostEstimate(flops=flops, bytes_accessed=read, transcendentals=0)


def silu_grads(hidden, gate, up):
    sigma = jax.nn.sigmoid(gate)
    both = hidden * sigma
    gg = both * up * (1.0 + gate * (1.0 - sigma))
    return gg.astype(BF16), (both * gate).astype(BF16)


def pack_kernel(at_ref, *refs):
    pieces, out_ref = refs[:-1], refs[-1]
    row = pieces[0].shape[0]
    start = 0
    for piece in pieces:
        part = piece.shape[0]
        base = at_ref[start // row] * row + start % row
        out_ref[pl.ds(pl.multiple_of(base, part), part), :] = piece[...]
        start += part


def pack(at, pieces):
    depth = pieces[0].shape[1]
    rows = sum(piece.shape[0] for piece in pieces)
    return pl.pallas_call(
        pack_kernel,
        in_specs=[pl.BlockSpec(memory_space=pltpu.SMEM)]
        + [pl.BlockSpec(memory_space=pltpu.VMEM)] * len(pieces),
        out_specs=pl.BlockSpec(memory_space=pltpu.VMEM),
        out_shape=jax.ShapeDtypeStruct((rows, depth), BF16),
        compiler_params=params(16),
        cost_estimate=cost(0, 4 * rows * depth),
        name="pack",
    )(at, *pieces)


def gate_up_kernel(row, core_ref, near_ref, far_ref, wg_ref, wu_ref, gate_ref, up_ref, x_ref):
    @pl.when(pl.program_id(0) == 0)
    def _():
        mine = core_ref[0]
        for c in range(near_ref.shape[0] // row):
            at = pl.ds(c * row, row)
            base = 2 * c * row
            x_ref[pl.ds(pl.multiple_of(base + mine * row, row), row), :] = near_ref[at, :]
            x_ref[pl.ds(pl.multiple_of(base + (1 - mine) * row, row), row), :] = far_ref[at, :]

    gate_ref[...] = jnp.dot(x_ref[...], wg_ref[...], preferred_element_type=F32)
    up_ref[...] = jnp.dot(x_ref[...], wu_ref[...], preferred_element_type=F32)


def gate_up(core, near, far, wg, wu, row):
    rows, depth = near.shape
    width = wg.shape[1]
    step = tile(width, 256)
    half = pl.BlockSpec((rows, depth), lambda j: (0, 0))
    column = pl.BlockSpec((depth, step), lambda j: (0, j))
    out = pl.BlockSpec((2 * rows, step), lambda j: (0, j))
    return pl.pallas_call(
        functools.partial(gate_up_kernel, row),
        grid=(width // step,),
        in_specs=[pl.BlockSpec(memory_space=pltpu.SMEM), half, half, column, column],
        out_specs=[out, out, pl.BlockSpec((2 * rows, depth), lambda j: (0, 0))],
        out_shape=[jax.ShapeDtypeStruct((2 * rows, width), F32)] * 2
        + [jax.ShapeDtypeStruct((2 * rows, depth), BF16)],
        compiler_params=params(36),
        cost_estimate=cost(8 * rows * depth * width, 4 * depth * width),
        name="gate_up",
    )(core, near, far, wg, wu)


def back_kernel(parts, dy_ref, wd_ref, gate_ref, up_ref, gg_ref, gu_ref):
    rows = dy_ref.shape[0] // parts
    for p in range(parts):
        at = pl.ds(p * rows, rows)
        hidden = lax.dot_general(dy_ref[at, :], wd_ref[...], NT, preferred_element_type=F32)
        gg_ref[at, :], gu_ref[at, :] = silu_grads(hidden, gate_ref[at, :], up_ref[at, :])


def back(dy, wd, gate, up):
    rows, depth = dy.shape
    width = wd.shape[0]
    step = tile(width, 256)
    column = pl.BlockSpec((rows, step), lambda j: (0, j))
    return pl.pallas_call(
        functools.partial(back_kernel, 2),
        grid=(width // step,),
        in_specs=[
            pl.BlockSpec((rows, depth), lambda j: (0, 0)),
            pl.BlockSpec((step, depth), lambda j: (j, 0)),
            column,
            column,
        ],
        out_specs=[column, column],
        out_shape=[jax.ShapeDtypeStruct((rows, width), BF16)] * 2,
        compiler_params=params(58),
        cost_estimate=cost(2 * rows * depth * width, 2 * depth * width),
        name="hidden_back",
    )(dy, wd, gate, up)


def input_kernel(gg_ref, gu_ref, wg_ref, wu_ref, *rest):
    out_ref = rest[-1]
    total = lax.dot_general(gg_ref[...], wg_ref[...], NT, preferred_element_type=F32)
    total += lax.dot_general(gu_ref[...], wu_ref[...], NT, preferred_element_type=F32)
    out_ref[...] = total.astype(BF16)


def input_terms(gg, gu, wg, wu, first, count, step, after=()):
    rows, width = gg.shape
    whole = pl.BlockSpec((rows, width), lambda j: (0, 0))
    weight = pl.BlockSpec((step, width), lambda j: (first + j, 0))
    return pl.pallas_call(
        input_kernel,
        grid=(count,),
        in_specs=[whole, whole, weight, weight]
        + [pl.BlockSpec(memory_space=pl.ANY)] * len(after),
        out_specs=pl.BlockSpec((rows, step), lambda j: (0, j)),
        out_shape=jax.ShapeDtypeStruct((rows, count * step), BF16),
        compiler_params=params(58),
        cost_estimate=cost(4 * rows * width * count * step, 4 * width * count * step),
        name="input_terms",
    )(gg, gu, wg, wu, *after)


def fisher_kernel(step, x_ref, gg_ref, gu_ref, *rest):
    fg_ref, fu_ref = rest[-2:]
    span = x_ref.shape[0] // SEQS
    seqs = [pl.ds(q * span, span) for q in range(SEQS)]
    cols = [x_ref[at, :].T for at in seqs]
    for g_ref, f_ref in ((gg_ref, fg_ref), (gu_ref, fu_ref)):
        for c in range(g_ref.shape[1] // step):
            at = pl.ds(c * step, step)
            total = None
            for q in range(SEQS):
                seq = jnp.dot(cols[q], g_ref[seqs[q], at], preferred_element_type=F32)
                total = seq * seq if total is None else total + seq * seq
            f_ref[:, at] = (total * (1.0 / SEQS)).astype(BF16)


def fisher(x, gg, gu, step, after=()):
    rows, depth = x.shape
    width = gg.shape[1]
    held = pl.BlockSpec((rows, width), lambda j: (0, 0))
    block = pl.BlockSpec((step, width), lambda j: (j, 0))
    return pl.pallas_call(
        functools.partial(fisher_kernel, tile(width, 256)),
        grid=(depth // step,),
        in_specs=[pl.BlockSpec((rows, step), lambda j: (0, j)), held, held]
        + [pl.BlockSpec(memory_space=pl.ANY)] * len(after),
        out_specs=[block, block],
        out_shape=[jax.ShapeDtypeStruct((depth, width), BF16)] * 2,
        compiler_params=params(58),
        cost_estimate=cost(4 * rows * depth * width, 4 * depth * width),
        name="fisher",
    )(x, gg, gu, *after)


def ring_part(tokens, grad_out, wg, wu, wd):
    chips = len(CYCLE)
    far = chips // 2
    row, depth = tokens.shape
    links = [(CYCLE[i], CYCLE[(i + 1) % chips]) for i in range(chips)]
    to_right = [(2 * a + c, 2 * b + c) for a, b in links for c in range(2)]
    to_left = [(b, a) for a, b in to_right]
    across = [(2 * i + c, 2 * i + 1 - c) for i in range(chips) for c in range(2)]

    def right(value):
        return lax.ppermute(value, "hid", to_right)

    def left(value):
        return lax.ppermute(value, "hid", to_left)

    device = lax.axis_index("hid")
    spot = [CYCLE.index(c) for c in range(chips)]
    me = jnp.array(spot, jnp.int32)[device // 2]
    at = jnp.array(CYCLE, jnp.int32)[(me - jnp.arange(chips, dtype=jnp.int32)) % chips]
    core = (device % 2).astype(jnp.int32).reshape(1)

    dy = lax.all_gather(grad_out, "hid", axis=0, tiled=True)
    from_left, from_right = [tokens], [tokens]
    for _ in range(1, far):
        from_left.append(right(from_left[-1]))
        from_right.append(left(from_right[-1]))
    ends = [right(from_left[-1][: row // 2]), left(from_right[-1][row // 2 :])]
    near = pack(at, from_left + ends + from_right[:0:-1])
    apart = lax.ppermute(near, "hid", across)
    gate, up, x = gate_up(core, near, apart, wg, wu, row)
    gg, gu = back(dy, wd, gate, up)
    half = depth // 512 // 2
    low = input_terms(gg, gu, wg, wu, 0, half, 512)
    high = input_terms(gg, gu, wg, wu, half, half, 512, (low,))
    mine = [
        lax.psum_scatter(terms, "hid", scatter_dimension=0, tiled=True)
        for terms in (low, high)
    ]
    fg, fu = fisher(x, gg, gu, 512, (high,))
    return fg, fu, jnp.concatenate(mine, axis=1)


def plain_forward_kernel(x_ref, wg_ref, wu_ref, gate_ref, up_ref):
    x = x_ref[...]
    gate_ref[...] = jnp.dot(x, wg_ref[...], preferred_element_type=jnp.float32)
    up_ref[...] = jnp.dot(x, wu_ref[...], preferred_element_type=jnp.float32)


def plain_forward(x, wg, wu):
    rows, depth = x.shape
    width = wg.shape[1]
    step = tile(width, 256)
    return pl.pallas_call(
        plain_forward_kernel,
        grid=(width // step,),
        in_specs=[
            pl.BlockSpec((rows, depth), lambda j: (0, 0)),
            pl.BlockSpec((depth, step), lambda j: (0, j)),
            pl.BlockSpec((depth, step), lambda j: (0, j)),
        ],
        out_specs=[pl.BlockSpec((rows, step), lambda j: (0, j))] * 2,
        out_shape=[jax.ShapeDtypeStruct((rows, width), jnp.float32)] * 2,
        compiler_params=params(40),
        cost_estimate=cost(4 * rows * depth * width, 4 * depth * width),
        name="gate_up",
    )(x, wg, wu)


def plain_back_kernel(parts, dy_ref, wd_ref, gate_ref, up_ref, gg_ref, gu_ref):
    rows = dy_ref.shape[0] // parts
    for p in range(parts):
        at = pl.ds(p * rows, rows)
        hidden = lax.dot_general(dy_ref[at, :], wd_ref[...], NT, preferred_element_type=jnp.float32)
        gate = gate_ref[at, :]
        sigma = jax.nn.sigmoid(gate)
        both = hidden * sigma
        gg_ref[at, :] = (both * up_ref[at, :] * (1.0 + gate * (1.0 - sigma))).astype(jnp.bfloat16)
        gu_ref[at, :] = (both * gate).astype(jnp.bfloat16)


def plain_back(dy, wd, gate, up):
    rows, depth = dy.shape
    width = wd.shape[0]
    step = tile(width, 256)
    column = pl.BlockSpec((rows, step), lambda j: (0, j))
    return pl.pallas_call(
        functools.partial(plain_back_kernel, 2),
        grid=(width // step,),
        in_specs=[
            pl.BlockSpec((rows, depth), lambda j: (0, 0)),
            pl.BlockSpec((step, depth), lambda j: (j, 0)),
            column,
            column,
        ],
        out_specs=[column, column],
        out_shape=[jax.ShapeDtypeStruct((rows, width), jnp.bfloat16)] * 2,
        compiler_params=params(40),
        cost_estimate=cost(2 * rows * depth * width, 2 * depth * width),
        name="hidden_back",
    )(dy, wd, gate, up)


def plain_input_kernel(gg_ref, gu_ref, wg_ref, wu_ref, out_ref):
    total = lax.dot_general(gg_ref[...], wg_ref[...], NT, preferred_element_type=jnp.float32)
    total += lax.dot_general(gu_ref[...], wu_ref[...], NT, preferred_element_type=jnp.float32)
    out_ref[...] = total.astype(jnp.bfloat16)


def plain_input_terms(gg, gu, wg, wu):
    rows, width = gg.shape
    depth = wg.shape[0]
    step = 512
    held = pl.BlockSpec((rows, width), lambda j: (0, 0))
    return pl.pallas_call(
        plain_input_kernel,
        grid=(depth // step,),
        in_specs=[
            held,
            held,
            pl.BlockSpec((step, width), lambda j: (j, 0)),
            pl.BlockSpec((step, width), lambda j: (j, 0)),
        ],
        out_specs=pl.BlockSpec((rows, step), lambda j: (0, j)),
        out_shape=jax.ShapeDtypeStruct((rows, depth), jnp.bfloat16),
        compiler_params=params(40),
        cost_estimate=cost(4 * rows * depth * width, 4 * depth * width),
        name="input_terms",
    )(gg, gu, wg, wu)


def plain_fisher_kernel(step, x_ref, gg_ref, gu_ref, fg_ref, fu_ref):
    half = x_ref.shape[0] // 2
    span = half // SEQS
    width = gg_ref.shape[1]

    def rows(ref, q, at):
        near = ref[pl.ds(q * span, span), at]
        far = ref[pl.ds(half + q * span, span), at]
        return jnp.concatenate([near, far], axis=0)

    xs = [rows(x_ref, q, slice(None)).T for q in range(SEQS)]
    for g_ref, f_ref in ((gg_ref, fg_ref), (gu_ref, fu_ref)):
        for c in range(width // step):
            at = pl.ds(c * step, step)
            total = None
            for q in range(SEQS):
                seq = jnp.dot(xs[q], rows(g_ref, q, at), preferred_element_type=jnp.float32)
                total = seq * seq if total is None else total + seq * seq
            f_ref[:, at] = (total * (1.0 / SEQS)).astype(jnp.bfloat16)


def plain_fisher(x, gg, gu):
    rows, depth = x.shape
    width = gg.shape[1]
    step = 512
    held = pl.BlockSpec((rows, width), lambda j: (0, 0))
    block = pl.BlockSpec((step, width), lambda j: (j, 0))
    return pl.pallas_call(
        functools.partial(plain_fisher_kernel, tile(width, 256)),
        grid=(depth // step,),
        in_specs=[pl.BlockSpec((rows, step), lambda j: (0, j)), held, held],
        out_specs=[block, block],
        out_shape=[jax.ShapeDtypeStruct((depth, width), jnp.bfloat16)] * 2,
        compiler_params=params(40),
        cost_estimate=cost(4 * rows * depth * width, 4 * depth * width),
        name="fisher",
    )(x, gg, gu)


def plain_part(size, tokens, grad_out, wg, wu, wd):
    chips = size // 2
    across = [[2 * i + c for i in range(chips)] for c in range(2)]
    pairs = [[2 * i, 2 * i + 1] for i in range(chips)]
    block, depth = tokens.shape

    def gather(rows):
        near = lax.all_gather(rows, "hid", axis=0, tiled=True, axis_index_groups=across)
        return lax.all_gather(near, "hid", axis=0, tiled=False, axis_index_groups=pairs)

    x = gather(tokens).reshape(-1, depth)
    dy = gather(grad_out).reshape(-1, depth)
    gate, up = plain_forward(x, wg, wu)
    gg, gu = plain_back(dy, wd, gate, up)
    terms = plain_input_terms(gg, gu, wg, wu).reshape(2, -1, depth)
    mine = lax.psum_scatter(
        terms, "hid", scatter_dimension=0, tiled=False, axis_index_groups=pairs
    )
    mine = lax.psum_scatter(
        mine, "hid", scatter_dimension=0, tiled=True, axis_index_groups=across
    )
    fg, fu = plain_fisher(x, gg, gu)
    return fg, fu, mine


def per_device(size, tokens, grad_out, wg, wu, wd):
    if size == 2 * len(CYCLE) and tokens.shape[0] % 32 == 0:
        return ring_part(tokens, grad_out, wg, wu, wd)
    return plain_part(size, tokens, grad_out, wg, wu, wd)


def solution(mesh):
    rows = P(("adjust", "hid"), None)
    weights = P("adjust", "hid")
    return jax.shard_map(
        functools.partial(per_device, mesh.shape["hid"]),
        mesh=mesh,
        in_specs=(rows, rows, weights, weights, rows),
        out_specs=(weights, weights, rows),
        check_vma=False,
    )
```

```python
import functools

import jax
import jax.numpy as jnp
from jax import lax
from jax.experimental import pallas as pl
from jax.experimental.pallas import tpu as pltpu
from jax.sharding import PartitionSpec as P

SEQS = 2
MIB = 1 << 20
CYCLE = (0, 2, 4, 6, 7, 5, 3, 1)
NT = (((1,), (1,)), ((), ()))
BF16 = jnp.bfloat16
F32 = jnp.float32


def tile(size, want):
    return want if size % want == 0 else size


def params(mib):
    return pltpu.CompilerParams(vmem_limit_bytes=mib * MIB)


def cost(flops, read):
    return pl.CostEstimate(flops=flops, bytes_accessed=read, transcendentals=0)


def any_specs(values):
    return [pl.BlockSpec(memory_space=pl.ANY)] * len(values)


def relay_kernel(in_ref, *rest):
    rest[-1][...] = in_ref[...]


def relay(value, after):
    whole = pl.BlockSpec(memory_space=pltpu.VMEM)
    return pl.pallas_call(
        relay_kernel,
        in_specs=[whole] + any_specs(after),
        out_specs=whole,
        out_shape=jax.ShapeDtypeStruct(value.shape, value.dtype),
        compiler_params=params(8),
        cost_estimate=cost(0, 4 * value.size),
        name="relay",
    )(value, *after)


def pack_kernel(*refs):
    pieces, out_ref = refs[:-1], refs[-1]
    start = 0
    for piece in pieces:
        out_ref[pl.ds(start, piece.shape[0]), :] = piece[...]
        start += piece.shape[0]


def pack(pieces):
    depth = pieces[0].shape[1]
    rows = sum(piece.shape[0] for piece in pieces)
    whole = pl.BlockSpec(memory_space=pltpu.VMEM)
    return pl.pallas_call(
        pack_kernel,
        in_specs=[whole] * len(pieces),
        out_specs=whole,
        out_shape=jax.ShapeDtypeStruct((rows, depth), BF16),
        compiler_params=params(8),
        cost_estimate=cost(0, 4 * rows * depth),
        name="pack",
    )(*pieces)


def places(chips, row):
    span = chips // SEQS
    for q in range(SEQS):
        for side in range(2):
            for k in range(span):
                yield q * span + k, side, ((q * 2 + side) * span + k) * row


def arrange(spot_ref, near_ref, far_ref, out_ref):
    chips = spot_ref.shape[0]
    row = near_ref.shape[0] // chips
    for chip, side, place in places(chips, row):
        start = pl.multiple_of(spot_ref[chip] * row, row)
        out_ref[pl.ds(place, row), :] = (near_ref, far_ref)[side][pl.ds(start, row), :]


def gate_up_kernel(parts, spot_ref, near_ref, far_ref, wg_ref, wu_ref, *rest):
    a_ref, b_ref, x_ref = rest[-3:]

    @pl.when(pl.program_id(0) == 0)
    def _():
        arrange(spot_ref, near_ref, far_ref, x_ref)

    rows = x_ref.shape[0] // parts
    for p in range(parts):
        at = pl.ds(p * rows, rows)
        gate = jnp.dot(x_ref[at, :], wg_ref[...], preferred_element_type=F32)
        up = jnp.dot(x_ref[at, :], wu_ref[...], preferred_element_type=F32)
        sigma = jax.nn.sigmoid(gate)
        a_ref[at, :] = up * sigma * (1.0 + gate * (1.0 - sigma))
        b_ref[at, :] = gate * sigma


def gate_up(spot, near, far, wg, wu, after):
    rows, depth = near.shape
    width = wg.shape[1]
    step = tile(width, 256)
    half = pl.BlockSpec((rows, depth), lambda j: (0, 0))
    column = pl.BlockSpec((depth, step), lambda j: (0, j))
    out = pl.BlockSpec((2 * rows, step), lambda j: (0, j))
    return pl.pallas_call(
        functools.partial(gate_up_kernel, 2),
        grid=(width // step,),
        in_specs=[pl.BlockSpec(memory_space=pltpu.SMEM), half, half, column, column]
        + any_specs(after),
        out_specs=[out, out, pl.BlockSpec((2 * rows, depth), lambda j: (0, 0))],
        out_shape=[jax.ShapeDtypeStruct((2 * rows, width), F32)] * 2
        + [jax.ShapeDtypeStruct((2 * rows, depth), BF16)],
        compiler_params=params(36),
        cost_estimate=cost(8 * rows * depth * width, 4 * depth * width),
        name="gate_up",
    )(spot, near, far, wg, wu, *after)


def back_kernel(
    tiles, spot_ref, near_ref, far_ref, wd_ref, a_ref, b_ref, wg_ref, wu_ref,
    gg_ref, gu_ref, own_ref, sent_ref, dy_ref,
):
    j = pl.program_id(0)
    chips = spot_ref.shape[0]
    row = near_ref.shape[0] // chips
    step = wd_ref.shape[0]

    @pl.when(j == 0)
    def _():
        arrange(spot_ref, near_ref, far_ref, dy_ref)

    @pl.when(j < tiles)
    def _():
        hidden = lax.dot_general(dy_ref[...], wd_ref[...], NT, preferred_element_type=F32)
        at = pl.ds(pl.multiple_of(j * step, step), step)
        gg_ref[:, at] = (hidden * a_ref[...]).astype(BF16)
        gu_ref[:, at] = (hidden * b_ref[...]).astype(BF16)

    @pl.when(j >= tiles)
    def _():
        total = lax.dot_general(gg_ref[...], wg_ref[...], NT, preferred_element_type=F32)
        total += lax.dot_general(gu_ref[...], wu_ref[...], NT, preferred_element_type=F32)
        for chip, side, place in places(chips, row):
            start = pl.multiple_of(spot_ref[chip] * row, row)
            terms = total[place : place + row, :]
            if side:
                sent_ref[pl.ds(start, row), :] = terms.astype(BF16)
            else:
                own_ref[pl.ds(start, row), :] = terms


def back(spot, near, far, wd, a, b, wg, wu):
    rows, depth = near.shape
    width = wd.shape[0]
    step = tile(width, 256)
    tiles = width // step
    deep = 256

    def early(j):
        return jnp.minimum(j, tiles - 1)

    def late(j):
        return jnp.maximum(j - tiles, 0)

    half = pl.BlockSpec((rows, depth), lambda j: (0, 0))
    column = pl.BlockSpec((2 * rows, step), lambda j: (0, early(j)))
    weight = pl.BlockSpec((deep, width), lambda j: (late(j), 0))
    grads = pl.BlockSpec((2 * rows, width), lambda j: (0, 0))
    terms = pl.BlockSpec((rows, deep), lambda j: (0, late(j)))
    return pl.pallas_call(
        functools.partial(back_kernel, tiles),
        grid=(tiles + depth // deep,),
        in_specs=[
            pl.BlockSpec(memory_space=pltpu.SMEM),
            half,
            half,
            pl.BlockSpec((step, depth), lambda j: (early(j), 0)),
            column,
            column,
            weight,
            weight,
        ],
        out_specs=[grads, grads, terms, terms],
        out_shape=[jax.ShapeDtypeStruct((2 * rows, width), BF16)] * 2
        + [
            jax.ShapeDtypeStruct((rows, depth), F32),
            jax.ShapeDtypeStruct((rows, depth), BF16),
        ],
        scratch_shapes=[pltpu.VMEM((2 * rows, depth), BF16)],
        compiler_params=params(34),
        cost_estimate=cost(12 * rows * depth * width, 6 * depth * width),
        name="hidden_back",
    )(spot, near, far, wd, a, b, wg, wu)


def fold_kernel(cuts, *refs):
    count = len(cuts)
    outs = refs[-count:]
    for i, (at, got_at) in enumerate(cuts):
        own_ref, near_ref, got_ref = refs[3 * i : 3 * i + 3]
        out_ref = outs[i]
        out_ref[...] = (own_ref[at, :] + near_ref[at, :].astype(F32)).astype(BF16)
        if got_at is not None:
            total = own_ref[got_at, :] + near_ref[got_at, :].astype(F32)
            out_ref[got_at, :] = (total + got_ref[...].astype(F32)).astype(BF16)


def fold(own, near, row, sends, after):
    depth = own.shape[1]
    operands, specs, shapes, cuts = [], [], [], []
    for p, at, got_at, got in sends:
        block = pl.BlockSpec((row, depth), lambda i, p=p: (p, 0))
        got = near if got is None else got
        size = got.shape[0] if got_at is not None else row
        operands += [own, near, got]
        specs += [block, block, pl.BlockSpec((size, depth), lambda i: (0, 0))]
        shapes.append(jax.ShapeDtypeStruct((at.size, depth), BF16))
        cuts.append((at, got_at))
    return pl.pallas_call(
        functools.partial(fold_kernel, cuts),
        grid=(1,),
        in_specs=specs + any_specs(after),
        out_specs=[pl.BlockSpec(shape.shape, lambda i: (0, 0)) for shape in shapes],
        out_shape=shapes,
        compiler_params=params(24),
        cost_estimate=cost(0, 16 * row * depth),
        name="fold",
    )(*operands, *after)


def last_kernel(own_ref, near_ref, r_ref, l_ref, out_ref):
    total = own_ref[...] + near_ref[...].astype(F32)
    out_ref[...] = (total + r_ref[...].astype(F32) + l_ref[...].astype(F32)).astype(BF16)


def last(own, near, r, l):
    block = pl.BlockSpec(r.shape, lambda i: (0, 0))
    return pl.pallas_call(
        last_kernel,
        grid=(1,),
        in_specs=[block] * 4,
        out_specs=block,
        out_shape=jax.ShapeDtypeStruct(r.shape, BF16),
        compiler_params=params(24),
        cost_estimate=cost(0, 12 * r.size),
        name="last",
    )(own, near, r, l)


def fisher_kernel(step, x_ref, gg_ref, gu_ref, *rest):
    fg_ref, fu_ref, done_ref = rest[-3:]
    done_ref[...] = jnp.zeros_like(done_ref)
    span = x_ref.shape[0] // SEQS
    seqs = [pl.ds(q * span, span) for q in range(SEQS)]
    cols = [x_ref[at, :].T for at in seqs]
    for g_ref, f_ref in ((gg_ref, fg_ref), (gu_ref, fu_ref)):
        for c in range(g_ref.shape[1] // step):
            at = pl.ds(c * step, step)
            total = None
            for q in range(SEQS):
                seq = jnp.dot(cols[q], g_ref[seqs[q], at], preferred_element_type=F32)
                total = seq * seq if total is None else total + seq * seq
            f_ref[:, at] = (total * (1.0 / SEQS)).astype(BF16)


def fisher(x, gg, gu, first, count, step, held, after):
    rows, depth = x.shape
    width = gg.shape[1]
    whole = pl.BlockSpec((rows, width), lambda j: (0, 0))
    block = pl.BlockSpec((step, width), lambda j: (first + j, 0))
    return pl.pallas_call(
        functools.partial(fisher_kernel, tile(width, 256)),
        grid=(count,),
        in_specs=[pl.BlockSpec((rows, step), lambda j: (0, first + j)), whole, whole]
        + any_specs((*held, *after)),
        out_specs=[block, block, pl.BlockSpec((8, 128), lambda j: (0, 0))],
        out_shape=[jax.ShapeDtypeStruct((depth, width), BF16)] * 2
        + [jax.ShapeDtypeStruct((8, 128), F32)],
        input_output_aliases={3 + i: i for i in range(len(held))},
        compiler_params=params(40),
        cost_estimate=cost(4 * rows * step * count * width, 4 * step * count * width),
        name="fisher",
    )(x, gg, gu, *held, *after)


def ring_part(tokens, grad_out, wg, wu, wd):
    chips = len(CYCLE)
    far = chips // 2
    row, depth = tokens.shape
    links = [(CYCLE[i], CYCLE[(i + 1) % chips]) for i in range(chips)]
    to_right = [(2 * a + c, 2 * b + c) for a, b in links for c in range(2)]
    to_left = [(b, a) for a, b in to_right]
    across = [(2 * i + c, 2 * i + 1 - c) for i in range(chips) for c in range(2)]

    def right(value):
        return lax.ppermute(value, "hid", to_right)

    def left(value):
        return lax.ppermute(value, "hid", to_left)

    def swap(value):
        return lax.ppermute(value, "hid", across)

    def gather(value):
        r, l = [value], [value]
        for _ in range(1, far):
            r.append(right(r[-1]))
            l.append(left(l[-1]))
        ends = [right(r[-1][: row // 2]), left(l[-1][row // 2 :])]
        return pack(r + ends + l[:0:-1]), (r[-1], l[-1])

    cycle = jnp.array([CYCLE.index(c) for c in range(chips)], jnp.int32)
    spot = (cycle[lax.axis_index("hid") // 2] - cycle) % chips

    near_x, busy = gather(tokens)
    far_x = swap(near_x)
    near_dy, _ = gather(relay(grad_out, busy))
    far_dy = swap(near_dy)
    a, b, x = gate_up(spot, near_x, far_x, wg, wu, (near_dy,))
    gg, gu, own, sent = back(spot, near_dy, far_dy, wd, a, b, wg, wu)

    near = swap(sent)
    full, head, tail = pl.ds(0, row), pl.ds(0, row // 2), pl.ds(row // 2, row // 2)
    step = 512
    counts = [2, 1, 2, 2, 1]
    held, first = (), 0
    r = l = None
    ready = ()
    for k in range(far, 0, -1):
        *held, done = fisher(x, gg, gu, first, counts[far - k], step, held, ready)
        first += counts[far - k]
        if k == far:
            sends = [(far, head, None, None), (far, tail, None, None)]
        elif k == far - 1:
            sends = [(chips - k, full, head, r), (k, full, tail, l)]
        else:
            sends = [(chips - k, full, full, r), (k, full, full, l)]
        ready = fold(own, near, row, sends, (done,))
        r, l = right(ready[0]), left(ready[1])
    fg, fu, _ = fisher(x, gg, gu, first, counts[far], step, held, ready)
    mine = last(own, near, r, l)
    return fg, fu, mine


def plain_forward_kernel(x_ref, wg_ref, wu_ref, gate_ref, up_ref):
    x = x_ref[...]
    gate_ref[...] = jnp.dot(x, wg_ref[...], preferred_element_type=jnp.float32)
    up_ref[...] = jnp.dot(x, wu_ref[...], preferred_element_type=jnp.float32)


def plain_forward(x, wg, wu):
    rows, depth = x.shape
    width = wg.shape[1]
    step = tile(width, 256)
    return pl.pallas_call(
        plain_forward_kernel,
        grid=(width // step,),
        in_specs=[
            pl.BlockSpec((rows, depth), lambda j: (0, 0)),
            pl.BlockSpec((depth, step), lambda j: (0, j)),
            pl.BlockSpec((depth, step), lambda j: (0, j)),
        ],
        out_specs=[pl.BlockSpec((rows, step), lambda j: (0, j))] * 2,
        out_shape=[jax.ShapeDtypeStruct((rows, width), jnp.float32)] * 2,
        compiler_params=params(40),
        cost_estimate=cost(4 * rows * depth * width, 4 * depth * width),
        name="gate_up",
    )(x, wg, wu)


def plain_back_kernel(parts, dy_ref, wd_ref, gate_ref, up_ref, gg_ref, gu_ref):
    rows = dy_ref.shape[0] // parts
    for p in range(parts):
        at = pl.ds(p * rows, rows)
        hidden = lax.dot_general(dy_ref[at, :], wd_ref[...], NT, preferred_element_type=jnp.float32)
        gate = gate_ref[at, :]
        sigma = jax.nn.sigmoid(gate)
        both = hidden * sigma
        gg_ref[at, :] = (both * up_ref[at, :] * (1.0 + gate * (1.0 - sigma))).astype(jnp.bfloat16)
        gu_ref[at, :] = (both * gate).astype(jnp.bfloat16)


def plain_back(dy, wd, gate, up):
    rows, depth = dy.shape
    width = wd.shape[0]
    step = tile(width, 256)
    column = pl.BlockSpec((rows, step), lambda j: (0, j))
    return pl.pallas_call(
        functools.partial(plain_back_kernel, 2),
        grid=(width // step,),
        in_specs=[
            pl.BlockSpec((rows, depth), lambda j: (0, 0)),
            pl.BlockSpec((step, depth), lambda j: (j, 0)),
            column,
            column,
        ],
        out_specs=[column, column],
        out_shape=[jax.ShapeDtypeStruct((rows, width), jnp.bfloat16)] * 2,
        compiler_params=params(40),
        cost_estimate=cost(2 * rows * depth * width, 2 * depth * width),
        name="hidden_back",
    )(dy, wd, gate, up)


def plain_input_kernel(gg_ref, gu_ref, wg_ref, wu_ref, out_ref):
    total = lax.dot_general(gg_ref[...], wg_ref[...], NT, preferred_element_type=jnp.float32)
    total += lax.dot_general(gu_ref[...], wu_ref[...], NT, preferred_element_type=jnp.float32)
    out_ref[...] = total.astype(jnp.bfloat16)


def plain_input_terms(gg, gu, wg, wu):
    rows, width = gg.shape
    depth = wg.shape[0]
    step = 512
    held = pl.BlockSpec((rows, width), lambda j: (0, 0))
    return pl.pallas_call(
        plain_input_kernel,
        grid=(depth // step,),
        in_specs=[
            held,
            held,
            pl.BlockSpec((step, width), lambda j: (j, 0)),
            pl.BlockSpec((step, width), lambda j: (j, 0)),
        ],
        out_specs=pl.BlockSpec((rows, step), lambda j: (0, j)),
        out_shape=jax.ShapeDtypeStruct((rows, depth), jnp.bfloat16),
        compiler_params=params(40),
        cost_estimate=cost(4 * rows * depth * width, 4 * depth * width),
        name="input_terms",
    )(gg, gu, wg, wu)


def plain_fisher_kernel(step, x_ref, gg_ref, gu_ref, fg_ref, fu_ref):
    half = x_ref.shape[0] // 2
    span = half // SEQS
    width = gg_ref.shape[1]

    def rows(ref, q, at):
        near = ref[pl.ds(q * span, span), at]
        far = ref[pl.ds(half + q * span, span), at]
        return jnp.concatenate([near, far], axis=0)

    xs = [rows(x_ref, q, slice(None)).T for q in range(SEQS)]
    for g_ref, f_ref in ((gg_ref, fg_ref), (gu_ref, fu_ref)):
        for c in range(width // step):
            at = pl.ds(c * step, step)
            total = None
            for q in range(SEQS):
                seq = jnp.dot(xs[q], rows(g_ref, q, at), preferred_element_type=jnp.float32)
                total = seq * seq if total is None else total + seq * seq
            f_ref[:, at] = (total * (1.0 / SEQS)).astype(jnp.bfloat16)


def plain_fisher(x, gg, gu):
    rows, depth = x.shape
    width = gg.shape[1]
    step = 512
    held = pl.BlockSpec((rows, width), lambda j: (0, 0))
    block = pl.BlockSpec((step, width), lambda j: (j, 0))
    return pl.pallas_call(
        functools.partial(plain_fisher_kernel, tile(width, 256)),
        grid=(depth // step,),
        in_specs=[pl.BlockSpec((rows, step), lambda j: (0, j)), held, held],
        out_specs=[block, block],
        out_shape=[jax.ShapeDtypeStruct((depth, width), jnp.bfloat16)] * 2,
        compiler_params=params(40),
        cost_estimate=cost(4 * rows * depth * width, 4 * depth * width),
        name="fisher",
    )(x, gg, gu)


def plain_part(size, tokens, grad_out, wg, wu, wd):
    chips = size // 2
    across = [[2 * i + c for i in range(chips)] for c in range(2)]
    pairs = [[2 * i, 2 * i + 1] for i in range(chips)]
    block, depth = tokens.shape

    def gather(rows):
        near = lax.all_gather(rows, "hid", axis=0, tiled=True, axis_index_groups=across)
        return lax.all_gather(near, "hid", axis=0, tiled=False, axis_index_groups=pairs)

    x = gather(tokens).reshape(-1, depth)
    dy = gather(grad_out).reshape(-1, depth)
    gate, up = plain_forward(x, wg, wu)
    gg, gu = plain_back(dy, wd, gate, up)
    terms = plain_input_terms(gg, gu, wg, wu).reshape(2, -1, depth)
    mine = lax.psum_scatter(
        terms, "hid", scatter_dimension=0, tiled=False, axis_index_groups=pairs
    )
    mine = lax.psum_scatter(
        mine, "hid", scatter_dimension=0, tiled=True, axis_index_groups=across
    )
    fg, fu = plain_fisher(x, gg, gu)
    return fg, fu, mine


def per_device(size, tokens, grad_out, wg, wu, wd):
    if size == 2 * len(CYCLE) and tokens.shape[0] % 32 == 0:
        return ring_part(tokens, grad_out, wg, wu, wd)
    return plain_part(size, tokens, grad_out, wg, wu, wd)


def solution(mesh):
    rows = P(("adjust", "hid"), None)
    weights = P("adjust", "hid")
    return jax.shard_map(
        functools.partial(per_device, mesh.shape["hid"]),
        mesh=mesh,
        in_specs=(rows, rows, weights, weights, rows),
        out_specs=(weights, weights, rows),
        check_vma=False,
    )
```

```python
import functools

import jax
import jax.numpy as jnp
from jax import lax
from jax.experimental import pallas as pl
from jax.experimental.pallas import tpu as pltpu
from jax.sharding import PartitionSpec as P

SEQS = 2
MIB = 1 << 20
CYCLE = (0, 2, 4, 6, 7, 5, 3, 1)
NT = (((1,), (1,)), ((), ()))
BF16 = jnp.bfloat16
F32 = jnp.float32


def tile(size, want):
    return want if size % want == 0 else size


def params(mib):
    return pltpu.CompilerParams(vmem_limit_bytes=mib * MIB)


def cost(flops, read):
    return pl.CostEstimate(flops=flops, bytes_accessed=read, transcendentals=0)


def any_specs(values):
    return [pl.BlockSpec(memory_space=pl.ANY)] * len(values)


def held_specs(count):
    return [pl.BlockSpec(memory_space=pltpu.VMEM)] * count


def pack_kernel(count, *refs):
    out_ref = refs[-1]
    start = 0
    for piece in refs[:count]:
        out_ref[pl.ds(start, piece.shape[0]), :] = piece[...]
        start += piece.shape[0]


def pack(pieces, after):
    depth = pieces[0].shape[1]
    rows = sum(piece.shape[0] for piece in pieces)
    whole = pl.BlockSpec(memory_space=pltpu.VMEM)
    return pl.pallas_call(
        functools.partial(pack_kernel, len(pieces)),
        in_specs=[whole] * len(pieces) + any_specs(after),
        out_specs=whole,
        out_shape=jax.ShapeDtypeStruct((rows, depth), BF16),
        compiler_params=params(8),
        cost_estimate=cost(0, 4 * rows * depth),
        name="pack",
    )(*pieces, *after)


def places(chips, row):
    span = chips // SEQS
    for q in range(SEQS):
        for side in range(2):
            for k in range(span):
                yield q * span + k, side, ((q * 2 + side) * span + k) * row


def arrange(spot_ref, near_ref, far_ref, out_ref):
    chips = spot_ref.shape[0]
    row = near_ref.shape[0] // chips
    for chip, side, place in places(chips, row):
        start = pl.multiple_of(spot_ref[chip] * row, row)
        out_ref[pl.ds(place, row), :] = (near_ref, far_ref)[side][pl.ds(start, row), :]


def gate_up_kernel(parts, spot_ref, near_ref, far_ref, wg_ref, wu_ref, *rest):
    a_ref, b_ref, x_ref = rest[-3:]

    @pl.when(pl.program_id(0) == 0)
    def _():
        arrange(spot_ref, near_ref, far_ref, x_ref)

    rows = x_ref.shape[0] // parts
    step = wg_ref.shape[1]
    to = pl.ds(pl.multiple_of(pl.program_id(0) * step, step), step)
    for p in range(parts):
        at = pl.ds(p * rows, rows)
        gate = jnp.dot(x_ref[at, :], wg_ref[...], preferred_element_type=F32)
        up = jnp.dot(x_ref[at, :], wu_ref[...], preferred_element_type=F32)
        sigma = jax.nn.sigmoid(gate)
        a_ref[at, to] = up * sigma * (1.0 + gate * (1.0 - sigma))
        b_ref[at, to] = gate * sigma


def gate_up(spot, near, far, wg, wu, after):
    rows, depth = near.shape
    width = wg.shape[1]
    step = tile(width, 256)
    column = pl.BlockSpec((depth, step), lambda j: (0, j))
    return pl.pallas_call(
        functools.partial(gate_up_kernel, 2),
        grid=(width // step,),
        in_specs=[pl.BlockSpec(memory_space=pltpu.SMEM)]
        + held_specs(2)
        + [column, column]
        + any_specs(after),
        out_specs=held_specs(3),
        out_shape=[jax.ShapeDtypeStruct((2 * rows, width), F32)] * 2
        + [jax.ShapeDtypeStruct((2 * rows, depth), BF16)],
        compiler_params=params(34),
        cost_estimate=cost(8 * rows * depth * width, 4 * depth * width),
        name="gate_up",
    )(spot, near, far, wg, wu, *after)


def back_kernel(
    tiles, spot_ref, near_ref, far_ref, wd_ref, a_ref, b_ref, wg_ref, wu_ref,
    gg_ref, gu_ref, own_ref, sent_ref, dy_ref,
):
    j = pl.program_id(0)
    chips = spot_ref.shape[0]
    row = near_ref.shape[0] // chips
    step = wd_ref.shape[0]

    @pl.when(j == 0)
    def _():
        arrange(spot_ref, near_ref, far_ref, dy_ref)

    @pl.when(j < tiles)
    def _():
        hidden = lax.dot_general(dy_ref[...], wd_ref[...], NT, preferred_element_type=F32)
        at = pl.ds(pl.multiple_of(j * step, step), step)
        gg_ref[:, at] = (hidden * a_ref[:, at]).astype(BF16)
        gu_ref[:, at] = (hidden * b_ref[:, at]).astype(BF16)

    @pl.when(j >= tiles)
    def _():
        total = lax.dot_general(gg_ref[...], wg_ref[...], NT, preferred_element_type=F32)
        total += lax.dot_general(gu_ref[...], wu_ref[...], NT, preferred_element_type=F32)
        for chip, side, place in places(chips, row):
            start = pl.multiple_of(spot_ref[chip] * row, row)
            terms = total[place : place + row, :]
            if side:
                sent_ref[pl.ds(start, row), :] = terms.astype(BF16)
            else:
                own_ref[pl.ds(start, row), :] = terms


def back(spot, near, far, wd, a, b, wg, wu):
    rows, depth = near.shape
    width = wd.shape[0]
    step = tile(width, 256)
    tiles = width // step
    deep = 256

    def early(j):
        return jnp.minimum(j, tiles - 1)

    def late(j):
        return jnp.maximum(j - tiles, 0)

    weight = pl.BlockSpec((deep, width), lambda j: (late(j), 0))
    terms = pl.BlockSpec((rows, deep), lambda j: (0, late(j)))
    return pl.pallas_call(
        functools.partial(back_kernel, tiles),
        grid=(tiles + depth // deep,),
        in_specs=[pl.BlockSpec(memory_space=pltpu.SMEM)]
        + held_specs(2)
        + [pl.BlockSpec((step, depth), lambda j: (early(j), 0))]
        + held_specs(2)
        + [weight, weight],
        out_specs=held_specs(2) + [terms, terms],
        out_shape=[jax.ShapeDtypeStruct((2 * rows, width), BF16)] * 2
        + [
            jax.ShapeDtypeStruct((rows, depth), F32),
            jax.ShapeDtypeStruct((rows, depth), BF16),
        ],
        scratch_shapes=[pltpu.VMEM((2 * rows, depth), BF16)],
        compiler_params=params(34),
        cost_estimate=cost(12 * rows * depth * width, 6 * depth * width),
        name="hidden_back",
    )(spot, near, far, wd, a, b, wg, wu)


def fold_kernel(cuts, *refs):
    count = len(cuts)
    outs = refs[-count:]
    for i, (at, got_at) in enumerate(cuts):
        own_ref, near_ref, got_ref = refs[3 * i : 3 * i + 3]
        out_ref = outs[i]
        out_ref[...] = (own_ref[at, :] + near_ref[at, :].astype(F32)).astype(BF16)
        if got_at is not None:
            total = own_ref[got_at, :] + near_ref[got_at, :].astype(F32)
            out_ref[got_at, :] = (total + got_ref[...].astype(F32)).astype(BF16)


def fold(own, near, row, sends, after):
    depth = own.shape[1]
    operands, specs, shapes, cuts = [], [], [], []
    for p, at, got_at, got in sends:
        block = pl.BlockSpec((row, depth), lambda i, p=p: (p, 0))
        got = near if got is None else got
        size = got.shape[0] if got_at is not None else row
        operands += [own, near, got]
        specs += [block, block, pl.BlockSpec((size, depth), lambda i: (0, 0))]
        shapes.append(jax.ShapeDtypeStruct((at.size, depth), BF16))
        cuts.append((at, got_at))
    return pl.pallas_call(
        functools.partial(fold_kernel, cuts),
        grid=(1,),
        in_specs=specs + any_specs(after),
        out_specs=[pl.BlockSpec(shape.shape, lambda i: (0, 0)) for shape in shapes],
        out_shape=shapes,
        compiler_params=params(24),
        cost_estimate=cost(0, 16 * row * depth),
        name="fold",
    )(*operands, *after)


def last_kernel(own_ref, near_ref, r_ref, l_ref, out_ref):
    total = own_ref[...] + near_ref[...].astype(F32)
    out_ref[...] = (total + r_ref[...].astype(F32) + l_ref[...].astype(F32)).astype(BF16)


def last(own, near, r, l):
    block = pl.BlockSpec(r.shape, lambda i: (0, 0))
    return pl.pallas_call(
        last_kernel,
        grid=(1,),
        in_specs=[block] * 4,
        out_specs=block,
        out_shape=jax.ShapeDtypeStruct(r.shape, BF16),
        compiler_params=params(24),
        cost_estimate=cost(0, 12 * r.size),
        name="last",
    )(own, near, r, l)


def fisher_kernel(step, first, x_ref, gg_ref, gu_ref, *rest):
    fg_ref, fu_ref, done_ref = rest[-3:]
    deep = fg_ref.shape[0]
    here = pl.ds(pl.multiple_of((first + pl.program_id(0)) * deep, deep), deep)
    done_ref[...] = jnp.zeros_like(done_ref)
    span = x_ref.shape[0] // SEQS
    seqs = [pl.ds(q * span, span) for q in range(SEQS)]
    cols = [x_ref[at, here].T for at in seqs]
    for g_ref, f_ref in ((gg_ref, fg_ref), (gu_ref, fu_ref)):
        for c in range(g_ref.shape[1] // step):
            at = pl.ds(c * step, step)
            total = None
            for q in range(SEQS):
                seq = jnp.dot(cols[q], g_ref[seqs[q], at], preferred_element_type=F32)
                total = seq * seq if total is None else total + seq * seq
            f_ref[:, at] = (total * (1.0 / SEQS)).astype(BF16)


def fisher(x, gg, gu, first, count, step, held, after):
    rows, depth = x.shape
    width = gg.shape[1]
    block = pl.BlockSpec((step, width), lambda j: (first + j, 0))
    return pl.pallas_call(
        functools.partial(fisher_kernel, tile(width, 256), first),
        grid=(count,),
        in_specs=held_specs(3) + any_specs((*held, *after)),
        out_specs=[block, block, pl.BlockSpec((8, 128), lambda j: (0, 0))],
        out_shape=[jax.ShapeDtypeStruct((depth, width), BF16)] * 2
        + [jax.ShapeDtypeStruct((8, 128), F32)],
        input_output_aliases={3 + i: i for i in range(len(held))},
        compiler_params=params(40),
        cost_estimate=cost(4 * rows * step * count * width, 4 * step * count * width),
        name="fisher",
    )(x, gg, gu, *held, *after)


def ring_part(tokens, grad_out, wg, wu, wd):
    chips = len(CYCLE)
    far = chips // 2
    row, depth = tokens.shape
    links = [(CYCLE[i], CYCLE[(i + 1) % chips]) for i in range(chips)]
    to_right = [(2 * a + c, 2 * b + c) for a, b in links for c in range(2)]
    to_left = [(b, a) for a, b in to_right]
    across = [(2 * i + c, 2 * i + 1 - c) for i in range(chips) for c in range(2)]

    def right(value):
        return lax.ppermute(value, "hid", to_right)

    def left(value):
        return lax.ppermute(value, "hid", to_left)

    def swap(value):
        return lax.ppermute(value, "hid", across)

    def gather_both(x, dy):
        r, l = [[x], [dy]], [[x], [dy]]
        halves = slice(None, row // 2), slice(row // 2, None)
        busy = ()
        for step in range(far + 1):
            live = [(i, step - i) for i in range(2) if 0 <= step - i < far]
            ends = [side[i][-1] for i, _ in live for side in (r, l)]
            ends, busy = lax.optimization_barrier((ends, busy))
            for at, (i, k) in enumerate(live):
                to_r, to_l = ends[2 * at : 2 * at + 2]
                if k == far - 1:
                    to_r, to_l = to_r[halves[0]], to_l[halves[1]]
                r[i].append(right(to_r))
                l[i].append(left(to_l))
            busy = [side[i][-1] for i, _ in live for side in (r, l)]
        return [r[i] + l[i][:0:-1] for i in range(2)]

    cycle = jnp.array([CYCLE.index(c) for c in range(chips)], jnp.int32)
    spot = (cycle[lax.axis_index("hid") // 2] - cycle) % chips

    blocks_x, blocks_dy = gather_both(tokens, grad_out)
    near_x = pack(blocks_x, (spot,))
    far_x = swap(near_x)
    near_dy = pack(blocks_dy, ())
    far_dy = swap(near_dy)
    a, b, x = gate_up(spot, near_x, far_x, wg, wu, (near_dy,))
    gg, gu, own, sent = back(spot, near_dy, far_dy, wd, a, b, wg, wu)

    near = swap(sent)
    full, head, tail = pl.ds(0, row), pl.ds(0, row // 2), pl.ds(row // 2, row // 2)
    step = 256
    counts = [4, 2, 4, 4, 2]
    held, first = (), 0
    r = l = None
    ready = ()
    for k in range(far, 0, -1):
        *held, done = fisher(x, gg, gu, first, counts[far - k], step, held, ready)
        first += counts[far - k]
        if k == far:
            sends = [(far, head, None, None), (far, tail, None, None)]
        elif k == far - 1:
            sends = [(chips - k, full, head, r), (k, full, tail, l)]
        else:
            sends = [(chips - k, full, full, r), (k, full, full, l)]
        ready = fold(own, near, row, sends, (done,))
        r, l = right(ready[0]), left(ready[1])
    fg, fu, _ = fisher(x, gg, gu, first, counts[far], step, held, ready)
    mine = last(own, near, r, l)
    return fg, fu, mine


def plain_forward_kernel(x_ref, wg_ref, wu_ref, gate_ref, up_ref):
    x = x_ref[...]
    gate_ref[...] = jnp.dot(x, wg_ref[...], preferred_element_type=jnp.float32)
    up_ref[...] = jnp.dot(x, wu_ref[...], preferred_element_type=jnp.float32)


def plain_forward(x, wg, wu):
    rows, depth = x.shape
    width = wg.shape[1]
    step = tile(width, 256)
    return pl.pallas_call(
        plain_forward_kernel,
        grid=(width // step,),
        in_specs=[
            pl.BlockSpec((rows, depth), lambda j: (0, 0)),
            pl.BlockSpec((depth, step), lambda j: (0, j)),
            pl.BlockSpec((depth, step), lambda j: (0, j)),
        ],
        out_specs=[pl.BlockSpec((rows, step), lambda j: (0, j))] * 2,
        out_shape=[jax.ShapeDtypeStruct((rows, width), jnp.float32)] * 2,
        compiler_params=params(40),
        cost_estimate=cost(4 * rows * depth * width, 4 * depth * width),
        name="gate_up",
    )(x, wg, wu)


def plain_back_kernel(parts, dy_ref, wd_ref, gate_ref, up_ref, gg_ref, gu_ref):
    rows = dy_ref.shape[0] // parts
    for p in range(parts):
        at = pl.ds(p * rows, rows)
        hidden = lax.dot_general(dy_ref[at, :], wd_ref[...], NT, preferred_element_type=jnp.float32)
        gate = gate_ref[at, :]
        sigma = jax.nn.sigmoid(gate)
        both = hidden * sigma
        gg_ref[at, :] = (both * up_ref[at, :] * (1.0 + gate * (1.0 - sigma))).astype(jnp.bfloat16)
        gu_ref[at, :] = (both * gate).astype(jnp.bfloat16)


def plain_back(dy, wd, gate, up):
    rows, depth = dy.shape
    width = wd.shape[0]
    step = tile(width, 256)
    column = pl.BlockSpec((rows, step), lambda j: (0, j))
    return pl.pallas_call(
        functools.partial(plain_back_kernel, 2),
        grid=(width // step,),
        in_specs=[
            pl.BlockSpec((rows, depth), lambda j: (0, 0)),
            pl.BlockSpec((step, depth), lambda j: (j, 0)),
            column,
            column,
        ],
        out_specs=[column, column],
        out_shape=[jax.ShapeDtypeStruct((rows, width), jnp.bfloat16)] * 2,
        compiler_params=params(40),
        cost_estimate=cost(2 * rows * depth * width, 2 * depth * width),
        name="hidden_back",
    )(dy, wd, gate, up)


def plain_input_kernel(gg_ref, gu_ref, wg_ref, wu_ref, out_ref):
    total = lax.dot_general(gg_ref[...], wg_ref[...], NT, preferred_element_type=jnp.float32)
    total += lax.dot_general(gu_ref[...], wu_ref[...], NT, preferred_element_type=jnp.float32)
    out_ref[...] = total.astype(jnp.bfloat16)


def plain_input_terms(gg, gu, wg, wu):
    rows, width = gg.shape
    depth = wg.shape[0]
    step = 512
    held = pl.BlockSpec((rows, width), lambda j: (0, 0))
    return pl.pallas_call(
        plain_input_kernel,
        grid=(depth // step,),
        in_specs=[
            held,
            held,
            pl.BlockSpec((step, width), lambda j: (j, 0)),
            pl.BlockSpec((step, width), lambda j: (j, 0)),
        ],
        out_specs=pl.BlockSpec((rows, step), lambda j: (0, j)),
        out_shape=jax.ShapeDtypeStruct((rows, depth), jnp.bfloat16),
        compiler_params=params(40),
        cost_estimate=cost(4 * rows * depth * width, 4 * depth * width),
        name="input_terms",
    )(gg, gu, wg, wu)


def plain_fisher_kernel(step, x_ref, gg_ref, gu_ref, fg_ref, fu_ref):
    half = x_ref.shape[0] // 2
    span = half // SEQS
    width = gg_ref.shape[1]

    def rows(ref, q, at):
        near = ref[pl.ds(q * span, span), at]
        far = ref[pl.ds(half + q * span, span), at]
        return jnp.concatenate([near, far], axis=0)

    xs = [rows(x_ref, q, slice(None)).T for q in range(SEQS)]
    for g_ref, f_ref in ((gg_ref, fg_ref), (gu_ref, fu_ref)):
        for c in range(width // step):
            at = pl.ds(c * step, step)
            total = None
            for q in range(SEQS):
                seq = jnp.dot(xs[q], rows(g_ref, q, at), preferred_element_type=jnp.float32)
                total = seq * seq if total is None else total + seq * seq
            f_ref[:, at] = (total * (1.0 / SEQS)).astype(jnp.bfloat16)


def plain_fisher(x, gg, gu):
    rows, depth = x.shape
    width = gg.shape[1]
    step = 512
    held = pl.BlockSpec((rows, width), lambda j: (0, 0))
    block = pl.BlockSpec((step, width), lambda j: (j, 0))
    return pl.pallas_call(
        functools.partial(plain_fisher_kernel, tile(width, 256)),
        grid=(depth // step,),
        in_specs=[pl.BlockSpec((rows, step), lambda j: (0, j)), held, held],
        out_specs=[block, block],
        out_shape=[jax.ShapeDtypeStruct((depth, width), jnp.bfloat16)] * 2,
        compiler_params=params(40),
        cost_estimate=cost(4 * rows * depth * width, 4 * depth * width),
        name="fisher",
    )(x, gg, gu)


def plain_part(size, tokens, grad_out, wg, wu, wd):
    chips = size // 2
    across = [[2 * i + c for i in range(chips)] for c in range(2)]
    pairs = [[2 * i, 2 * i + 1] for i in range(chips)]
    block, depth = tokens.shape

    def gather(rows):
        near = lax.all_gather(rows, "hid", axis=0, tiled=True, axis_index_groups=across)
        return lax.all_gather(near, "hid", axis=0, tiled=False, axis_index_groups=pairs)

    x = gather(tokens).reshape(-1, depth)
    dy = gather(grad_out).reshape(-1, depth)
    gate, up = plain_forward(x, wg, wu)
    gg, gu = plain_back(dy, wd, gate, up)
    terms = plain_input_terms(gg, gu, wg, wu).reshape(2, -1, depth)
    mine = lax.psum_scatter(
        terms, "hid", scatter_dimension=0, tiled=False, axis_index_groups=pairs
    )
    mine = lax.psum_scatter(
        mine, "hid", scatter_dimension=0, tiled=True, axis_index_groups=across
    )
    fg, fu = plain_fisher(x, gg, gu)
    return fg, fu, mine


def per_device(size, tokens, grad_out, wg, wu, wd):
    if size == 2 * len(CYCLE) and tokens.shape[0] % 32 == 0:
        return ring_part(tokens, grad_out, wg, wu, wd)
    return plain_part(size, tokens, grad_out, wg, wu, wd)


def solution(mesh):
    rows = P(("adjust", "hid"), None)
    weights = P("adjust", "hid")
    return jax.shard_map(
        functools.partial(per_device, mesh.shape["hid"]),
        mesh=mesh,
        in_specs=(rows, rows, weights, weights, rows),
        out_specs=(weights, weights, rows),
        check_vma=False,
    )
```

```python
import functools

import jax
import jax.numpy as jnp
from jax import lax
from jax.experimental import pallas as pl
from jax.experimental.pallas import tpu as pltpu
from jax.sharding import PartitionSpec as P

SEQS = 2
MIB = 1 << 20
CYCLE = (0, 2, 4, 6, 7, 5, 3, 1)
NT = (((1,), (1,)), ((), ()))
BF16 = jnp.bfloat16
F32 = jnp.float32


def tile(size, want):
    return want if size % want == 0 else size


def params(mib):
    return pltpu.CompilerParams(vmem_limit_bytes=mib * MIB)


def cost(flops, read):
    return pl.CostEstimate(flops=flops, bytes_accessed=read, transcendentals=0)


def any_specs(values):
    return [pl.BlockSpec(memory_space=pl.ANY)] * len(values)


def hbm_specs(count):
    return [pl.BlockSpec(memory_space=pltpu.HBM)] * count


def held_specs(count):
    return [pl.BlockSpec(memory_space=pltpu.VMEM)] * count


def pack_kernel(count, *refs):
    out_ref = refs[-1]
    start = 0
    for piece in refs[:count]:
        out_ref[pl.ds(start, piece.shape[0]), :] = piece[...]
        start += piece.shape[0]


def pack(pieces, after):
    depth = pieces[0].shape[1]
    rows = sum(piece.shape[0] for piece in pieces)
    whole = pl.BlockSpec(memory_space=pltpu.VMEM)
    return pl.pallas_call(
        functools.partial(pack_kernel, len(pieces)),
        in_specs=[whole] * len(pieces) + any_specs(after),
        out_specs=whole,
        out_shape=jax.ShapeDtypeStruct((rows, depth), BF16),
        compiler_params=params(8),
        cost_estimate=cost(0, 4 * rows * depth),
        name="pack",
    )(*pieces, *after)


def pack_turned_kernel(count, *refs):
    pieces, out_ref = refs[:count], refs[-1]
    step = 512
    for c in range(0, out_ref.shape[0], step):
        block = jnp.concatenate([piece[:, c : c + step] for piece in pieces], axis=0)
        out_ref[c : c + step, :] = block.T


def pack_turned(pieces, after):
    depth = pieces[0].shape[1]
    rows = sum(piece.shape[0] for piece in pieces)
    return pl.pallas_call(
        functools.partial(pack_turned_kernel, len(pieces)),
        in_specs=held_specs(len(pieces)) + any_specs(after),
        out_specs=pl.BlockSpec(memory_space=pltpu.VMEM),
        out_shape=jax.ShapeDtypeStruct((depth, rows), BF16),
        compiler_params=params(8),
        cost_estimate=cost(0, 4 * rows * depth),
        name="pack_turned",
    )(*pieces, *after)


def put_rows(spot_ref, side, value, out_ref, cols):
    chips = spot_ref.shape[0]
    row = value.shape[0] // chips
    for p in range(chips):
        start = pl.multiple_of(spot_ref[p] + side * chips // SEQS * row, row)
        out_ref[pl.ds(start, row), cols] = value[p * row : (p + 1) * row, :]


def arrange_kernel(spot_ref, near_ref, far_ref, *rest):
    for side, ref in enumerate((near_ref, far_ref)):
        put_rows(spot_ref, side, ref[...], rest[-1], slice(None))


def arrange(spot, near, far, after):
    rows, depth = near.shape
    return pl.pallas_call(
        arrange_kernel,
        in_specs=[pl.BlockSpec(memory_space=pltpu.SMEM)] + held_specs(2) + any_specs(after),
        out_specs=pl.BlockSpec(memory_space=pltpu.VMEM),
        out_shape=jax.ShapeDtypeStruct((2 * rows, depth), BF16),
        compiler_params=params(6),
        cost_estimate=cost(0, 8 * rows * depth),
        name="arrange",
    )(spot, near, far, *after)


CHUNKS = 4


def gate_up_kernel(first, step, near_ref, far_ref, wg_ref, wu_ref, *rest):
    a_ref, b_ref, w_buf, out_buf, sems, out_sems = rest[-6:]
    rows, depth = near_ref.shape
    part = depth // CHUNKS
    tiles = a_ref.shape[0] // step

    def fetch(t, k):
        cols, deep, slot = pl.ds((first + t) * step, step), pl.ds(k * part, part), t % 2
        return [
            pltpu.make_async_copy(w_ref.at[deep, cols], w_buf.at[slot, i, deep], sems.at[slot, i, k])
            for i, w_ref in enumerate((wg_ref, wu_ref))
        ]

    def store(t):
        to = pl.ds(t * step, step)
        return [
            pltpu.make_async_copy(out_buf.at[t, i], ref.at[to, :], out_sems.at[t, i])
            for i, ref in enumerate((a_ref, b_ref))
        ]

    def begin(t):
        for k in range(CHUNKS):
            for copy in fetch(t, k):
                copy.start()

    for t in range(min(2, tiles)):
        begin(t)
    for t in range(tiles):
        sums = [[None, None], [None, None]]
        for k in range(CHUNKS):
            deep = pl.ds(k * part, part)
            for copy in fetch(t, k):
                copy.wait()
            for side, x_ref in enumerate((near_ref, far_ref)):
                for i in range(2):
                    term = jnp.dot(
                        x_ref[:, deep], w_buf[t % 2, i, deep, :], preferred_element_type=F32
                    )
                    before = sums[side][i]
                    sums[side][i] = term if before is None else before + term
        if t + 2 < tiles:
            begin(t + 2)
        for side, (gate, up) in enumerate(sums):
            at = pl.ds(side * rows, rows)
            sigma = jax.nn.sigmoid(gate)
            out_buf[t, 0, :, at] = (up * sigma * (1.0 + gate * (1.0 - sigma))).T
            out_buf[t, 1, :, at] = (gate * sigma).T
        for copy in store(t):
            copy.start()
    for t in range(tiles):
        for copy in store(t):
            copy.wait()


def gate_up(near, far, wg, wu, first, count, step, grant, after):
    rows, depth = near.shape
    return pl.pallas_call(
        functools.partial(gate_up_kernel, first, step),
        in_specs=held_specs(2)
        + hbm_specs(2)
        + any_specs(after),
        out_specs=hbm_specs(2),
        out_shape=[jax.ShapeDtypeStruct((count * step, 2 * rows), F32)] * 2,
        scratch_shapes=[
            pltpu.VMEM((2, 2, depth, step), BF16),
            pltpu.VMEM((count, 2, step, 2 * rows), F32),
            pltpu.SemaphoreType.DMA((2, 2, CHUNKS)),
            pltpu.SemaphoreType.DMA((count, 2)),
        ],
        compiler_params=params(grant),
        cost_estimate=cost(8 * rows * depth * count * step, 4 * depth * count * step),
        name="gate_up",
    )(near, far, wg, wu, *after)


def back_kernel(step, deep, pieces, spot_ref, near_ref, far_ref, wg_ref, wu_ref, wd_ref, *refs):
    a_refs, b_refs = refs[:pieces], refs[pieces : 2 * pieces]
    ggs_ref, gus_ref, own_ref, sent_ref, gg_ref, gu_ref = refs[2 * pieces : 2 * pieces + 6]
    wd_buf, w_buf, factor_buf, sems, w_sems, factor_sems = refs[2 * pieces + 6 :]
    rows = near_ref.shape[1]
    tiles = wd_ref.shape[0] // step

    part = wd_ref.shape[1] // CHUNKS

    def fetch(t, k):
        at = pl.ds(pl.multiple_of(t * step, step), step)
        deep = pl.ds(k * part, part)
        slot = lax.rem(t, 2)
        return pltpu.make_async_copy(
            wd_ref.at[at, deep], wd_buf.at[slot, :, deep], sems.at[slot, k]
        )

    def fetch_rows(i):
        at = pl.ds(pl.multiple_of(i * deep, deep), deep)
        slot = lax.rem(i, 2)
        return [
            pltpu.make_async_copy(w_ref.at[at, :], w_buf.at[slot, k], w_sems.at[slot, k])
            for k, w_ref in enumerate((wg_ref, wu_ref))
        ]

    starts = [0]
    for a_ref in a_refs:
        starts.append(starts[-1] + a_ref.shape[0])

    def fetch_factors(p):
        at = pl.ds(starts[p], starts[p + 1] - starts[p])
        return [
            pltpu.make_async_copy(ref, factor_buf.at[k, at, :], factor_sems.at[k, p])
            for k, ref in enumerate((a_refs[p], b_refs[p]))
        ]

    blocks = wg_ref.shape[0] // deep
    for t in range(min(2, tiles)):
        for k in range(CHUNKS):
            fetch(jnp.int32(t), k).start()
        if t == 0:
            for copy in fetch_factors(0):
                copy.start()
    for p in range(pieces):
        if p + 1 < pieces:
            for copy in fetch_factors(p + 1):
                copy.start()
        else:
            for i in range(2):
                for copy in fetch_rows(jnp.int32(i)):
                    copy.start()
        for copy in fetch_factors(p):
            copy.wait()

        @pl.loop(starts[p] // step, starts[p + 1] // step)
        def _(t):
            cols = pl.ds(pl.multiple_of(t * step, step), step)
            sums = [None, None]
            for k in range(CHUNKS):
                deep_k = pl.ds(k * part, part)
                fetch(t, k).wait()
                for side, dy_ref in enumerate((near_ref, far_ref)):
                    term = jnp.dot(
                        wd_buf[lax.rem(t, 2), :, deep_k], dy_ref[deep_k, :],
                        preferred_element_type=F32,
                    )
                    sums[side] = term if sums[side] is None else sums[side] + term
            for side, hidden in enumerate(sums):
                at = pl.ds(side * rows, rows)
                for f, (g_ref, gs_ref) in enumerate(((gg_ref, ggs_ref), (gu_ref, gus_ref))):
                    grad = (hidden * factor_buf[f, cols, at]).astype(BF16)
                    g_ref[cols, at] = grad
                    put_rows(spot_ref, side, grad.T, gs_ref, cols)

            @pl.when(t + 2 < tiles)
            def _():
                for k in range(CHUNKS):
                    fetch(t + 2, k).start()

    @pl.loop(0, blocks)
    def _(i):
        at = pl.ds(pl.multiple_of(i * deep, deep), deep)
        slot = lax.rem(i, 2)
        for copy in fetch_rows(i):
            copy.wait()
        for side, out_ref in enumerate((own_ref, sent_ref)):
            of = pl.ds(side * rows, rows)
            total = jnp.dot(w_buf[slot, 0], gg_ref[:, of], preferred_element_type=F32)
            total += jnp.dot(w_buf[slot, 1], gu_ref[:, of], preferred_element_type=F32)
            out_ref[:, at] = total.astype(BF16).T

        @pl.when(i + 2 < blocks)
        def _():
            for copy in fetch_rows(i + 2):
                copy.start()


def back(spot, near, far, wg, wu, wd, factors):
    depth, rows = near.shape
    width = wd.shape[0]
    step = tile(width, 256)
    a = [pair[0] for pair in factors]
    b = [pair[1] for pair in factors]
    return pl.pallas_call(
        functools.partial(back_kernel, step, 512, len(a)),
        in_specs=[pl.BlockSpec(memory_space=pltpu.SMEM)]
        + held_specs(2)
        + hbm_specs(3)
        + any_specs(a + b),
        out_specs=held_specs(4),
        out_shape=[jax.ShapeDtypeStruct((2 * rows, width), BF16)] * 2
        + [jax.ShapeDtypeStruct((rows, depth), BF16)] * 2,
        scratch_shapes=[pltpu.VMEM((width, 2 * rows), BF16)] * 2
        + [
            pltpu.VMEM((2, step, depth), BF16),
            pltpu.VMEM((2, 2, 512, width), BF16),
            pltpu.VMEM((2, width, 2 * rows), F32),
            pltpu.SemaphoreType.DMA((2, CHUNKS)),
            pltpu.SemaphoreType.DMA((2, 2)),
            pltpu.SemaphoreType.DMA((2, len(a))),
        ],
        compiler_params=params(28),
        cost_estimate=cost(12 * rows * depth * width, 6 * depth * width),
        name="hidden_back",
    )(spot, near, far, wg, wu, wd, *a, *b)


def fold_kernel(cuts, *refs):
    count = len(cuts)
    outs = refs[-count:]
    for i, (at, got_at) in enumerate(cuts):
        own_ref, near_ref, got_ref = refs[3 * i : 3 * i + 3]
        out_ref = outs[i]
        out_ref[...] = (own_ref[at, :].astype(F32) + near_ref[at, :].astype(F32)).astype(BF16)
        if got_at is not None:
            total = own_ref[got_at, :].astype(F32) + near_ref[got_at, :].astype(F32)
            out_ref[got_at, :] = (total + got_ref[...].astype(F32)).astype(BF16)


def fold(own, near, row, sends, after):
    depth = own.shape[1]
    operands, specs, shapes, cuts = [], [], [], []
    for p, at, got_at, got in sends:
        block = pl.BlockSpec((row, depth), lambda i, p=p: (p, 0))
        got = near if got is None else got
        size = got.shape[0] if got_at is not None else row
        operands += [own, near, got]
        specs += [block, block, pl.BlockSpec((size, depth), lambda i: (0, 0))]
        shapes.append(jax.ShapeDtypeStruct((at.size, depth), BF16))
        cuts.append((at, got_at))
    return pl.pallas_call(
        functools.partial(fold_kernel, cuts),
        grid=(1,),
        in_specs=specs + any_specs(after),
        out_specs=[pl.BlockSpec(shape.shape, lambda i: (0, 0)) for shape in shapes],
        out_shape=shapes,
        compiler_params=params(24),
        cost_estimate=cost(0, 16 * row * depth),
        name="fold",
    )(*operands, *after)


def last_kernel(own_ref, near_ref, r_ref, l_ref, out_ref):
    total = own_ref[...].astype(F32) + near_ref[...].astype(F32)
    out_ref[...] = (total + r_ref[...].astype(F32) + l_ref[...].astype(F32)).astype(BF16)


def last(own, near, r, l):
    block = pl.BlockSpec(r.shape, lambda i: (0, 0))
    return pl.pallas_call(
        last_kernel,
        grid=(1,),
        in_specs=[block] * 4,
        out_specs=block,
        out_shape=jax.ShapeDtypeStruct(r.shape, BF16),
        compiler_params=params(24),
        cost_estimate=cost(0, 12 * r.size),
        name="last",
    )(own, near, r, l)


def fisher_kernel(step, x_ref, gg_ref, gu_ref, *rest):
    fg_ref, fu_ref, done_ref = rest[-3:]
    done_ref[...] = jnp.zeros_like(done_ref)
    span = x_ref.shape[0] // SEQS
    seqs = [pl.ds(q * span, span) for q in range(SEQS)]
    cols = [x_ref[at, :].T for at in seqs]
    for g_ref, f_ref in ((gg_ref, fg_ref), (gu_ref, fu_ref)):
        for c in range(g_ref.shape[1] // step):
            at = pl.ds(c * step, step)
            total = None
            for q in range(SEQS):
                seq = jnp.dot(cols[q], g_ref[seqs[q], at], preferred_element_type=F32)
                total = seq * seq if total is None else total + seq * seq
            f_ref[:, at] = (total * (1.0 / SEQS)).astype(BF16)


def fisher(x, gg, gu, first, count, step, held, after):
    rows, depth = x.shape
    width = gg.shape[1]
    block = pl.BlockSpec((step, width), lambda j: (first + j, 0))
    return pl.pallas_call(
        functools.partial(fisher_kernel, tile(width, 256)),
        grid=(count,),
        in_specs=[pl.BlockSpec((rows, step), lambda j: (0, first + j))]
        + held_specs(2)
        + any_specs((*held, *after)),
        out_specs=[block, block, pl.BlockSpec((8, 128), lambda j: (0, 0))],
        out_shape=[jax.ShapeDtypeStruct((depth, width), BF16)] * 2
        + [jax.ShapeDtypeStruct((8, 128), F32)],
        input_output_aliases={3 + i: i for i in range(len(held))},
        compiler_params=params(40),
        cost_estimate=cost(4 * rows * step * count * width, 4 * step * count * width),
        name="fisher",
    )(x, gg, gu, *held, *after)


def ring_part(tokens, grad_out, wg, wu, wd):
    chips = len(CYCLE)
    far = chips // 2
    row, depth = tokens.shape
    width = wg.shape[1]
    links = [(CYCLE[i], CYCLE[(i + 1) % chips]) for i in range(chips)]
    to_right = [(2 * a + c, 2 * b + c) for a, b in links for c in range(2)]
    to_left = [(b, a) for a, b in to_right]
    across = [(2 * i + c, 2 * i + 1 - c) for i in range(chips) for c in range(2)]

    def right(value):
        return lax.ppermute(value, "hid", to_right)

    def left(value):
        return lax.ppermute(value, "hid", to_left)

    def swap(value):
        return lax.ppermute(value, "hid", across)

    cycle = jnp.array(CYCLE, jnp.int32)
    where = jnp.array([CYCLE.index(c) for c in range(chips)], jnp.int32)
    around = jnp.arange(chips, dtype=jnp.int32)
    chip = cycle[(where[lax.axis_index("hid") // 2] - around) % chips]
    span = chips // SEQS
    spot = (chip // span * 2 * span + chip % span) * row

    def both(r, l, after=()):
        (r, l), _ = lax.optimization_barrier(((r, l), after))
        return right(r), left(l)

    def halves(r, l):
        return r[: row // 2], l[row // 2 :]

    def blocks(own, rounds):
        return [own] + [r for r, _ in rounds] + [l for _, l in rounds[::-1]]

    lane = tile(width, 256)
    tiles = width // lane
    cuts = [0, 2, 5, 7] if tiles == 7 else [0, 0, 0, tiles]

    def piece(i, after):
        if cuts[i] == cuts[i + 1]:
            return []
        count = cuts[i + 1] - cuts[i]
        grant = (40, 38, 32)[i]
        return [gate_up(near_x, far_x, wg, wu, cuts[i], count, lane, grant, after)]

    in_x = [both(tokens, tokens)]
    for _ in range(2, far):
        in_x.append(both(*in_x[-1]))
    in_x.append(both(*halves(*in_x[-1])))
    near_x = pack(blocks(tokens, in_x), (spot,))
    far_x = swap(near_x)

    in_dy = [both(grad_out, grad_out, in_x[-2])]
    in_dy.append(both(*in_dy[-1]))
    factors = piece(0, in_dy[0])
    in_dy.append(both(*in_dy[-1], factors))
    factors += piece(1, in_dy[1])
    in_dy.append(both(*halves(*in_dy[-1]), factors))
    x = arrange(spot, near_x, far_x, in_dy[2])
    near_dy = pack_turned(blocks(grad_out, in_dy), (x,))
    far_dy = swap(near_dy)
    factors += piece(2, (near_dy,))
    gg, gu, own, sent = back(spot, near_dy, far_dy, wg, wu, wd, factors)

    near = swap(sent)
    full, head, tail = pl.ds(0, row), pl.ds(0, row // 2), pl.ds(row // 2, row // 2)
    step = 256
    counts = [4, 2, 4, 4, 2]
    held, first = (), 0
    r = l = None
    ready = ()
    for k in range(far, 0, -1):
        *held, done = fisher(x, gg, gu, first, counts[far - k], step, held, ready)
        first += counts[far - k]
        if k == far:
            sends = [(far, head, None, None), (far, tail, None, None)]
        elif k == far - 1:
            sends = [(chips - k, full, head, r), (k, full, tail, l)]
        else:
            sends = [(chips - k, full, full, r), (k, full, full, l)]
        ready = fold(own, near, row, sends, (done,))
        r, l = right(ready[0]), left(ready[1])
    fg, fu, _ = fisher(x, gg, gu, first, counts[far], step, held, ready)
    mine = last(own, near, r, l)
    return fg, fu, mine


def plain_forward_kernel(x_ref, wg_ref, wu_ref, gate_ref, up_ref):
    x = x_ref[...]
    gate_ref[...] = jnp.dot(x, wg_ref[...], preferred_element_type=jnp.float32)
    up_ref[...] = jnp.dot(x, wu_ref[...], preferred_element_type=jnp.float32)


def plain_forward(x, wg, wu):
    rows, depth = x.shape
    width = wg.shape[1]
    step = tile(width, 256)
    return pl.pallas_call(
        plain_forward_kernel,
        grid=(width // step,),
        in_specs=[
            pl.BlockSpec((rows, depth), lambda j: (0, 0)),
            pl.BlockSpec((depth, step), lambda j: (0, j)),
            pl.BlockSpec((depth, step), lambda j: (0, j)),
        ],
        out_specs=[pl.BlockSpec((rows, step), lambda j: (0, j))] * 2,
        out_shape=[jax.ShapeDtypeStruct((rows, width), jnp.float32)] * 2,
        compiler_params=params(40),
        cost_estimate=cost(4 * rows * depth * width, 4 * depth * width),
        name="gate_up",
    )(x, wg, wu)


def plain_back_kernel(parts, dy_ref, wd_ref, gate_ref, up_ref, gg_ref, gu_ref):
    rows = dy_ref.shape[0] // parts
    for p in range(parts):
        at = pl.ds(p * rows, rows)
        hidden = lax.dot_general(dy_ref[at, :], wd_ref[...], NT, preferred_element_type=jnp.float32)
        gate = gate_ref[at, :]
        sigma = jax.nn.sigmoid(gate)
        both = hidden * sigma
        gg_ref[at, :] = (both * up_ref[at, :] * (1.0 + gate * (1.0 - sigma))).astype(jnp.bfloat16)
        gu_ref[at, :] = (both * gate).astype(jnp.bfloat16)


def plain_back(dy, wd, gate, up):
    rows, depth = dy.shape
    width = wd.shape[0]
    step = tile(width, 256)
    column = pl.BlockSpec((rows, step), lambda j: (0, j))
    return pl.pallas_call(
        functools.partial(plain_back_kernel, 2),
        grid=(width // step,),
        in_specs=[
            pl.BlockSpec((rows, depth), lambda j: (0, 0)),
            pl.BlockSpec((step, depth), lambda j: (j, 0)),
            column,
            column,
        ],
        out_specs=[column, column],
        out_shape=[jax.ShapeDtypeStruct((rows, width), jnp.bfloat16)] * 2,
        compiler_params=params(40),
        cost_estimate=cost(2 * rows * depth * width, 2 * depth * width),
        name="hidden_back",
    )(dy, wd, gate, up)


def plain_input_kernel(gg_ref, gu_ref, wg_ref, wu_ref, out_ref):
    total = lax.dot_general(gg_ref[...], wg_ref[...], NT, preferred_element_type=jnp.float32)
    total += lax.dot_general(gu_ref[...], wu_ref[...], NT, preferred_element_type=jnp.float32)
    out_ref[...] = total.astype(jnp.bfloat16)


def plain_input_terms(gg, gu, wg, wu):
    rows, width = gg.shape
    depth = wg.shape[0]
    step = 512
    held = pl.BlockSpec((rows, width), lambda j: (0, 0))
    return pl.pallas_call(
        plain_input_kernel,
        grid=(depth // step,),
        in_specs=[
            held,
            held,
            pl.BlockSpec((step, width), lambda j: (j, 0)),
            pl.BlockSpec((step, width), lambda j: (j, 0)),
        ],
        out_specs=pl.BlockSpec((rows, step), lambda j: (0, j)),
        out_shape=jax.ShapeDtypeStruct((rows, depth), jnp.bfloat16),
        compiler_params=params(40),
        cost_estimate=cost(4 * rows * depth * width, 4 * depth * width),
        name="input_terms",
    )(gg, gu, wg, wu)


def plain_fisher_kernel(step, x_ref, gg_ref, gu_ref, fg_ref, fu_ref):
    half = x_ref.shape[0] // 2
    span = half // SEQS
    width = gg_ref.shape[1]

    def rows(ref, q, at):
        near = ref[pl.ds(q * span, span), at]
        far = ref[pl.ds(half + q * span, span), at]
        return jnp.concatenate([near, far], axis=0)

    xs = [rows(x_ref, q, slice(None)).T for q in range(SEQS)]
    for g_ref, f_ref in ((gg_ref, fg_ref), (gu_ref, fu_ref)):
        for c in range(width // step):
            at = pl.ds(c * step, step)
            total = None
            for q in range(SEQS):
                seq = jnp.dot(xs[q], rows(g_ref, q, at), preferred_element_type=jnp.float32)
                total = seq * seq if total is None else total + seq * seq
            f_ref[:, at] = (total * (1.0 / SEQS)).astype(jnp.bfloat16)


def plain_fisher(x, gg, gu):
    rows, depth = x.shape
    width = gg.shape[1]
    step = 512
    held = pl.BlockSpec((rows, width), lambda j: (0, 0))
    block = pl.BlockSpec((step, width), lambda j: (j, 0))
    return pl.pallas_call(
        functools.partial(plain_fisher_kernel, tile(width, 256)),
        grid=(depth // step,),
        in_specs=[pl.BlockSpec((rows, step), lambda j: (0, j)), held, held],
        out_specs=[block, block],
        out_shape=[jax.ShapeDtypeStruct((depth, width), jnp.bfloat16)] * 2,
        compiler_params=params(40),
        cost_estimate=cost(4 * rows * depth * width, 4 * depth * width),
        name="fisher",
    )(x, gg, gu)


def plain_part(size, tokens, grad_out, wg, wu, wd):
    chips = size // 2
    across = [[2 * i + c for i in range(chips)] for c in range(2)]
    pairs = [[2 * i, 2 * i + 1] for i in range(chips)]
    block, depth = tokens.shape

    def gather(rows):
        near = lax.all_gather(rows, "hid", axis=0, tiled=True, axis_index_groups=across)
        return lax.all_gather(near, "hid", axis=0, tiled=False, axis_index_groups=pairs)

    x = gather(tokens).reshape(-1, depth)
    dy = gather(grad_out).reshape(-1, depth)
    gate, up = plain_forward(x, wg, wu)
    gg, gu = plain_back(dy, wd, gate, up)
    terms = plain_input_terms(gg, gu, wg, wu).reshape(2, -1, depth)
    mine = lax.psum_scatter(
        terms, "hid", scatter_dimension=0, tiled=False, axis_index_groups=pairs
    )
    mine = lax.psum_scatter(
        mine, "hid", scatter_dimension=0, tiled=True, axis_index_groups=across
    )
    fg, fu = plain_fisher(x, gg, gu)
    return fg, fu, mine


def per_device(size, tokens, grad_out, wg, wu, wd):
    if size == 2 * len(CYCLE) and tokens.shape[0] % 32 == 0:
        return ring_part(tokens, grad_out, wg, wu, wd)
    return plain_part(size, tokens, grad_out, wg, wu, wd)


def solution(mesh):
    rows = P(("adjust", "hid"), None)
    weights = P("adjust", "hid")
    return jax.shard_map(
        functools.partial(per_device, mesh.shape["hid"]),
        mesh=mesh,
        in_specs=(rows, rows, weights, weights, rows),
        out_specs=(weights, weights, rows),
        check_vma=False,
    )
```

```python
import functools

import jax
import jax.numpy as jnp
from jax import lax
from jax.experimental import pallas as pl
from jax.experimental.pallas import tpu as pltpu
from jax.sharding import PartitionSpec as P

SEQS = 2
MIB = 1 << 20
CYCLE = (0, 2, 4, 6, 7, 5, 3, 1)
NT = (((1,), (1,)), ((), ()))
BF16 = jnp.bfloat16
F32 = jnp.float32


def tile(size, want):
    return want if size % want == 0 else size


def params(mib):
    return pltpu.CompilerParams(vmem_limit_bytes=mib * MIB)


def cost(flops, read):
    return pl.CostEstimate(flops=flops, bytes_accessed=read, transcendentals=0)


def any_specs(values):
    return [pl.BlockSpec(memory_space=pl.ANY)] * len(values)


def hbm_specs(count):
    return [pl.BlockSpec(memory_space=pltpu.HBM)] * count


def held_specs(count):
    return [pl.BlockSpec(memory_space=pltpu.VMEM)] * count


def bring_kernel(x_ref, dy_ref, x_out, dy_out):
    x_out[...] = x_ref[...]
    dy_out[...] = dy_ref[...]


def bring(x, dy):
    return pl.pallas_call(
        bring_kernel,
        in_specs=held_specs(2),
        out_specs=held_specs(2),
        out_shape=[jax.ShapeDtypeStruct(x.shape, BF16)] * 2,
        compiler_params=params(4),
        cost_estimate=cost(0, 8 * x.size),
        name="bring",
    )(x, dy)


def pack_kernel(count, *refs):
    out_ref = refs[-1]
    start = 0
    for piece in refs[:count]:
        out_ref[pl.ds(start, piece.shape[0]), :] = piece[...]
        start += piece.shape[0]


def pack(pieces, after):
    depth = pieces[0].shape[1]
    rows = sum(piece.shape[0] for piece in pieces)
    whole = pl.BlockSpec(memory_space=pltpu.VMEM)
    return pl.pallas_call(
        functools.partial(pack_kernel, len(pieces)),
        in_specs=[whole] * len(pieces) + any_specs(after),
        out_specs=whole,
        out_shape=jax.ShapeDtypeStruct((rows, depth), BF16),
        compiler_params=params(8),
        cost_estimate=cost(0, 4 * rows * depth),
        name="pack",
    )(*pieces, *after)


def pack_turned_kernel(count, *refs):
    pieces, out_ref = refs[:count], refs[-1]
    step = 512
    for c in range(0, out_ref.shape[0], step):
        block = jnp.concatenate([piece[:, c : c + step] for piece in pieces], axis=0)
        out_ref[c : c + step, :] = block.T


def pack_turned(pieces, after):
    depth = pieces[0].shape[1]
    rows = sum(piece.shape[0] for piece in pieces)
    return pl.pallas_call(
        functools.partial(pack_turned_kernel, len(pieces)),
        in_specs=held_specs(len(pieces)) + any_specs(after),
        out_specs=pl.BlockSpec(memory_space=pltpu.VMEM),
        out_shape=jax.ShapeDtypeStruct((depth, rows), BF16),
        compiler_params=params(8),
        cost_estimate=cost(0, 4 * rows * depth),
        name="pack_turned",
    )(*pieces, *after)


def put_rows(spot_ref, side, value, out_ref, cols):
    chips = spot_ref.shape[0]
    row = value.shape[0] // chips
    for p in range(chips):
        start = pl.multiple_of(spot_ref[p] + side * chips // SEQS * row, row)
        out_ref[pl.ds(start, row), cols] = value[p * row : (p + 1) * row, :]


def arrange_kernel(spot_ref, near_ref, far_ref, *rest):
    for side, ref in enumerate((near_ref, far_ref)):
        put_rows(spot_ref, side, ref[...], rest[-1], slice(None))


def arrange(spot, near, far, after):
    rows, depth = near.shape
    return pl.pallas_call(
        arrange_kernel,
        in_specs=[pl.BlockSpec(memory_space=pltpu.SMEM)] + held_specs(2) + any_specs(after),
        out_specs=pl.BlockSpec(memory_space=pltpu.VMEM),
        out_shape=jax.ShapeDtypeStruct((2 * rows, depth), BF16),
        compiler_params=params(6),
        cost_estimate=cost(0, 8 * rows * depth),
        name="arrange",
    )(spot, near, far, *after)


CHUNKS = 4


def gate_up_kernel(first, step, near_ref, far_ref, wg_ref, wu_ref, *rest):
    a_ref, b_ref, w_buf, out_buf, sems, out_sems = rest[-6:]
    rows, depth = near_ref.shape
    part = depth // CHUNKS
    tiles = a_ref.shape[0] // step

    def fetch(t, k):
        cols, deep, slot = pl.ds((first + t) * step, step), pl.ds(k * part, part), t % 2
        return [
            pltpu.make_async_copy(w_ref.at[deep, cols], w_buf.at[slot, i, deep], sems.at[slot, i, k])
            for i, w_ref in enumerate((wg_ref, wu_ref))
        ]

    def store(t):
        to = pl.ds(t * step, step)
        return [
            pltpu.make_async_copy(out_buf.at[t, i], ref.at[to, :], out_sems.at[t, i])
            for i, ref in enumerate((a_ref, b_ref))
        ]

    def begin(t):
        for k in range(CHUNKS):
            for copy in fetch(t, k):
                copy.start()

    for t in range(min(2, tiles)):
        begin(t)
    for t in range(tiles):
        sums = [[None, None], [None, None]]
        pieces = CHUNKS if t == 0 else 1
        for k in range(pieces):
            deep = pl.ds(k * (depth // pieces), depth // pieces)
            for c in range(k, k + 1) if t == 0 else range(CHUNKS):
                for copy in fetch(t, c):
                    copy.wait()
            for side, x_ref in enumerate((near_ref, far_ref)):
                for i in range(2):
                    term = jnp.dot(
                        x_ref[:, deep], w_buf[t % 2, i, deep, :], preferred_element_type=F32
                    )
                    before = sums[side][i]
                    sums[side][i] = term if before is None else before + term
        if t + 2 < tiles:
            begin(t + 2)
        for side, (gate, up) in enumerate(sums):
            at = pl.ds(side * rows, rows)
            sigma = jax.nn.sigmoid(gate)
            out_buf[t, 0, :, at] = (up * sigma * (1.0 + gate * (1.0 - sigma))).T
            out_buf[t, 1, :, at] = (gate * sigma).T
        for copy in store(t):
            copy.start()
    for t in range(tiles):
        for copy in store(t):
            copy.wait()


def gate_up(near, far, wg, wu, first, count, step, grant, after):
    rows, depth = near.shape
    return pl.pallas_call(
        functools.partial(gate_up_kernel, first, step),
        in_specs=held_specs(2)
        + hbm_specs(2)
        + any_specs(after),
        out_specs=hbm_specs(2),
        out_shape=[jax.ShapeDtypeStruct((count * step, 2 * rows), F32)] * 2,
        scratch_shapes=[
            pltpu.VMEM((2, 2, depth, step), BF16),
            pltpu.VMEM((count, 2, step, 2 * rows), F32),
            pltpu.SemaphoreType.DMA((2, 2, CHUNKS)),
            pltpu.SemaphoreType.DMA((count, 2)),
        ],
        compiler_params=params(grant),
        cost_estimate=cost(8 * rows * depth * count * step, 4 * depth * count * step),
        name="gate_up",
    )(near, far, wg, wu, *after)


def back_kernel(step, deep, pieces, spot_ref, near_ref, far_ref, wg_ref, wu_ref, wd_ref, *refs):
    a_refs, b_refs = refs[:pieces], refs[pieces : 2 * pieces]
    ggs_ref, gus_ref, own_ref, sent_ref, g_ref = refs[2 * pieces : 2 * pieces + 5]
    wd_buf, w_buf, factor_buf, sems, w_sems, factor_sems = refs[2 * pieces + 5 :]
    width = wg_ref.shape[1]
    rows = near_ref.shape[1]
    tiles = wd_ref.shape[0] // step

    part = wd_ref.shape[1] // CHUNKS

    def fetch(t, k):
        at = pl.ds(pl.multiple_of(t * step, step), step)
        deep = pl.ds(k * part, part)
        slot = lax.rem(t, 2)
        return pltpu.make_async_copy(
            wd_ref.at[at, deep], wd_buf.at[slot, :, deep], sems.at[slot, k]
        )

    def fetch_rows(i):
        at = pl.ds(pl.multiple_of(i * deep, deep), deep)
        slot = lax.rem(i, 2)
        return [
            pltpu.make_async_copy(
                w_ref.at[at, :], w_buf.at[slot, :, pl.ds(k * width, width)], w_sems.at[slot, k]
            )
            for k, w_ref in enumerate((wg_ref, wu_ref))
        ]

    starts = [0]
    for a_ref in a_refs:
        starts.append(starts[-1] + a_ref.shape[0])

    def fetch_factors(p):
        at = pl.ds(starts[p], starts[p + 1] - starts[p])
        return [
            pltpu.make_async_copy(ref, factor_buf.at[k, at, :], factor_sems.at[k, p])
            for k, ref in enumerate((a_refs[p], b_refs[p]))
        ]

    def hidden_tile(t, pieces):
        cols = pl.ds(pl.multiple_of(t * step, step), step)
        sums = [None, None]
        size = wd_ref.shape[1] // pieces
        for k in range(pieces):
            part_k = pl.ds(k * size, size)
            for c in range(k, k + 1) if pieces > 1 else range(CHUNKS):
                fetch(t, c).wait()
            for side, dy_ref in enumerate((near_ref, far_ref)):
                term = jnp.dot(
                    wd_buf[lax.rem(t, 2), :, part_k], dy_ref[part_k, :],
                    preferred_element_type=F32,
                )
                sums[side] = term if sums[side] is None else sums[side] + term
        for side, hidden in enumerate(sums):
            at = pl.ds(side * rows, rows)
            for f, gs_ref in enumerate((ggs_ref, gus_ref)):
                grad = (hidden * factor_buf[f, cols, at]).astype(BF16)
                to = pl.multiple_of(t * step + f * width, step)
                g_ref[pl.ds(to, step), at] = grad
                put_rows(spot_ref, side, grad.T, gs_ref, cols)

        @pl.when(t + 2 < tiles)
        def _():
            for k in range(CHUNKS):
                fetch(t + 2, k).start()

    blocks = wg_ref.shape[0] // deep
    for t in range(min(2, tiles)):
        for k in range(CHUNKS):
            fetch(jnp.int32(t), k).start()
        if t == 0:
            for copy in fetch_factors(0):
                copy.start()
    for p in range(pieces):
        if p + 1 < pieces:
            for copy in fetch_factors(p + 1):
                copy.start()
        else:
            for i in range(2):
                for copy in fetch_rows(jnp.int32(i)):
                    copy.start()
        for copy in fetch_factors(p):
            copy.wait()

        if p == 0:
            hidden_tile(0, CHUNKS)

        @pl.loop(max(starts[p] // step, 1), starts[p + 1] // step)
        def _(t):
            hidden_tile(t, 1)

    @pl.loop(0, blocks)
    def _(i):
        at = pl.ds(pl.multiple_of(i * deep, deep), deep)
        slot = lax.rem(i, 2)
        for copy in fetch_rows(i):
            copy.wait()
        for side, out_ref in enumerate((own_ref, sent_ref)):
            of = pl.ds(side * rows, rows)
            total = jnp.dot(w_buf[slot], g_ref[:, of], preferred_element_type=F32)
            out_ref[:, at] = total.astype(BF16).T

        @pl.when(i + 2 < blocks)
        def _():
            for copy in fetch_rows(i + 2):
                copy.start()


def back(spot, near, far, wg, wu, wd, factors):
    depth, rows = near.shape
    width = wd.shape[0]
    step = tile(width, 256)
    a = [pair[0] for pair in factors]
    b = [pair[1] for pair in factors]
    return pl.pallas_call(
        functools.partial(back_kernel, step, 512, len(a)),
        in_specs=[pl.BlockSpec(memory_space=pltpu.SMEM)]
        + held_specs(2)
        + hbm_specs(3)
        + any_specs(a + b),
        out_specs=held_specs(4),
        out_shape=[jax.ShapeDtypeStruct((2 * rows, width), BF16)] * 2
        + [jax.ShapeDtypeStruct((rows, depth), BF16)] * 2,
        scratch_shapes=[
            pltpu.VMEM((2 * width, 2 * rows), BF16),
            pltpu.VMEM((2, step, depth), BF16),
            pltpu.VMEM((2, 512, 2 * width), BF16),
            pltpu.VMEM((2, width, 2 * rows), F32),
            pltpu.SemaphoreType.DMA((2, CHUNKS)),
            pltpu.SemaphoreType.DMA((2, 2)),
            pltpu.SemaphoreType.DMA((2, len(a))),
        ],
        compiler_params=params(28),
        cost_estimate=cost(12 * rows * depth * width, 6 * depth * width),
        name="hidden_back",
    )(spot, near, far, wg, wu, wd, *a, *b)


def fold_kernel(cuts, *refs):
    count = len(cuts)
    outs = refs[-count:]
    for i, (at, got_at) in enumerate(cuts):
        own_ref, near_ref, got_ref = refs[3 * i : 3 * i + 3]
        out_ref = outs[i]
        out_ref[...] = (own_ref[at, :].astype(F32) + near_ref[at, :].astype(F32)).astype(BF16)
        if got_at is not None:
            total = own_ref[got_at, :].astype(F32) + near_ref[got_at, :].astype(F32)
            out_ref[got_at, :] = (total + got_ref[...].astype(F32)).astype(BF16)


def fold(own, near, row, sends, after):
    depth = own.shape[1]
    operands, specs, shapes, cuts = [], [], [], []
    for p, at, got_at, got in sends:
        block = pl.BlockSpec((row, depth), lambda i, p=p: (p, 0))
        got = near if got is None else got
        size = got.shape[0] if got_at is not None else row
        operands += [own, near, got]
        specs += [block, block, pl.BlockSpec((size, depth), lambda i: (0, 0))]
        shapes.append(jax.ShapeDtypeStruct((at.size, depth), BF16))
        cuts.append((at, got_at))
    return pl.pallas_call(
        functools.partial(fold_kernel, cuts),
        grid=(1,),
        in_specs=specs + any_specs(after),
        out_specs=[pl.BlockSpec(shape.shape, lambda i: (0, 0)) for shape in shapes],
        out_shape=shapes,
        compiler_params=params(24),
        cost_estimate=cost(0, 16 * row * depth),
        name="fold",
    )(*operands, *after)


def last_kernel(own_ref, near_ref, r_ref, l_ref, out_ref):
    total = own_ref[...].astype(F32) + near_ref[...].astype(F32)
    out_ref[...] = (total + r_ref[...].astype(F32) + l_ref[...].astype(F32)).astype(BF16)


def last(own, near, r, l):
    block = pl.BlockSpec(r.shape, lambda i: (0, 0))
    return pl.pallas_call(
        last_kernel,
        grid=(1,),
        in_specs=[block] * 4,
        out_specs=block,
        out_shape=jax.ShapeDtypeStruct(r.shape, BF16),
        compiler_params=params(24),
        cost_estimate=cost(0, 12 * r.size),
        name="last",
    )(own, near, r, l)


def fisher_kernel(step, x_ref, gg_ref, gu_ref, *rest):
    fg_ref, fu_ref, done_ref = rest[-3:]
    done_ref[...] = jnp.zeros_like(done_ref)
    span = x_ref.shape[0] // SEQS
    seqs = [pl.ds(q * span, span) for q in range(SEQS)]
    cols = [x_ref[at, :].T for at in seqs]
    for g_ref, f_ref in ((gg_ref, fg_ref), (gu_ref, fu_ref)):
        for c in range(g_ref.shape[1] // step):
            at = pl.ds(c * step, step)
            total = None
            for q in range(SEQS):
                seq = jnp.dot(cols[q], g_ref[seqs[q], at], preferred_element_type=F32)
                total = seq * seq if total is None else total + seq * seq
            f_ref[:, at] = (total * (1.0 / SEQS)).astype(BF16)


def fisher(x, gg, gu, first, count, step, held, after):
    rows, depth = x.shape
    width = gg.shape[1]
    block = pl.BlockSpec((step, width), lambda j: (first + j, 0))
    return pl.pallas_call(
        functools.partial(fisher_kernel, tile(width, 256)),
        grid=(count,),
        in_specs=[pl.BlockSpec((rows, step), lambda j: (0, first + j))]
        + held_specs(2)
        + any_specs((*held, *after)),
        out_specs=[block, block, pl.BlockSpec((8, 128), lambda j: (0, 0))],
        out_shape=[jax.ShapeDtypeStruct((depth, width), BF16)] * 2
        + [jax.ShapeDtypeStruct((8, 128), F32)],
        input_output_aliases={3 + i: i for i in range(len(held))},
        compiler_params=params(40),
        cost_estimate=cost(4 * rows * step * count * width, 4 * step * count * width),
        name="fisher",
    )(x, gg, gu, *held, *after)


def ring_part(tokens, grad_out, wg, wu, wd):
    chips = len(CYCLE)
    far = chips // 2
    row, depth = tokens.shape
    width = wg.shape[1]
    links = [(CYCLE[i], CYCLE[(i + 1) % chips]) for i in range(chips)]
    to_right = [(2 * a + c, 2 * b + c) for a, b in links for c in range(2)]
    to_left = [(b, a) for a, b in to_right]
    across = [(2 * i + c, 2 * i + 1 - c) for i in range(chips) for c in range(2)]

    def right(value):
        return lax.ppermute(value, "hid", to_right)

    def left(value):
        return lax.ppermute(value, "hid", to_left)

    def swap(value):
        return lax.ppermute(value, "hid", across)

    cycle = jnp.array(CYCLE, jnp.int32)
    where = jnp.array([CYCLE.index(c) for c in range(chips)], jnp.int32)
    around = jnp.arange(chips, dtype=jnp.int32)
    chip = cycle[(where[lax.axis_index("hid") // 2] - around) % chips]
    span = chips // SEQS
    spot = (chip // span * 2 * span + chip % span) * row

    def both(r, l, after=(), ends=False):
        (r, l), _ = lax.optimization_barrier(((r, l), after))
        if ends:
            r, l = r[: row // 2], l[row // 2 :]
        return right(r), left(l)

    def blocks(own, rounds):
        return [own] + [r for r, _ in rounds] + [l for _, l in rounds[::-1]]

    lane = tile(width, 256)
    tiles = width // lane
    cuts = [0, 2, 5, 7] if tiles == 7 else [0, 0, 0, tiles]

    def piece(i, after):
        if cuts[i] == cuts[i + 1]:
            return []
        count = cuts[i + 1] - cuts[i]
        grant = (40, 38, 32)[i]
        return [gate_up(near_x, far_x, wg, wu, cuts[i], count, lane, grant, after)]

    def two(x, dy, after=()):
        (x, dy), _ = lax.optimization_barrier(((x, dy), after))
        return (right(x[0]), left(x[1])), (right(dy[0]), left(dy[1]))

    own_x, own_dy = bring(tokens, grad_out)
    in_x, in_dy = [both(tokens, tokens)], []
    got = two(in_x[0], (own_dy, own_dy), own_x)
    for k in range(2, far):
        in_x.append(got[0])
        in_dy.append(got[1])
        if k < far - 1:
            got = two(in_x[-1], in_dy[-1])
    in_x.append(both(*in_x[-1], in_dy[-1], True))
    near_x = pack(blocks(own_x, in_x), (spot,))
    far_x = swap(near_x)

    in_dy.append(both(*in_dy[-1], in_x[-2]))
    factors = piece(0, in_dy[-2])
    in_dy.append(both(*in_dy[-1], factors, True))
    factors += piece(1, in_dy[-2])
    x = arrange(spot, near_x, far_x, in_dy[-2])
    near_dy = pack_turned(blocks(own_dy, in_dy), (x, *factors[-1]))
    far_dy = swap(near_dy)
    factors += piece(2, (near_dy,))
    gg, gu, own, sent = back(spot, near_dy, far_dy, wg, wu, wd, factors)

    near = swap(sent)
    full, head, tail = pl.ds(0, row), pl.ds(0, row // 2), pl.ds(row // 2, row // 2)
    step = 256
    counts = [4, 2, 4, 4, 2]
    held, first = (), 0
    r = l = None
    ready = ()
    for k in range(far, 0, -1):
        *held, done = fisher(x, gg, gu, first, counts[far - k], step, held, ready)
        first += counts[far - k]
        if k == far:
            sends = [(far, head, None, None), (far, tail, None, None)]
        elif k == far - 1:
            sends = [(chips - k, full, head, r), (k, full, tail, l)]
        else:
            sends = [(chips - k, full, full, r), (k, full, full, l)]
        ready = fold(own, near, row, sends, (done,))
        r, l = right(ready[0]), left(ready[1])
    fg, fu, _ = fisher(x, gg, gu, first, counts[far], step, held, ready)
    mine = last(own, near, r, l)
    return fg, fu, mine


def plain_forward_kernel(x_ref, wg_ref, wu_ref, gate_ref, up_ref):
    x = x_ref[...]
    gate_ref[...] = jnp.dot(x, wg_ref[...], preferred_element_type=jnp.float32)
    up_ref[...] = jnp.dot(x, wu_ref[...], preferred_element_type=jnp.float32)


def plain_forward(x, wg, wu):
    rows, depth = x.shape
    width = wg.shape[1]
    step = tile(width, 256)
    return pl.pallas_call(
        plain_forward_kernel,
        grid=(width // step,),
        in_specs=[
            pl.BlockSpec((rows, depth), lambda j: (0, 0)),
            pl.BlockSpec((depth, step), lambda j: (0, j)),
            pl.BlockSpec((depth, step), lambda j: (0, j)),
        ],
        out_specs=[pl.BlockSpec((rows, step), lambda j: (0, j))] * 2,
        out_shape=[jax.ShapeDtypeStruct((rows, width), jnp.float32)] * 2,
        compiler_params=params(40),
        cost_estimate=cost(4 * rows * depth * width, 4 * depth * width),
        name="gate_up",
    )(x, wg, wu)


def plain_back_kernel(parts, dy_ref, wd_ref, gate_ref, up_ref, gg_ref, gu_ref):
    rows = dy_ref.shape[0] // parts
    for p in range(parts):
        at = pl.ds(p * rows, rows)
        hidden = lax.dot_general(dy_ref[at, :], wd_ref[...], NT, preferred_element_type=jnp.float32)
        gate = gate_ref[at, :]
        sigma = jax.nn.sigmoid(gate)
        both = hidden * sigma
        gg_ref[at, :] = (both * up_ref[at, :] * (1.0 + gate * (1.0 - sigma))).astype(jnp.bfloat16)
        gu_ref[at, :] = (both * gate).astype(jnp.bfloat16)


def plain_back(dy, wd, gate, up):
    rows, depth = dy.shape
    width = wd.shape[0]
    step = tile(width, 256)
    column = pl.BlockSpec((rows, step), lambda j: (0, j))
    return pl.pallas_call(
        functools.partial(plain_back_kernel, 2),
        grid=(width // step,),
        in_specs=[
            pl.BlockSpec((rows, depth), lambda j: (0, 0)),
            pl.BlockSpec((step, depth), lambda j: (j, 0)),
            column,
            column,
        ],
        out_specs=[column, column],
        out_shape=[jax.ShapeDtypeStruct((rows, width), jnp.bfloat16)] * 2,
        compiler_params=params(40),
        cost_estimate=cost(2 * rows * depth * width, 2 * depth * width),
        name="hidden_back",
    )(dy, wd, gate, up)


def plain_input_kernel(gg_ref, gu_ref, wg_ref, wu_ref, out_ref):
    total = lax.dot_general(gg_ref[...], wg_ref[...], NT, preferred_element_type=jnp.float32)
    total += lax.dot_general(gu_ref[...], wu_ref[...], NT, preferred_element_type=jnp.float32)
    out_ref[...] = total.astype(jnp.bfloat16)


def plain_input_terms(gg, gu, wg, wu):
    rows, width = gg.shape
    depth = wg.shape[0]
    step = 512
    held = pl.BlockSpec((rows, width), lambda j: (0, 0))
    return pl.pallas_call(
        plain_input_kernel,
        grid=(depth // step,),
        in_specs=[
            held,
            held,
            pl.BlockSpec((step, width), lambda j: (j, 0)),
            pl.BlockSpec((step, width), lambda j: (j, 0)),
        ],
        out_specs=pl.BlockSpec((rows, step), lambda j: (0, j)),
        out_shape=jax.ShapeDtypeStruct((rows, depth), jnp.bfloat16),
        compiler_params=params(40),
        cost_estimate=cost(4 * rows * depth * width, 4 * depth * width),
        name="input_terms",
    )(gg, gu, wg, wu)


def plain_fisher_kernel(step, x_ref, gg_ref, gu_ref, fg_ref, fu_ref):
    half = x_ref.shape[0] // 2
    span = half // SEQS
    width = gg_ref.shape[1]

    def rows(ref, q, at):
        near = ref[pl.ds(q * span, span), at]
        far = ref[pl.ds(half + q * span, span), at]
        return jnp.concatenate([near, far], axis=0)

    xs = [rows(x_ref, q, slice(None)).T for q in range(SEQS)]
    for g_ref, f_ref in ((gg_ref, fg_ref), (gu_ref, fu_ref)):
        for c in range(width // step):
            at = pl.ds(c * step, step)
            total = None
            for q in range(SEQS):
                seq = jnp.dot(xs[q], rows(g_ref, q, at), preferred_element_type=jnp.float32)
                total = seq * seq if total is None else total + seq * seq
            f_ref[:, at] = (total * (1.0 / SEQS)).astype(jnp.bfloat16)


def plain_fisher(x, gg, gu):
    rows, depth = x.shape
    width = gg.shape[1]
    step = 512
    held = pl.BlockSpec((rows, width), lambda j: (0, 0))
    block = pl.BlockSpec((step, width), lambda j: (j, 0))
    return pl.pallas_call(
        functools.partial(plain_fisher_kernel, tile(width, 256)),
        grid=(depth // step,),
        in_specs=[pl.BlockSpec((rows, step), lambda j: (0, j)), held, held],
        out_specs=[block, block],
        out_shape=[jax.ShapeDtypeStruct((depth, width), jnp.bfloat16)] * 2,
        compiler_params=params(40),
        cost_estimate=cost(4 * rows * depth * width, 4 * depth * width),
        name="fisher",
    )(x, gg, gu)


def plain_part(size, tokens, grad_out, wg, wu, wd):
    chips = size // 2
    across = [[2 * i + c for i in range(chips)] for c in range(2)]
    pairs = [[2 * i, 2 * i + 1] for i in range(chips)]
    block, depth = tokens.shape

    def gather(rows):
        near = lax.all_gather(rows, "hid", axis=0, tiled=True, axis_index_groups=across)
        return lax.all_gather(near, "hid", axis=0, tiled=False, axis_index_groups=pairs)

    x = gather(tokens).reshape(-1, depth)
    dy = gather(grad_out).reshape(-1, depth)
    gate, up = plain_forward(x, wg, wu)
    gg, gu = plain_back(dy, wd, gate, up)
    terms = plain_input_terms(gg, gu, wg, wu).reshape(2, -1, depth)
    mine = lax.psum_scatter(
        terms, "hid", scatter_dimension=0, tiled=False, axis_index_groups=pairs
    )
    mine = lax.psum_scatter(
        mine, "hid", scatter_dimension=0, tiled=True, axis_index_groups=across
    )
    fg, fu = plain_fisher(x, gg, gu)
    return fg, fu, mine


def per_device(size, tokens, grad_out, wg, wu, wd):
    if size == 2 * len(CYCLE) and tokens.shape[0] % 32 == 0:
        return ring_part(tokens, grad_out, wg, wu, wd)
    return plain_part(size, tokens, grad_out, wg, wu, wd)


def solution(mesh):
    rows = P(("adjust", "hid"), None)
    weights = P("adjust", "hid")
    return jax.shard_map(
        functools.partial(per_device, mesh.shape["hid"]),
        mesh=mesh,
        in_specs=(rows, rows, weights, weights, rows),
        out_specs=(weights, weights, rows),
        check_vma=False,
    )
```

```python
import functools

import jax
import jax.numpy as jnp
from jax import lax
from jax.experimental import pallas as pl
from jax.experimental.pallas import tpu as pltpu
from jax.sharding import PartitionSpec as P

SEQS = 2
MIB = 1 << 20
CYCLE = (0, 2, 4, 6, 7, 5, 3, 1)
NT = (((1,), (1,)), ((), ()))
BF16 = jnp.bfloat16
F32 = jnp.float32


def tile(size, want):
    return want if size % want == 0 else size


def params(mib):
    return pltpu.CompilerParams(vmem_limit_bytes=mib * MIB)


def cost(flops, read):
    return pl.CostEstimate(flops=flops, bytes_accessed=read, transcendentals=0)


def any_specs(values):
    return [pl.BlockSpec(memory_space=pl.ANY)] * len(values)


def hbm_specs(count):
    return [pl.BlockSpec(memory_space=pltpu.HBM)] * count


def held_specs(count):
    return [pl.BlockSpec(memory_space=pltpu.VMEM)] * count


def head_copies(wg_ref, wu_ref, first, step, head_ref, sems):
    cols = pl.ds(first * step, step)
    return [
        pltpu.make_async_copy(ref.at[:, cols], head_ref.at[i], sems.at[i])
        for i, ref in enumerate((wg_ref, wu_ref))
    ]


def bring_kernel(step, x_ref, dy_ref, wg_ref, wu_ref, x_out, dy_out, head_ref, sems):
    copies = head_copies(wg_ref, wu_ref, 0, step, head_ref, sems)
    for copy in copies:
        copy.start()
    x_out[...] = x_ref[...]
    dy_out[...] = dy_ref[...]
    for copy in copies:
        copy.wait()


def bring(x, dy, wg, wu, step):
    return pl.pallas_call(
        functools.partial(bring_kernel, step),
        in_specs=held_specs(2) + hbm_specs(2),
        out_specs=held_specs(3),
        out_shape=[jax.ShapeDtypeStruct(x.shape, BF16)] * 2
        + [jax.ShapeDtypeStruct((2, wg.shape[0], step), BF16)],
        scratch_shapes=[pltpu.SemaphoreType.DMA((2,))],
        compiler_params=params(46),
        cost_estimate=cost(0, 4 * wg.shape[0] * step),
        name="bring",
    )(x, dy, wg, wu)


def pack_kernel(count, *refs):
    out_ref = refs[-1]
    start = 0
    for piece in refs[:count]:
        out_ref[pl.ds(start, piece.shape[0]), :] = piece[...]
        start += piece.shape[0]


def pack(pieces, after):
    depth = pieces[0].shape[1]
    rows = sum(piece.shape[0] for piece in pieces)
    whole = pl.BlockSpec(memory_space=pltpu.VMEM)
    return pl.pallas_call(
        functools.partial(pack_kernel, len(pieces)),
        in_specs=[whole] * len(pieces) + any_specs(after),
        out_specs=whole,
        out_shape=jax.ShapeDtypeStruct((rows, depth), BF16),
        compiler_params=params(8),
        cost_estimate=cost(0, 4 * rows * depth),
        name="pack",
    )(*pieces, *after)


def pack_turned_kernel(count, *refs):
    pieces, out_ref = refs[:count], refs[-1]
    step = 512
    for c in range(0, out_ref.shape[0], step):
        block = jnp.concatenate([piece[:, c : c + step] for piece in pieces], axis=0)
        out_ref[c : c + step, :] = block.T


def pack_turned(pieces, after):
    depth = pieces[0].shape[1]
    rows = sum(piece.shape[0] for piece in pieces)
    return pl.pallas_call(
        functools.partial(pack_turned_kernel, len(pieces)),
        in_specs=held_specs(len(pieces)) + any_specs(after),
        out_specs=pl.BlockSpec(memory_space=pltpu.VMEM),
        out_shape=jax.ShapeDtypeStruct((depth, rows), BF16),
        compiler_params=params(8),
        cost_estimate=cost(0, 4 * rows * depth),
        name="pack_turned",
    )(*pieces, *after)


def put_rows(spot_ref, side, value, out_ref, cols):
    chips = spot_ref.shape[0]
    row = value.shape[0] // chips
    for p in range(chips):
        start = pl.multiple_of(spot_ref[p] + side * chips // SEQS * row, row)
        out_ref[pl.ds(start, row), cols] = value[p * row : (p + 1) * row, :]


def arrange_kernel(spot_ref, near_ref, far_ref, *rest):
    for side, ref in enumerate((near_ref, far_ref)):
        put_rows(spot_ref, side, ref[...], rest[-1], slice(None))


def arrange(spot, near, far, after):
    rows, depth = near.shape
    return pl.pallas_call(
        arrange_kernel,
        in_specs=[pl.BlockSpec(memory_space=pltpu.SMEM)] + held_specs(2) + any_specs(after),
        out_specs=pl.BlockSpec(memory_space=pltpu.VMEM),
        out_shape=jax.ShapeDtypeStruct((2 * rows, depth), BF16),
        compiler_params=params(6),
        cost_estimate=cost(0, 8 * rows * depth),
        name="arrange",
    )(spot, near, far, *after)


def gate_up_kernel(first, step, near_ref, far_ref, head_ref, wg_ref, wu_ref, wd_ref, *rest):
    a_ref, b_ref, next_ref, w_buf, out_buf, sems, out_sems, next_sems = rest[-8:]
    rows = near_ref.shape[0]
    tiles = a_ref.shape[0] // step

    def fetch(t):
        slot = t % 2
        return head_copies(wg_ref, wu_ref, first + t, step, w_buf.at[slot], sems.at[slot])

    def fetch_next():
        if next_ref.shape[0] == 2:
            return head_copies(wg_ref, wu_ref, first + tiles, step, next_ref, next_sems)
        return [pltpu.make_async_copy(wd_ref.at[pl.ds(0, step), :], next_ref, next_sems.at[0])]

    def store(t):
        to = pl.ds(t * step, step)
        return [
            pltpu.make_async_copy(out_buf.at[t, i], ref.at[to, :], out_sems.at[t, i])
            for i, ref in enumerate((a_ref, b_ref))
        ]

    def begin(copies):
        for copy in copies:
            copy.start()

    def finish(copies):
        for copy in copies:
            copy.wait()

    for t in range(1, min(3, tiles)):
        begin(fetch(t))
    for t in range(tiles):
        if t:
            finish(fetch(t))
        if t == tiles - 1:
            begin(fetch_next())
        w_ref = w_buf.at[t % 2] if t else head_ref
        for side, x_ref in enumerate((near_ref, far_ref)):
            gate = jnp.dot(x_ref[...], w_ref[0], preferred_element_type=F32)
            up = jnp.dot(x_ref[...], w_ref[1], preferred_element_type=F32)
            at = pl.ds(side * rows, rows)
            sigma = jax.nn.sigmoid(gate)
            out_buf[t, 0, :, at] = (up * sigma * (1.0 + gate * (1.0 - sigma))).T
            out_buf[t, 1, :, at] = (gate * sigma).T
        if t and t + 2 < tiles:
            begin(fetch(t + 2))
        begin(store(t))
    for t in range(tiles):
        finish(store(t))
    finish(fetch_next())


def gate_up(near, far, head, wg, wu, wd, first, count, step, grant, after):
    rows, depth = near.shape
    last = (first + count) * step == wg.shape[1]
    return pl.pallas_call(
        functools.partial(gate_up_kernel, first, step),
        in_specs=held_specs(3) + hbm_specs(3) + any_specs(after),
        out_specs=hbm_specs(2) + held_specs(1),
        out_shape=[jax.ShapeDtypeStruct((count * step, 2 * rows), F32)] * 2
        + [jax.ShapeDtypeStruct((step, depth) if last else (2, depth, step), BF16)],
        scratch_shapes=[
            pltpu.VMEM((2, 2, depth, step), BF16),
            pltpu.VMEM((count, 2, step, 2 * rows), F32),
            pltpu.SemaphoreType.DMA((2, 2)),
            pltpu.SemaphoreType.DMA((count, 2)),
            pltpu.SemaphoreType.DMA((2,)),
        ],
        compiler_params=params(grant),
        cost_estimate=cost(8 * rows * depth * count * step, 4 * depth * count * step),
        name="gate_up",
    )(near, far, head, wg, wu, wd, *after)


def back_kernel(
    step, deep, pieces, spot_ref, near_ref, far_ref, head_ref, wg_ref, wu_ref, wd_ref, *refs
):
    a_refs, b_refs = refs[:pieces], refs[pieces : 2 * pieces]
    ggs_ref, gus_ref, own_ref, sent_ref, g_ref = refs[2 * pieces : 2 * pieces + 5]
    wd_buf, w_buf, factor_buf, sems, w_sems, factor_sems = refs[2 * pieces + 5 :]
    width = wg_ref.shape[1]
    rows = near_ref.shape[1]
    tiles = wd_ref.shape[0] // step

    def fetch(t):
        at = pl.ds(pl.multiple_of(t * step, step), step)
        slot = lax.rem(t, 2)
        return pltpu.make_async_copy(wd_ref.at[at, :], wd_buf.at[slot], sems.at[slot])

    def fetch_rows(i):
        at = pl.ds(pl.multiple_of(i * deep, deep), deep)
        slot = lax.rem(i, 2)
        return [
            pltpu.make_async_copy(
                w_ref.at[at, :], w_buf.at[slot, :, pl.ds(k * width, width)], w_sems.at[slot, k]
            )
            for k, w_ref in enumerate((wg_ref, wu_ref))
        ]

    starts = [0]
    for a_ref in a_refs:
        starts.append(starts[-1] + a_ref.shape[0])

    def fetch_factors(p):
        at = pl.ds(starts[p], starts[p + 1] - starts[p])
        return [
            pltpu.make_async_copy(ref, factor_buf.at[k, at, :], factor_sems.at[k, p])
            for k, ref in enumerate((a_refs[p], b_refs[p]))
        ]

    def hidden_tile(t, wd):
        cols = pl.ds(pl.multiple_of(t * step, step), step)
        for side, dy_ref in enumerate((near_ref, far_ref)):
            hidden = jnp.dot(wd, dy_ref[...], preferred_element_type=F32)
            at = pl.ds(side * rows, rows)
            for f, gs_ref in enumerate((ggs_ref, gus_ref)):
                grad = (hidden * factor_buf[f, cols, at]).astype(BF16)
                to = pl.multiple_of(t * step + f * width, step)
                g_ref[pl.ds(to, step), at] = grad
                put_rows(spot_ref, side, grad.T, gs_ref, cols)

    blocks = wg_ref.shape[0] // deep
    for copy in fetch_factors(0):
        copy.start()
    for t in range(1, min(3, tiles)):
        fetch(jnp.int32(t)).start()
    for p in range(pieces):
        if p + 1 < pieces:
            for copy in fetch_factors(p + 1):
                copy.start()
        else:
            for i in range(2):
                for copy in fetch_rows(jnp.int32(i)):
                    copy.start()
        for copy in fetch_factors(p):
            copy.wait()

        if p == 0:
            hidden_tile(0, head_ref[...])

        @pl.loop(max(starts[p] // step, 1), starts[p + 1] // step)
        def _(t):
            fetch(t).wait()
            hidden_tile(t, wd_buf[lax.rem(t, 2)])

            @pl.when(t + 2 < tiles)
            def _():
                fetch(t + 2).start()

    @pl.loop(0, blocks)
    def _(i):
        at = pl.ds(pl.multiple_of(i * deep, deep), deep)
        slot = lax.rem(i, 2)
        for copy in fetch_rows(i):
            copy.wait()
        for side, out_ref in enumerate((own_ref, sent_ref)):
            of = pl.ds(side * rows, rows)
            total = jnp.dot(w_buf[slot], g_ref[:, of], preferred_element_type=F32)
            out_ref[:, at] = total.astype(BF16).T

        @pl.when(i + 2 < blocks)
        def _():
            for copy in fetch_rows(i + 2):
                copy.start()


def back(spot, near, far, head, wg, wu, wd, factors):
    depth, rows = near.shape
    width = wd.shape[0]
    step = tile(width, 256)
    a = [pair[0] for pair in factors]
    b = [pair[1] for pair in factors]
    return pl.pallas_call(
        functools.partial(back_kernel, step, 512, len(a)),
        in_specs=[pl.BlockSpec(memory_space=pltpu.SMEM)]
        + held_specs(3)
        + hbm_specs(3)
        + any_specs(a + b),
        out_specs=held_specs(4),
        out_shape=[jax.ShapeDtypeStruct((2 * rows, width), BF16)] * 2
        + [jax.ShapeDtypeStruct((rows, depth), BF16)] * 2,
        scratch_shapes=[
            pltpu.VMEM((2 * width, 2 * rows), BF16),
            pltpu.VMEM((2, step, depth), BF16),
            pltpu.VMEM((2, 512, 2 * width), BF16),
            pltpu.VMEM((2, width, 2 * rows), F32),
            pltpu.SemaphoreType.DMA((2,)),
            pltpu.SemaphoreType.DMA((2, 2)),
            pltpu.SemaphoreType.DMA((2, len(a))),
        ],
        compiler_params=params(28),
        cost_estimate=cost(12 * rows * depth * width, 6 * depth * width),
        name="hidden_back",
    )(spot, near, far, head, wg, wu, wd, *a, *b)


def fold_kernel(cuts, *refs):
    count = len(cuts)
    outs = refs[-count:]
    for i, (at, got_at) in enumerate(cuts):
        own_ref, near_ref, got_ref = refs[3 * i : 3 * i + 3]
        out_ref = outs[i]
        out_ref[...] = (own_ref[at, :].astype(F32) + near_ref[at, :].astype(F32)).astype(BF16)
        if got_at is not None:
            total = own_ref[got_at, :].astype(F32) + near_ref[got_at, :].astype(F32)
            out_ref[got_at, :] = (total + got_ref[...].astype(F32)).astype(BF16)


def fold(own, near, row, sends, after):
    depth = own.shape[1]
    operands, specs, shapes, cuts = [], [], [], []
    for p, at, got_at, got in sends:
        block = pl.BlockSpec((row, depth), lambda i, p=p: (p, 0))
        got = near if got is None else got
        size = got.shape[0] if got_at is not None else row
        operands += [own, near, got]
        specs += [block, block, pl.BlockSpec((size, depth), lambda i: (0, 0))]
        shapes.append(jax.ShapeDtypeStruct((at.size, depth), BF16))
        cuts.append((at, got_at))
    return pl.pallas_call(
        functools.partial(fold_kernel, cuts),
        grid=(1,),
        in_specs=specs + any_specs(after),
        out_specs=[pl.BlockSpec(shape.shape, lambda i: (0, 0)) for shape in shapes],
        out_shape=shapes,
        compiler_params=params(24),
        cost_estimate=cost(0, 16 * row * depth),
        name="fold",
    )(*operands, *after)


def last_kernel(own_ref, near_ref, r_ref, l_ref, out_ref):
    total = own_ref[...].astype(F32) + near_ref[...].astype(F32)
    out_ref[...] = (total + r_ref[...].astype(F32) + l_ref[...].astype(F32)).astype(BF16)


def last(own, near, r, l):
    block = pl.BlockSpec(r.shape, lambda i: (0, 0))
    return pl.pallas_call(
        last_kernel,
        grid=(1,),
        in_specs=[block] * 4,
        out_specs=block,
        out_shape=jax.ShapeDtypeStruct(r.shape, BF16),
        compiler_params=params(24),
        cost_estimate=cost(0, 12 * r.size),
        name="last",
    )(own, near, r, l)


def fisher_kernel(step, x_ref, gg_ref, gu_ref, *rest):
    fg_ref, fu_ref, done_ref = rest[-3:]
    done_ref[...] = jnp.zeros_like(done_ref)
    span = x_ref.shape[0] // SEQS
    seqs = [pl.ds(q * span, span) for q in range(SEQS)]
    cols = [x_ref[at, :].T for at in seqs]
    for g_ref, f_ref in ((gg_ref, fg_ref), (gu_ref, fu_ref)):
        for c in range(g_ref.shape[1] // step):
            at = pl.ds(c * step, step)
            total = None
            for q in range(SEQS):
                seq = jnp.dot(cols[q], g_ref[seqs[q], at], preferred_element_type=F32)
                total = seq * seq if total is None else total + seq * seq
            f_ref[:, at] = (total * (1.0 / SEQS)).astype(BF16)


def fisher(x, gg, gu, first, count, step, held, after):
    rows, depth = x.shape
    width = gg.shape[1]
    block = pl.BlockSpec((step, width), lambda j: (first + j, 0))
    return pl.pallas_call(
        functools.partial(fisher_kernel, tile(width, 256)),
        grid=(count,),
        in_specs=[pl.BlockSpec((rows, step), lambda j: (0, first + j))]
        + held_specs(2)
        + any_specs((*held, *after)),
        out_specs=[block, block, pl.BlockSpec((8, 128), lambda j: (0, 0))],
        out_shape=[jax.ShapeDtypeStruct((depth, width), BF16)] * 2
        + [jax.ShapeDtypeStruct((8, 128), F32)],
        input_output_aliases={3 + i: i for i in range(len(held))},
        compiler_params=params(40),
        cost_estimate=cost(4 * rows * step * count * width, 4 * step * count * width),
        name="fisher",
    )(x, gg, gu, *held, *after)


def ring_part(tokens, grad_out, wg, wu, wd):
    chips = len(CYCLE)
    far = chips // 2
    row, depth = tokens.shape
    width = wg.shape[1]
    links = [(CYCLE[i], CYCLE[(i + 1) % chips]) for i in range(chips)]
    to_right = [(2 * a + c, 2 * b + c) for a, b in links for c in range(2)]
    to_left = [(b, a) for a, b in to_right]
    across = [(2 * i + c, 2 * i + 1 - c) for i in range(chips) for c in range(2)]

    def right(value):
        return lax.ppermute(value, "hid", to_right)

    def left(value):
        return lax.ppermute(value, "hid", to_left)

    def swap(value):
        return lax.ppermute(value, "hid", across)

    cycle = jnp.array(CYCLE, jnp.int32)
    where = jnp.array([CYCLE.index(c) for c in range(chips)], jnp.int32)
    around = jnp.arange(chips, dtype=jnp.int32)
    chip = cycle[(where[lax.axis_index("hid") // 2] - around) % chips]
    span = chips // SEQS
    spot = (chip // span * 2 * span + chip % span) * row

    def both(r, l, after=(), ends=False):
        (r, l), _ = lax.optimization_barrier(((r, l), after))
        if ends:
            r, l = r[: row // 2], l[row // 2 :]
        return right(r), left(l)

    def blocks(own, rounds):
        return [own] + [r for r, _ in rounds] + [l for _, l in rounds[::-1]]

    lane = tile(width, 256)
    tiles = width // lane
    cuts = [0, 2, 5, 7]

    def piece(i, head, after):
        grant = (30, 28, 28)[i]
        count = cuts[i + 1] - cuts[i]
        a, b, head = gate_up(
            near_x, far_x, head, wg, wu, wd, cuts[i], count, lane, grant, after
        )
        return (a, b), head

    own_x, own_dy, head = bring(tokens, grad_out, wg, wu, lane)
    in_x = [both(tokens, tokens)]
    in_x.append(both(*in_x[-1], (own_x, head)))
    in_dy = [both(own_dy, own_dy, in_x[0])]
    for _ in range(3, far):
        in_x.append(both(*in_x[-1]))
        in_dy.append(both(*in_dy[-1]))
    in_x.append(both(*in_x[-1], in_dy[-1], True))
    near_x = pack(blocks(own_x, in_x), (spot,))
    far_x = swap(near_x)

    in_dy.append(both(*in_dy[-1], in_x[-2]))
    some, head = piece(0, head, in_dy[-2])
    factors = [some]
    in_dy.append(both(*in_dy[-1], some, True))
    some, head = piece(1, head, in_dy[-2])
    factors.append(some)
    x = arrange(spot, near_x, far_x, in_dy[-2])
    near_dy = pack_turned(blocks(own_dy, in_dy), (x, *some))
    far_dy = swap(near_dy)
    some, head = piece(2, head, (near_dy,))
    factors.append(some)
    gg, gu, own, sent = back(spot, near_dy, far_dy, head, wg, wu, wd, factors)

    near = swap(sent)
    full, head, tail = pl.ds(0, row), pl.ds(0, row // 2), pl.ds(row // 2, row // 2)
    step = 256
    counts = [4, 2, 4, 4, 2]
    held, first = (), 0
    r = l = None
    ready = ()
    for k in range(far, 0, -1):
        *held, done = fisher(x, gg, gu, first, counts[far - k], step, held, ready)
        first += counts[far - k]
        if k == far:
            sends = [(far, head, None, None), (far, tail, None, None)]
        elif k == far - 1:
            sends = [(chips - k, full, head, r), (k, full, tail, l)]
        else:
            sends = [(chips - k, full, full, r), (k, full, full, l)]
        ready = fold(own, near, row, sends, (done,))
        r, l = right(ready[0]), left(ready[1])
    fg, fu, _ = fisher(x, gg, gu, first, counts[far], step, held, ready)
    mine = last(own, near, r, l)
    return fg, fu, mine


def plain_forward_kernel(x_ref, wg_ref, wu_ref, gate_ref, up_ref):
    x = x_ref[...]
    gate_ref[...] = jnp.dot(x, wg_ref[...], preferred_element_type=jnp.float32)
    up_ref[...] = jnp.dot(x, wu_ref[...], preferred_element_type=jnp.float32)


def plain_forward(x, wg, wu):
    rows, depth = x.shape
    width = wg.shape[1]
    step = tile(width, 256)
    return pl.pallas_call(
        plain_forward_kernel,
        grid=(width // step,),
        in_specs=[
            pl.BlockSpec((rows, depth), lambda j: (0, 0)),
            pl.BlockSpec((depth, step), lambda j: (0, j)),
            pl.BlockSpec((depth, step), lambda j: (0, j)),
        ],
        out_specs=[pl.BlockSpec((rows, step), lambda j: (0, j))] * 2,
        out_shape=[jax.ShapeDtypeStruct((rows, width), jnp.float32)] * 2,
        compiler_params=params(40),
        cost_estimate=cost(4 * rows * depth * width, 4 * depth * width),
        name="gate_up",
    )(x, wg, wu)


def plain_back_kernel(parts, dy_ref, wd_ref, gate_ref, up_ref, gg_ref, gu_ref):
    rows = dy_ref.shape[0] // parts
    for p in range(parts):
        at = pl.ds(p * rows, rows)
        hidden = lax.dot_general(dy_ref[at, :], wd_ref[...], NT, preferred_element_type=jnp.float32)
        gate = gate_ref[at, :]
        sigma = jax.nn.sigmoid(gate)
        both = hidden * sigma
        gg_ref[at, :] = (both * up_ref[at, :] * (1.0 + gate * (1.0 - sigma))).astype(jnp.bfloat16)
        gu_ref[at, :] = (both * gate).astype(jnp.bfloat16)


def plain_back(dy, wd, gate, up):
    rows, depth = dy.shape
    width = wd.shape[0]
    step = tile(width, 256)
    column = pl.BlockSpec((rows, step), lambda j: (0, j))
    return pl.pallas_call(
        functools.partial(plain_back_kernel, 2),
        grid=(width // step,),
        in_specs=[
            pl.BlockSpec((rows, depth), lambda j: (0, 0)),
            pl.BlockSpec((step, depth), lambda j: (j, 0)),
            column,
            column,
        ],
        out_specs=[column, column],
        out_shape=[jax.ShapeDtypeStruct((rows, width), jnp.bfloat16)] * 2,
        compiler_params=params(40),
        cost_estimate=cost(2 * rows * depth * width, 2 * depth * width),
        name="hidden_back",
    )(dy, wd, gate, up)


def plain_input_kernel(gg_ref, gu_ref, wg_ref, wu_ref, out_ref):
    total = lax.dot_general(gg_ref[...], wg_ref[...], NT, preferred_element_type=jnp.float32)
    total += lax.dot_general(gu_ref[...], wu_ref[...], NT, preferred_element_type=jnp.float32)
    out_ref[...] = total.astype(jnp.bfloat16)


def plain_input_terms(gg, gu, wg, wu):
    rows, width = gg.shape
    depth = wg.shape[0]
    step = 512
    held = pl.BlockSpec((rows, width), lambda j: (0, 0))
    return pl.pallas_call(
        plain_input_kernel,
        grid=(depth // step,),
        in_specs=[
            held,
            held,
            pl.BlockSpec((step, width), lambda j: (j, 0)),
            pl.BlockSpec((step, width), lambda j: (j, 0)),
        ],
        out_specs=pl.BlockSpec((rows, step), lambda j: (0, j)),
        out_shape=jax.ShapeDtypeStruct((rows, depth), jnp.bfloat16),
        compiler_params=params(40),
        cost_estimate=cost(4 * rows * depth * width, 4 * depth * width),
        name="input_terms",
    )(gg, gu, wg, wu)


def plain_fisher_kernel(step, x_ref, gg_ref, gu_ref, fg_ref, fu_ref):
    half = x_ref.shape[0] // 2
    span = half // SEQS
    width = gg_ref.shape[1]

    def rows(ref, q, at):
        near = ref[pl.ds(q * span, span), at]
        far = ref[pl.ds(half + q * span, span), at]
        return jnp.concatenate([near, far], axis=0)

    xs = [rows(x_ref, q, slice(None)).T for q in range(SEQS)]
    for g_ref, f_ref in ((gg_ref, fg_ref), (gu_ref, fu_ref)):
        for c in range(width // step):
            at = pl.ds(c * step, step)
            total = None
            for q in range(SEQS):
                seq = jnp.dot(xs[q], rows(g_ref, q, at), preferred_element_type=jnp.float32)
                total = seq * seq if total is None else total + seq * seq
            f_ref[:, at] = (total * (1.0 / SEQS)).astype(jnp.bfloat16)


def plain_fisher(x, gg, gu):
    rows, depth = x.shape
    width = gg.shape[1]
    step = 512
    held = pl.BlockSpec((rows, width), lambda j: (0, 0))
    block = pl.BlockSpec((step, width), lambda j: (j, 0))
    return pl.pallas_call(
        functools.partial(plain_fisher_kernel, tile(width, 256)),
        grid=(depth // step,),
        in_specs=[pl.BlockSpec((rows, step), lambda j: (0, j)), held, held],
        out_specs=[block, block],
        out_shape=[jax.ShapeDtypeStruct((depth, width), jnp.bfloat16)] * 2,
        compiler_params=params(40),
        cost_estimate=cost(4 * rows * depth * width, 4 * depth * width),
        name="fisher",
    )(x, gg, gu)


def plain_part(size, tokens, grad_out, wg, wu, wd):
    chips = size // 2
    across = [[2 * i + c for i in range(chips)] for c in range(2)]
    pairs = [[2 * i, 2 * i + 1] for i in range(chips)]
    block, depth = tokens.shape

    def gather(rows):
        near = lax.all_gather(rows, "hid", axis=0, tiled=True, axis_index_groups=across)
        return lax.all_gather(near, "hid", axis=0, tiled=False, axis_index_groups=pairs)

    x = gather(tokens).reshape(-1, depth)
    dy = gather(grad_out).reshape(-1, depth)
    gate, up = plain_forward(x, wg, wu)
    gg, gu = plain_back(dy, wd, gate, up)
    terms = plain_input_terms(gg, gu, wg, wu).reshape(2, -1, depth)
    mine = lax.psum_scatter(
        terms, "hid", scatter_dimension=0, tiled=False, axis_index_groups=pairs
    )
    mine = lax.psum_scatter(
        mine, "hid", scatter_dimension=0, tiled=True, axis_index_groups=across
    )
    fg, fu = plain_fisher(x, gg, gu)
    return fg, fu, mine


def per_device(size, tokens, grad_out, wg, wu, wd):
    fits = tokens.shape[0] == 32 and wg.shape == (4096, 1792)
    if size == 2 * len(CYCLE) and fits:
        return ring_part(tokens, grad_out, wg, wu, wd)
    return plain_part(size, tokens, grad_out, wg, wu, wd)


def solution(mesh):
    rows = P(("adjust", "hid"), None)
    weights = P("adjust", "hid")
    return jax.shard_map(
        functools.partial(per_device, mesh.shape["hid"]),
        mesh=mesh,
        in_specs=(rows, rows, weights, weights, rows),
        out_specs=(weights, weights, rows),
        check_vma=False,
    )
```

```python
import functools

import jax
import jax.numpy as jnp
from jax import lax
from jax.experimental import pallas as pl
from jax.experimental.pallas import tpu as pltpu
from jax.sharding import PartitionSpec as P

SEQS = 2
MIB = 1 << 20
CYCLE = (0, 2, 4, 6, 7, 5, 3, 1)
NT = (((1,), (1,)), ((), ()))
BF16 = jnp.bfloat16
F32 = jnp.float32


def tile(size, want):
    return want if size % want == 0 else size


def params(mib):
    return pltpu.CompilerParams(vmem_limit_bytes=mib * MIB)


def cost(flops, read):
    return pl.CostEstimate(flops=flops, bytes_accessed=read, transcendentals=0)


def any_specs(values):
    return [pl.BlockSpec(memory_space=pl.ANY)] * len(values)


def hbm_specs(count):
    return [pl.BlockSpec(memory_space=pltpu.HBM)] * count


def held_specs(count):
    return [pl.BlockSpec(memory_space=pltpu.VMEM)] * count


def head_copies(wg_ref, wu_ref, first, step, head_ref, sems):
    cols = pl.ds(first * step, step)
    return [
        pltpu.make_async_copy(ref.at[:, cols], head_ref.at[i], sems.at[i])
        for i, ref in enumerate((wg_ref, wu_ref))
    ]


def bring_kernel(step, x_ref, dy_ref, wg_ref, wu_ref, x_out, dy_out, head_ref, sems):
    copies = head_copies(wg_ref, wu_ref, 0, step, head_ref, sems)
    for copy in copies:
        copy.start()
    x_out[...] = x_ref[...]
    dy_out[...] = dy_ref[...]
    for copy in copies:
        copy.wait()


def bring(x, dy, wg, wu, step):
    return pl.pallas_call(
        functools.partial(bring_kernel, step),
        in_specs=held_specs(2) + hbm_specs(2),
        out_specs=held_specs(3),
        out_shape=[jax.ShapeDtypeStruct(x.shape, BF16)] * 2
        + [jax.ShapeDtypeStruct((2, wg.shape[0], step), BF16)],
        scratch_shapes=[pltpu.SemaphoreType.DMA((2,))],
        compiler_params=params(46),
        cost_estimate=cost(0, 4 * wg.shape[0] * step),
        name="bring",
    )(x, dy, wg, wu)


def pack_kernel(count, *refs):
    out_ref = refs[-1]
    start = 0
    for piece in refs[:count]:
        out_ref[pl.ds(start, piece.shape[0]), :] = piece[...]
        start += piece.shape[0]


def pack(pieces, after):
    depth = pieces[0].shape[1]
    rows = sum(piece.shape[0] for piece in pieces)
    whole = pl.BlockSpec(memory_space=pltpu.VMEM)
    return pl.pallas_call(
        functools.partial(pack_kernel, len(pieces)),
        in_specs=[whole] * len(pieces) + any_specs(after),
        out_specs=whole,
        out_shape=jax.ShapeDtypeStruct((rows, depth), BF16),
        compiler_params=params(8),
        cost_estimate=cost(0, 4 * rows * depth),
        name="pack",
    )(*pieces, *after)


def pack_turned_kernel(count, *refs):
    pieces, out_ref = refs[:count], refs[-1]
    step = 512
    for c in range(0, out_ref.shape[0], step):
        block = jnp.concatenate([piece[:, c : c + step] for piece in pieces], axis=0)
        out_ref[c : c + step, :] = block.T


def pack_turned(pieces, after):
    depth = pieces[0].shape[1]
    rows = sum(piece.shape[0] for piece in pieces)
    return pl.pallas_call(
        functools.partial(pack_turned_kernel, len(pieces)),
        in_specs=held_specs(len(pieces)) + any_specs(after),
        out_specs=pl.BlockSpec(memory_space=pltpu.VMEM),
        out_shape=jax.ShapeDtypeStruct((depth, rows), BF16),
        compiler_params=params(8),
        cost_estimate=cost(0, 4 * rows * depth),
        name="pack_turned",
    )(*pieces, *after)


def put_rows(spot_ref, side, value, out_ref, cols):
    chips = spot_ref.shape[0]
    row = value.shape[0] // chips
    for p in range(chips):
        start = pl.multiple_of(spot_ref[p] + side * chips // SEQS * row, row)
        out_ref[pl.ds(start, row), cols] = value[p * row : (p + 1) * row, :]


def arrange_kernel(spot_ref, near_ref, far_ref, *rest):
    for side, ref in enumerate((near_ref, far_ref)):
        put_rows(spot_ref, side, ref[...], rest[-1], slice(None))


def arrange(spot, near, far, after):
    rows, depth = near.shape
    return pl.pallas_call(
        arrange_kernel,
        in_specs=[pl.BlockSpec(memory_space=pltpu.SMEM)] + held_specs(2) + any_specs(after),
        out_specs=pl.BlockSpec(memory_space=pltpu.VMEM),
        out_shape=jax.ShapeDtypeStruct((2 * rows, depth), BF16),
        compiler_params=params(6),
        cost_estimate=cost(0, 8 * rows * depth),
        name="arrange",
    )(spot, near, far, *after)


def gate_up_kernel(first, step, near_ref, far_ref, head_ref, wg_ref, wu_ref, wd_ref, *rest):
    a_ref, b_ref, next_ref, w_buf, out_buf, sems, out_sems, next_sems = rest[-8:]
    rows = near_ref.shape[0]
    tiles = a_ref.shape[0] // step

    def fetch(t):
        slot = t % 2
        return head_copies(wg_ref, wu_ref, first + t, step, w_buf.at[slot], sems.at[slot])

    def fetch_next():
        if next_ref.shape[0] == 2:
            return head_copies(wg_ref, wu_ref, first + tiles, step, next_ref, next_sems)
        return [pltpu.make_async_copy(wd_ref.at[pl.ds(0, step), :], next_ref, next_sems.at[0])]

    def store(t):
        to = pl.ds(t * step, step)
        return [
            pltpu.make_async_copy(out_buf.at[t, i], ref.at[to, :], out_sems.at[t, i])
            for i, ref in enumerate((a_ref, b_ref))
        ]

    def begin(copies):
        for copy in copies:
            copy.start()

    def finish(copies):
        for copy in copies:
            copy.wait()

    for t in range(1, min(3, tiles)):
        begin(fetch(t))
    for t in range(tiles):
        if t:
            finish(fetch(t))
        if t == tiles - 1:
            begin(fetch_next())
        w_ref = w_buf.at[t % 2] if t else head_ref
        for side, x_ref in enumerate((near_ref, far_ref)):
            gate = jnp.dot(x_ref[...], w_ref[0], preferred_element_type=F32)
            up = jnp.dot(x_ref[...], w_ref[1], preferred_element_type=F32)
            at = pl.ds(side * rows, rows)
            sigma = jax.nn.sigmoid(gate)
            out_buf[t, 0, :, at] = (up * sigma * (1.0 + gate * (1.0 - sigma))).T
            out_buf[t, 1, :, at] = (gate * sigma).T
        if t and t + 2 < tiles:
            begin(fetch(t + 2))
        begin(store(t))
    for t in range(tiles):
        finish(store(t))
    finish(fetch_next())


def gate_up(near, far, head, wg, wu, wd, first, count, step, grant, after):
    rows, depth = near.shape
    last = (first + count) * step == wg.shape[1]
    return pl.pallas_call(
        functools.partial(gate_up_kernel, first, step),
        in_specs=held_specs(3) + hbm_specs(3) + any_specs(after),
        out_specs=hbm_specs(2) + held_specs(1),
        out_shape=[jax.ShapeDtypeStruct((count * step, 2 * rows), F32)] * 2
        + [jax.ShapeDtypeStruct((step, depth) if last else (2, depth, step), BF16)],
        scratch_shapes=[
            pltpu.VMEM((2, 2, depth, step), BF16),
            pltpu.VMEM((count, 2, step, 2 * rows), F32),
            pltpu.SemaphoreType.DMA((2, 2)),
            pltpu.SemaphoreType.DMA((count, 2)),
            pltpu.SemaphoreType.DMA((2,)),
        ],
        compiler_params=params(grant),
        cost_estimate=cost(8 * rows * depth * count * step, 4 * depth * count * step),
        name="gate_up",
    )(near, far, head, wg, wu, wd, *after)


def back_kernel(
    step, deep, pieces, spot_ref, near_ref, far_ref, head_ref, wg_ref, wu_ref, wd_ref, *refs
):
    a_refs, b_refs = refs[:pieces], refs[pieces : 2 * pieces]
    ggs_ref, gus_ref, own_ref, sent_ref, g_ref = refs[2 * pieces : 2 * pieces + 5]
    wd_buf, w_buf, factor_buf, sems, w_sems, factor_sems = refs[2 * pieces + 5 :]
    width = wg_ref.shape[1]
    rows = near_ref.shape[1]
    tiles = wd_ref.shape[0] // step

    def fetch(t):
        at = pl.ds(pl.multiple_of(t * step, step), step)
        slot = lax.rem(t, 2)
        return pltpu.make_async_copy(wd_ref.at[at, :], wd_buf.at[slot], sems.at[slot])

    def fetch_rows(i):
        at = pl.ds(pl.multiple_of(i * deep, deep), deep)
        slot = lax.rem(i, 2)
        return [
            pltpu.make_async_copy(
                w_ref.at[at, :], w_buf.at[slot, :, pl.ds(k * width, width)], w_sems.at[slot, k]
            )
            for k, w_ref in enumerate((wg_ref, wu_ref))
        ]

    starts = [0]
    for a_ref in a_refs:
        starts.append(starts[-1] + a_ref.shape[0])

    def fetch_factors(p):
        at = pl.ds(starts[p], starts[p + 1] - starts[p])
        return [
            pltpu.make_async_copy(ref, factor_buf.at[k, at, :], factor_sems.at[k, p])
            for k, ref in enumerate((a_refs[p], b_refs[p]))
        ]

    def hidden_tile(t, wd):
        cols = pl.ds(pl.multiple_of(t * step, step), step)
        for side, dy_ref in enumerate((near_ref, far_ref)):
            hidden = jnp.dot(wd, dy_ref[...], preferred_element_type=F32)
            at = pl.ds(side * rows, rows)
            for f, gs_ref in enumerate((ggs_ref, gus_ref)):
                grad = (hidden * factor_buf[f, cols, at]).astype(BF16)
                to = pl.multiple_of(t * step + f * width, step)
                g_ref[pl.ds(to, step), at] = grad
                put_rows(spot_ref, side, grad.T, gs_ref, cols)

    blocks = wg_ref.shape[0] // deep
    for copy in fetch_factors(0):
        copy.start()
    for t in range(1, min(3, tiles)):
        fetch(jnp.int32(t)).start()
    for p in range(pieces):
        if p + 1 < pieces:
            for copy in fetch_factors(p + 1):
                copy.start()
        else:
            for i in range(2):
                for copy in fetch_rows(jnp.int32(i)):
                    copy.start()
        for copy in fetch_factors(p):
            copy.wait()

        if p == 0:
            hidden_tile(0, head_ref[...])

        @pl.loop(max(starts[p] // step, 1), starts[p + 1] // step)
        def _(t):
            fetch(t).wait()
            hidden_tile(t, wd_buf[lax.rem(t, 2)])

            @pl.when(t + 2 < tiles)
            def _():
                fetch(t + 2).start()

    @pl.loop(0, blocks)
    def _(i):
        at = pl.ds(pl.multiple_of(i * deep, deep), deep)
        slot = lax.rem(i, 2)
        for copy in fetch_rows(i):
            copy.wait()
        for side, out_ref in enumerate((own_ref, sent_ref)):
            of = pl.ds(side * rows, rows)
            total = jnp.dot(w_buf[slot], g_ref[:, of], preferred_element_type=F32)
            out_ref[:, at] = total.astype(BF16).T

        @pl.when(i + 2 < blocks)
        def _():
            for copy in fetch_rows(i + 2):
                copy.start()


def back(spot, near, far, head, wg, wu, wd, factors):
    depth, rows = near.shape
    width = wd.shape[0]
    step = tile(width, 256)
    a = [pair[0] for pair in factors]
    b = [pair[1] for pair in factors]
    return pl.pallas_call(
        functools.partial(back_kernel, step, 512, len(a)),
        in_specs=[pl.BlockSpec(memory_space=pltpu.SMEM)]
        + held_specs(3)
        + hbm_specs(3)
        + any_specs(a + b),
        out_specs=held_specs(4),
        out_shape=[jax.ShapeDtypeStruct((2 * rows, width), BF16)] * 2
        + [jax.ShapeDtypeStruct((rows, depth), BF16)] * 2,
        scratch_shapes=[
            pltpu.VMEM((2 * width, 2 * rows), BF16),
            pltpu.VMEM((2, step, depth), BF16),
            pltpu.VMEM((2, 512, 2 * width), BF16),
            pltpu.VMEM((2, width, 2 * rows), F32),
            pltpu.SemaphoreType.DMA((2,)),
            pltpu.SemaphoreType.DMA((2, 2)),
            pltpu.SemaphoreType.DMA((2, len(a))),
        ],
        compiler_params=params(28),
        cost_estimate=cost(12 * rows * depth * width, 6 * depth * width),
        name="hidden_back",
    )(spot, near, far, head, wg, wu, wd, *a, *b)


def fold_kernel(got, *refs):
    outs = refs[-len(got) :]
    refs = list(refs)
    for has, out_ref in zip(got, outs):
        total = refs.pop(0)[...].astype(F32) + refs.pop(0)[...].astype(F32)
        if has:
            total += refs.pop(0)[...].astype(F32)
        out_ref[...] = total.astype(BF16)


def fold(own, near, row, sends, after):
    depth = own.shape[1]
    operands, specs = [], []
    for p, got in sends:
        block = pl.BlockSpec((row, depth), lambda i, p=p: (p, 0))
        operands += [own, near]
        specs += [block, block]
        if got is not None:
            operands.append(got)
            specs.append(pl.BlockSpec((row, depth), lambda i: (0, 0)))
    return pl.pallas_call(
        functools.partial(fold_kernel, [got is not None for _, got in sends]),
        grid=(1,),
        in_specs=specs + any_specs(after),
        out_specs=[pl.BlockSpec((row, depth), lambda i: (0, 0))] * len(sends),
        out_shape=[jax.ShapeDtypeStruct((row, depth), BF16)] * len(sends),
        compiler_params=params(24),
        cost_estimate=cost(0, 16 * row * depth),
        name="fold",
    )(*operands, *after)


def last_kernel(*refs):
    total = refs[0][...].astype(F32)
    for ref in refs[1:-1]:
        total += ref[...].astype(F32)
    refs[-1][...] = total.astype(BF16)


def last(own, near, got):
    block = pl.BlockSpec(got[0].shape, lambda i: (0, 0))
    return pl.pallas_call(
        last_kernel,
        grid=(1,),
        in_specs=[block] * (2 + len(got)),
        out_specs=block,
        out_shape=jax.ShapeDtypeStruct(got[0].shape, BF16),
        compiler_params=params(24),
        cost_estimate=cost(0, 12 * got[0].size),
        name="last",
    )(own, near, *got)


def fisher_kernel(step, x_ref, gg_ref, gu_ref, *rest):
    fg_ref, fu_ref, done_ref = rest[-3:]
    done_ref[...] = jnp.zeros_like(done_ref)
    span = x_ref.shape[0] // SEQS
    seqs = [pl.ds(q * span, span) for q in range(SEQS)]
    cols = [x_ref[at, :].T for at in seqs]
    for g_ref, f_ref in ((gg_ref, fg_ref), (gu_ref, fu_ref)):
        for c in range(g_ref.shape[1] // step):
            at = pl.ds(c * step, step)
            total = None
            for q in range(SEQS):
                seq = jnp.dot(cols[q], g_ref[seqs[q], at], preferred_element_type=F32)
                total = seq * seq if total is None else total + seq * seq
            f_ref[:, at] = (total * (1.0 / SEQS)).astype(BF16)


def fisher(x, gg, gu, first, count, step, held, after):
    rows, depth = x.shape
    width = gg.shape[1]
    block = pl.BlockSpec((step, width), lambda j: (first + j, 0))
    return pl.pallas_call(
        functools.partial(fisher_kernel, tile(width, 256)),
        grid=(count,),
        in_specs=[pl.BlockSpec((rows, step), lambda j: (0, first + j))]
        + held_specs(2)
        + any_specs((*held, *after)),
        out_specs=[block, block, pl.BlockSpec((8, 128), lambda j: (0, 0))],
        out_shape=[jax.ShapeDtypeStruct((depth, width), BF16)] * 2
        + [jax.ShapeDtypeStruct((8, 128), F32)],
        input_output_aliases={3 + i: i for i in range(len(held))},
        compiler_params=params(40),
        cost_estimate=cost(4 * rows * step * count * width, 4 * step * count * width),
        name="fisher",
    )(x, gg, gu, *held, *after)


def ring_part(tokens, grad_out, wg, wu, wd):
    chips = len(CYCLE)
    far = chips // 2
    row, depth = tokens.shape
    width = wg.shape[1]
    links = [(CYCLE[i], CYCLE[(i + 1) % chips]) for i in range(chips)]
    to_right = [(2 * a + c, 2 * b + c) for a, b in links for c in range(2)]
    to_left = [(b, a) for a, b in to_right]
    across = [(2 * i + c, 2 * i + 1 - c) for i in range(chips) for c in range(2)]
    ends = [(CYCLE[i], CYCLE[(i + far) % chips]) for i in range(chips)]
    to_far = [(2 * a + c, 2 * b + c) for a, b in ends for c in range(2)]

    def straight(value):
        return lax.ppermute(value, "hid", to_far)

    def right(value):
        return lax.ppermute(value, "hid", to_right)

    def left(value):
        return lax.ppermute(value, "hid", to_left)

    def swap(value):
        return lax.ppermute(value, "hid", across)

    cycle = jnp.array(CYCLE, jnp.int32)
    where = jnp.array([CYCLE.index(c) for c in range(chips)], jnp.int32)
    around = jnp.arange(chips, dtype=jnp.int32)
    chip = cycle[(where[lax.axis_index("hid") // 2] - around) % chips]
    span = chips // SEQS
    spot = (chip // span * 2 * span + chip % span) * row

    def both(r, l, after=()):
        (r, l), _ = lax.optimization_barrier(((r, l), after))
        return right(r), left(l)

    def blocks(own, rounds, end):
        return [own] + [r for r, _ in rounds] + [end] + [l for _, l in rounds[::-1]]

    lane = tile(width, 256)
    tiles = width // lane
    cuts = [0, 4, 7]

    def piece(i, head, after):
        grant = (30, 28)[i]
        count = cuts[i + 1] - cuts[i]
        a, b, head = gate_up(
            near_x, far_x, head, wg, wu, wd, cuts[i], count, lane, grant, after
        )
        return (a, b), head

    own_x, own_dy, head = bring(tokens, grad_out, wg, wu, lane)
    in_x = [both(tokens, tokens)]
    end_x = straight(tokens)
    in_x.append(both(*in_x[-1], (own_x, head)))
    in_dy = [both(own_dy, own_dy, (in_x[0], end_x))]
    in_x.append(both(*in_x[-1], in_dy[-1]))
    in_dy.append(both(*in_dy[-1]))
    near_x = pack(blocks(own_x, in_x, end_x), (spot, *in_dy[-1]))
    far_x = swap(near_x)

    in_dy.append(both(*in_dy[-1], in_x[-1]))
    end_dy = straight(lax.optimization_barrier((own_dy, in_x[-1]))[0])
    some, head = piece(0, head, in_dy[-2])
    factors = [some]
    x = arrange(spot, near_x, far_x, in_dy[-2])
    near_dy = pack_turned(blocks(own_dy, in_dy, end_dy), (x, *some))
    far_dy = swap(near_dy)
    some, head = piece(1, head, (near_dy,))
    factors.append(some)
    gg, gu, own, sent = back(spot, near_dy, far_dy, head, wg, wu, wd, factors)

    near = swap(sent)
    step = 256
    counts = [3, 5, 4, 4]
    held, first = (), 0
    r = l = end = None
    ready = ()
    for k in range(far - 1, 0, -1):
        *held, done = fisher(x, gg, gu, first, counts[far - 1 - k], step, held, ready)
        first += counts[far - 1 - k]
        sends = [(chips - k, r), (k, l)]
        if end is None:
            sends.append((far, None))
        ready = fold(own, near, row, sends, (done,))
        r, l = right(ready[0]), left(ready[1])
        if end is None:
            end = straight(ready[2])
    fg, fu, _ = fisher(x, gg, gu, first, counts[-1], step, held, ready)
    mine = last(own, near, (r, l, end))
    return fg, fu, mine


def plain_forward_kernel(x_ref, wg_ref, wu_ref, gate_ref, up_ref):
    x = x_ref[...]
    gate_ref[...] = jnp.dot(x, wg_ref[...], preferred_element_type=jnp.float32)
    up_ref[...] = jnp.dot(x, wu_ref[...], preferred_element_type=jnp.float32)


def plain_forward(x, wg, wu):
    rows, depth = x.shape
    width = wg.shape[1]
    step = tile(width, 256)
    return pl.pallas_call(
        plain_forward_kernel,
        grid=(width // step,),
        in_specs=[
            pl.BlockSpec((rows, depth), lambda j: (0, 0)),
            pl.BlockSpec((depth, step), lambda j: (0, j)),
            pl.BlockSpec((depth, step), lambda j: (0, j)),
        ],
        out_specs=[pl.BlockSpec((rows, step), lambda j: (0, j))] * 2,
        out_shape=[jax.ShapeDtypeStruct((rows, width), jnp.float32)] * 2,
        compiler_params=params(40),
        cost_estimate=cost(4 * rows * depth * width, 4 * depth * width),
        name="gate_up",
    )(x, wg, wu)


def plain_back_kernel(parts, dy_ref, wd_ref, gate_ref, up_ref, gg_ref, gu_ref):
    rows = dy_ref.shape[0] // parts
    for p in range(parts):
        at = pl.ds(p * rows, rows)
        hidden = lax.dot_general(dy_ref[at, :], wd_ref[...], NT, preferred_element_type=jnp.float32)
        gate = gate_ref[at, :]
        sigma = jax.nn.sigmoid(gate)
        both = hidden * sigma
        gg_ref[at, :] = (both * up_ref[at, :] * (1.0 + gate * (1.0 - sigma))).astype(jnp.bfloat16)
        gu_ref[at, :] = (both * gate).astype(jnp.bfloat16)


def plain_back(dy, wd, gate, up):
    rows, depth = dy.shape
    width = wd.shape[0]
    step = tile(width, 256)
    column = pl.BlockSpec((rows, step), lambda j: (0, j))
    return pl.pallas_call(
        functools.partial(plain_back_kernel, 2),
        grid=(width // step,),
        in_specs=[
            pl.BlockSpec((rows, depth), lambda j: (0, 0)),
            pl.BlockSpec((step, depth), lambda j: (j, 0)),
            column,
            column,
        ],
        out_specs=[column, column],
        out_shape=[jax.ShapeDtypeStruct((rows, width), jnp.bfloat16)] * 2,
        compiler_params=params(40),
        cost_estimate=cost(2 * rows * depth * width, 2 * depth * width),
        name="hidden_back",
    )(dy, wd, gate, up)


def plain_input_kernel(gg_ref, gu_ref, wg_ref, wu_ref, out_ref):
    total = lax.dot_general(gg_ref[...], wg_ref[...], NT, preferred_element_type=jnp.float32)
    total += lax.dot_general(gu_ref[...], wu_ref[...], NT, preferred_element_type=jnp.float32)
    out_ref[...] = total.astype(jnp.bfloat16)


def plain_input_terms(gg, gu, wg, wu):
    rows, width = gg.shape
    depth = wg.shape[0]
    step = 512
    held = pl.BlockSpec((rows, width), lambda j: (0, 0))
    return pl.pallas_call(
        plain_input_kernel,
        grid=(depth // step,),
        in_specs=[
            held,
            held,
            pl.BlockSpec((step, width), lambda j: (j, 0)),
            pl.BlockSpec((step, width), lambda j: (j, 0)),
        ],
        out_specs=pl.BlockSpec((rows, step), lambda j: (0, j)),
        out_shape=jax.ShapeDtypeStruct((rows, depth), jnp.bfloat16),
        compiler_params=params(40),
        cost_estimate=cost(4 * rows * depth * width, 4 * depth * width),
        name="input_terms",
    )(gg, gu, wg, wu)


def plain_fisher_kernel(step, x_ref, gg_ref, gu_ref, fg_ref, fu_ref):
    half = x_ref.shape[0] // 2
    span = half // SEQS
    width = gg_ref.shape[1]

    def rows(ref, q, at):
        near = ref[pl.ds(q * span, span), at]
        far = ref[pl.ds(half + q * span, span), at]
        return jnp.concatenate([near, far], axis=0)

    xs = [rows(x_ref, q, slice(None)).T for q in range(SEQS)]
    for g_ref, f_ref in ((gg_ref, fg_ref), (gu_ref, fu_ref)):
        for c in range(width // step):
            at = pl.ds(c * step, step)
            total = None
            for q in range(SEQS):
                seq = jnp.dot(xs[q], rows(g_ref, q, at), preferred_element_type=jnp.float32)
                total = seq * seq if total is None else total + seq * seq
            f_ref[:, at] = (total * (1.0 / SEQS)).astype(jnp.bfloat16)


def plain_fisher(x, gg, gu):
    rows, depth = x.shape
    width = gg.shape[1]
    step = 512
    held = pl.BlockSpec((rows, width), lambda j: (0, 0))
    block = pl.BlockSpec((step, width), lambda j: (j, 0))
    return pl.pallas_call(
        functools.partial(plain_fisher_kernel, tile(width, 256)),
        grid=(depth // step,),
        in_specs=[pl.BlockSpec((rows, step), lambda j: (0, j)), held, held],
        out_specs=[block, block],
        out_shape=[jax.ShapeDtypeStruct((depth, width), jnp.bfloat16)] * 2,
        compiler_params=params(40),
        cost_estimate=cost(4 * rows * depth * width, 4 * depth * width),
        name="fisher",
    )(x, gg, gu)


def plain_part(size, tokens, grad_out, wg, wu, wd):
    chips = size // 2
    across = [[2 * i + c for i in range(chips)] for c in range(2)]
    pairs = [[2 * i, 2 * i + 1] for i in range(chips)]
    block, depth = tokens.shape

    def gather(rows):
        near = lax.all_gather(rows, "hid", axis=0, tiled=True, axis_index_groups=across)
        return lax.all_gather(near, "hid", axis=0, tiled=False, axis_index_groups=pairs)

    x = gather(tokens).reshape(-1, depth)
    dy = gather(grad_out).reshape(-1, depth)
    gate, up = plain_forward(x, wg, wu)
    gg, gu = plain_back(dy, wd, gate, up)
    terms = plain_input_terms(gg, gu, wg, wu).reshape(2, -1, depth)
    mine = lax.psum_scatter(
        terms, "hid", scatter_dimension=0, tiled=False, axis_index_groups=pairs
    )
    mine = lax.psum_scatter(
        mine, "hid", scatter_dimension=0, tiled=True, axis_index_groups=across
    )
    fg, fu = plain_fisher(x, gg, gu)
    return fg, fu, mine


def per_device(size, tokens, grad_out, wg, wu, wd):
    fits = tokens.shape[0] == 32 and wg.shape == (4096, 1792)
    if size == 2 * len(CYCLE) and fits:
        return ring_part(tokens, grad_out, wg, wu, wd)
    return plain_part(size, tokens, grad_out, wg, wu, wd)


def solution(mesh):
    rows = P(("adjust", "hid"), None)
    weights = P("adjust", "hid")
    return jax.shard_map(
        functools.partial(per_device, mesh.shape["hid"]),
        mesh=mesh,
        in_specs=(rows, rows, weights, weights, rows),
        out_specs=(weights, weights, rows),
        check_vma=False,
    )
```

```python
import functools

import jax
import jax.numpy as jnp
from jax import lax
from jax.experimental import pallas as pl
from jax.experimental.pallas import tpu as pltpu
from jax.sharding import PartitionSpec as P

SEQS = 2
MIB = 1 << 20
CYCLE = (0, 2, 4, 6, 7, 5, 3, 1)
NT = (((1,), (1,)), ((), ()))
BF16 = jnp.bfloat16
F32 = jnp.float32


def tile(size, want):
    return want if size % want == 0 else size


def params(mib):
    return pltpu.CompilerParams(vmem_limit_bytes=mib * MIB)


def cost(flops, read):
    return pl.CostEstimate(flops=flops, bytes_accessed=read, transcendentals=0)


def any_specs(values):
    return [pl.BlockSpec(memory_space=pl.ANY)] * len(values)


def hbm_specs(count):
    return [pl.BlockSpec(memory_space=pltpu.HBM)] * count


def held_specs(count):
    return [pl.BlockSpec(memory_space=pltpu.VMEM)] * count


def head_copies(wg_ref, wu_ref, first, step, head_ref, sems):
    cols = pl.ds(first * step, step)
    return [
        pltpu.make_async_copy(ref.at[:, cols], head_ref.at[i], sems.at[i])
        for i, ref in enumerate((wg_ref, wu_ref))
    ]


def bring_kernel(step, x_ref, dy_ref, wg_ref, wu_ref, x_out, dy_out, head_ref, sems):
    copies = head_copies(wg_ref, wu_ref, 0, step, head_ref, sems)
    for copy in copies:
        copy.start()
    x_out[...] = x_ref[...]
    dy_out[...] = dy_ref[...]
    for copy in copies:
        copy.wait()


def bring(x, dy, wg, wu, step):
    return pl.pallas_call(
        functools.partial(bring_kernel, step),
        in_specs=held_specs(2) + hbm_specs(2),
        out_specs=held_specs(3),
        out_shape=[jax.ShapeDtypeStruct(x.shape, BF16)] * 2
        + [jax.ShapeDtypeStruct((2, wg.shape[0], step), BF16)],
        scratch_shapes=[pltpu.SemaphoreType.DMA((2,))],
        compiler_params=params(46),
        cost_estimate=cost(0, 4 * wg.shape[0] * step),
        name="bring",
    )(x, dy, wg, wu)


def relay_kernel(in_ref, *rest):
    rest[-1][...] = in_ref[...]


def relay(value, after):
    return pl.pallas_call(
        relay_kernel,
        in_specs=held_specs(1) + any_specs(after),
        out_specs=pl.BlockSpec(memory_space=pltpu.VMEM),
        out_shape=jax.ShapeDtypeStruct(value.shape, value.dtype),
        compiler_params=params(4),
        cost_estimate=cost(0, 4 * value.size),
        name="relay",
    )(value, *after)


def pack_kernel(count, *refs):
    out_ref = refs[-1]
    start = 0
    for piece in refs[:count]:
        out_ref[pl.ds(start, piece.shape[0]), :] = piece[...]
        start += piece.shape[0]


def pack(pieces, after):
    depth = pieces[0].shape[1]
    rows = sum(piece.shape[0] for piece in pieces)
    whole = pl.BlockSpec(memory_space=pltpu.VMEM)
    return pl.pallas_call(
        functools.partial(pack_kernel, len(pieces)),
        in_specs=[whole] * len(pieces) + any_specs(after),
        out_specs=whole,
        out_shape=jax.ShapeDtypeStruct((rows, depth), BF16),
        compiler_params=params(8),
        cost_estimate=cost(0, 4 * rows * depth),
        name="pack",
    )(*pieces, *after)


def pack_turned_kernel(count, *refs):
    pieces, out_ref = refs[:count], refs[-1]
    step = 512
    for c in range(0, out_ref.shape[0], step):
        block = jnp.concatenate([piece[:, c : c + step] for piece in pieces], axis=0)
        out_ref[c : c + step, :] = block.T


def pack_turned(pieces, after):
    depth = pieces[0].shape[1]
    rows = sum(piece.shape[0] for piece in pieces)
    return pl.pallas_call(
        functools.partial(pack_turned_kernel, len(pieces)),
        in_specs=held_specs(len(pieces)) + any_specs(after),
        out_specs=pl.BlockSpec(memory_space=pltpu.VMEM),
        out_shape=jax.ShapeDtypeStruct((depth, rows), BF16),
        compiler_params=params(8),
        cost_estimate=cost(0, 4 * rows * depth),
        name="pack_turned",
    )(*pieces, *after)


def put_rows(spot_ref, side, value, out_ref, cols):
    chips = spot_ref.shape[0]
    row = value.shape[0] // chips
    for p in range(chips):
        start = pl.multiple_of(spot_ref[p] + side * chips // SEQS * row, row)
        out_ref[pl.ds(start, row), cols] = value[p * row : (p + 1) * row, :]


def arrange_kernel(spot_ref, near_ref, far_ref, *rest):
    for side, ref in enumerate((near_ref, far_ref)):
        put_rows(spot_ref, side, ref[...], rest[-1], slice(None))


def arrange(spot, near, far, after):
    rows, depth = near.shape
    return pl.pallas_call(
        arrange_kernel,
        in_specs=[pl.BlockSpec(memory_space=pltpu.SMEM)] + held_specs(2) + any_specs(after),
        out_specs=pl.BlockSpec(memory_space=pltpu.VMEM),
        out_shape=jax.ShapeDtypeStruct((2 * rows, depth), BF16),
        compiler_params=params(6),
        cost_estimate=cost(0, 8 * rows * depth),
        name="arrange",
    )(spot, near, far, *after)


def gate_up_kernel(first, step, near_ref, far_ref, head_ref, wg_ref, wu_ref, wd_ref, *rest):
    a_ref, b_ref, next_ref, w_buf, out_buf, sems, out_sems, next_sems = rest[-8:]
    rows = near_ref.shape[0]
    tiles = a_ref.shape[0] // step

    def fetch(t):
        slot = t % 2
        return head_copies(wg_ref, wu_ref, first + t, step, w_buf.at[slot], sems.at[slot])

    def fetch_next():
        if next_ref.shape[0] == 2:
            return head_copies(wg_ref, wu_ref, first + tiles, step, next_ref, next_sems)
        return [pltpu.make_async_copy(wd_ref.at[pl.ds(0, step), :], next_ref, next_sems.at[0])]

    def store(t):
        to = pl.ds(t * step, step)
        return [
            pltpu.make_async_copy(out_buf.at[t, i], ref.at[to, :], out_sems.at[t, i])
            for i, ref in enumerate((a_ref, b_ref))
        ]

    def begin(copies):
        for copy in copies:
            copy.start()

    def finish(copies):
        for copy in copies:
            copy.wait()

    for t in range(1, min(3, tiles)):
        begin(fetch(t))
    for t in range(tiles):
        if t:
            finish(fetch(t))
        if t == tiles - 1:
            begin(fetch_next())
        w_ref = w_buf.at[t % 2] if t else head_ref
        for side, x_ref in enumerate((near_ref, far_ref)):
            gate = jnp.dot(x_ref[...], w_ref[0], preferred_element_type=F32)
            up = jnp.dot(x_ref[...], w_ref[1], preferred_element_type=F32)
            at = pl.ds(side * rows, rows)
            sigma = jax.nn.sigmoid(gate)
            out_buf[t, 0, :, at] = (up * sigma * (1.0 + gate * (1.0 - sigma))).T
            out_buf[t, 1, :, at] = (gate * sigma).T
        if t and t + 2 < tiles:
            begin(fetch(t + 2))
        begin(store(t))
    for t in range(tiles):
        finish(store(t))
    finish(fetch_next())


def gate_up(near, far, head, wg, wu, wd, first, count, step, grant, after):
    rows, depth = near.shape
    last = (first + count) * step == wg.shape[1]
    return pl.pallas_call(
        functools.partial(gate_up_kernel, first, step),
        in_specs=held_specs(3) + hbm_specs(3) + any_specs(after),
        out_specs=hbm_specs(2) + held_specs(1),
        out_shape=[jax.ShapeDtypeStruct((count * step, 2 * rows), F32)] * 2
        + [jax.ShapeDtypeStruct((step, depth) if last else (2, depth, step), BF16)],
        scratch_shapes=[
            pltpu.VMEM((2, 2, depth, step), BF16),
            pltpu.VMEM((count, 2, step, 2 * rows), F32),
            pltpu.SemaphoreType.DMA((2, 2)),
            pltpu.SemaphoreType.DMA((count, 2)),
            pltpu.SemaphoreType.DMA((2,)),
        ],
        compiler_params=params(grant),
        cost_estimate=cost(8 * rows * depth * count * step, 4 * depth * count * step),
        name="gate_up",
    )(near, far, head, wg, wu, wd, *after)


def back_kernel(
    step, deep, pieces, spot_ref, near_ref, far_ref, head_ref, wg_ref, wu_ref, wd_ref, *refs
):
    a_refs, b_refs = refs[:pieces], refs[pieces : 2 * pieces]
    ggs_ref, gus_ref, own_ref, sent_ref, g_ref = refs[2 * pieces : 2 * pieces + 5]
    wd_buf, w_buf, factor_buf, sems, w_sems, factor_sems = refs[2 * pieces + 5 :]
    width = wg_ref.shape[1]
    rows = near_ref.shape[1]
    tiles = wd_ref.shape[0] // step

    def fetch(t):
        at = pl.ds(pl.multiple_of(t * step, step), step)
        slot = lax.rem(t, 2)
        return pltpu.make_async_copy(wd_ref.at[at, :], wd_buf.at[slot], sems.at[slot])

    def fetch_rows(i):
        at = pl.ds(pl.multiple_of(i * deep, deep), deep)
        slot = lax.rem(i, 2)
        return [
            pltpu.make_async_copy(
                w_ref.at[at, :], w_buf.at[slot, :, pl.ds(k * width, width)], w_sems.at[slot, k]
            )
            for k, w_ref in enumerate((wg_ref, wu_ref))
        ]

    starts = [0]
    for a_ref in a_refs:
        starts.append(starts[-1] + a_ref.shape[0])

    def fetch_factors(p):
        at = pl.ds(starts[p], starts[p + 1] - starts[p])
        return [
            pltpu.make_async_copy(ref, factor_buf.at[k, at, :], factor_sems.at[k, p])
            for k, ref in enumerate((a_refs[p], b_refs[p]))
        ]

    def hidden_tile(t, wd):
        cols = pl.ds(pl.multiple_of(t * step, step), step)
        for side, dy_ref in enumerate((near_ref, far_ref)):
            hidden = jnp.dot(wd, dy_ref[...], preferred_element_type=F32)
            at = pl.ds(side * rows, rows)
            for f, gs_ref in enumerate((ggs_ref, gus_ref)):
                grad = (hidden * factor_buf[f, cols, at]).astype(BF16)
                to = pl.multiple_of(t * step + f * width, step)
                g_ref[pl.ds(to, step), at] = grad
                put_rows(spot_ref, side, grad.T, gs_ref, cols)

    blocks = wg_ref.shape[0] // deep
    for copy in fetch_factors(0):
        copy.start()
    for t in range(1, min(3, tiles)):
        fetch(jnp.int32(t)).start()
    for p in range(pieces):
        if p + 1 < pieces:
            for copy in fetch_factors(p + 1):
                copy.start()
        else:
            for i in range(2):
                for copy in fetch_rows(jnp.int32(i)):
                    copy.start()
        for copy in fetch_factors(p):
            copy.wait()

        if p == 0:
            hidden_tile(0, head_ref[...])

        @pl.loop(max(starts[p] // step, 1), starts[p + 1] // step)
        def _(t):
            fetch(t).wait()
            hidden_tile(t, wd_buf[lax.rem(t, 2)])

            @pl.when(t + 2 < tiles)
            def _():
                fetch(t + 2).start()

    @pl.loop(0, blocks)
    def _(i):
        at = pl.ds(pl.multiple_of(i * deep, deep), deep)
        slot = lax.rem(i, 2)
        for copy in fetch_rows(i):
            copy.wait()
        for side, out_ref in enumerate((own_ref, sent_ref)):
            of = pl.ds(side * rows, rows)
            total = jnp.dot(w_buf[slot], g_ref[:, of], preferred_element_type=F32)
            out_ref[:, at] = total.astype(BF16).T

        @pl.when(i + 2 < blocks)
        def _():
            for copy in fetch_rows(i + 2):
                copy.start()


def back(spot, near, far, head, wg, wu, wd, factors):
    depth, rows = near.shape
    width = wd.shape[0]
    step = tile(width, 256)
    a = [pair[0] for pair in factors]
    b = [pair[1] for pair in factors]
    return pl.pallas_call(
        functools.partial(back_kernel, step, 512, len(a)),
        in_specs=[pl.BlockSpec(memory_space=pltpu.SMEM)]
        + held_specs(3)
        + hbm_specs(3)
        + any_specs(a + b),
        out_specs=held_specs(4),
        out_shape=[jax.ShapeDtypeStruct((2 * rows, width), BF16)] * 2
        + [jax.ShapeDtypeStruct((rows, depth), BF16)] * 2,
        scratch_shapes=[
            pltpu.VMEM((2 * width, 2 * rows), BF16),
            pltpu.VMEM((2, step, depth), BF16),
            pltpu.VMEM((2, 512, 2 * width), BF16),
            pltpu.VMEM((2, width, 2 * rows), F32),
            pltpu.SemaphoreType.DMA((2,)),
            pltpu.SemaphoreType.DMA((2, 2)),
            pltpu.SemaphoreType.DMA((2, len(a))),
        ],
        compiler_params=params(28),
        cost_estimate=cost(12 * rows * depth * width, 6 * depth * width),
        name="hidden_back",
    )(spot, near, far, head, wg, wu, wd, *a, *b)


def fold_kernel(cuts, *refs):
    count = len(cuts)
    outs = refs[-count:]
    for i, (at, got_at) in enumerate(cuts):
        own_ref, near_ref, got_ref = refs[3 * i : 3 * i + 3]
        out_ref = outs[i]
        out_ref[...] = (own_ref[at, :].astype(F32) + near_ref[at, :].astype(F32)).astype(BF16)
        if got_at is not None:
            total = own_ref[got_at, :].astype(F32) + near_ref[got_at, :].astype(F32)
            out_ref[got_at, :] = (total + got_ref[...].astype(F32)).astype(BF16)


def fold(own, near, row, sends, after):
    depth = own.shape[1]
    operands, specs, shapes, cuts = [], [], [], []
    for p, at, got_at, got in sends:
        block = pl.BlockSpec((row, depth), lambda i, p=p: (p, 0))
        got = near if got is None else got
        size = got.shape[0] if got_at is not None else row
        operands += [own, near, got]
        specs += [block, block, pl.BlockSpec((size, depth), lambda i: (0, 0))]
        shapes.append(jax.ShapeDtypeStruct((at.size, depth), BF16))
        cuts.append((at, got_at))
    return pl.pallas_call(
        functools.partial(fold_kernel, cuts),
        grid=(1,),
        in_specs=specs + any_specs(after),
        out_specs=[pl.BlockSpec(shape.shape, lambda i: (0, 0)) for shape in shapes],
        out_shape=shapes,
        compiler_params=params(24),
        cost_estimate=cost(0, 16 * row * depth),
        name="fold",
    )(*operands, *after)


def last_kernel(own_ref, near_ref, r_ref, l_ref, out_ref):
    total = own_ref[...].astype(F32) + near_ref[...].astype(F32)
    out_ref[...] = (total + r_ref[...].astype(F32) + l_ref[...].astype(F32)).astype(BF16)


def last(own, near, r, l):
    block = pl.BlockSpec(r.shape, lambda i: (0, 0))
    return pl.pallas_call(
        last_kernel,
        grid=(1,),
        in_specs=[block] * 4,
        out_specs=block,
        out_shape=jax.ShapeDtypeStruct(r.shape, BF16),
        compiler_params=params(24),
        cost_estimate=cost(0, 12 * r.size),
        name="last",
    )(own, near, r, l)


def fisher_kernel(step, x_ref, gg_ref, gu_ref, *rest):
    fg_ref, fu_ref, done_ref = rest[-3:]
    done_ref[...] = jnp.zeros_like(done_ref)
    span = x_ref.shape[0] // SEQS
    seqs = [pl.ds(q * span, span) for q in range(SEQS)]
    cols = [x_ref[at, :].T for at in seqs]
    for g_ref, f_ref in ((gg_ref, fg_ref), (gu_ref, fu_ref)):
        for c in range(g_ref.shape[1] // step):
            at = pl.ds(c * step, step)
            total = None
            for q in range(SEQS):
                seq = jnp.dot(cols[q], g_ref[seqs[q], at], preferred_element_type=F32)
                total = seq * seq if total is None else total + seq * seq
            f_ref[:, at] = (total * (1.0 / SEQS)).astype(BF16)


def fisher(x, gg, gu, first, count, step, held, after):
    rows, depth = x.shape
    width = gg.shape[1]
    block = pl.BlockSpec((step, width), lambda j: (first + j, 0))
    return pl.pallas_call(
        functools.partial(fisher_kernel, tile(width, 256)),
        grid=(count,),
        in_specs=[pl.BlockSpec((rows, step), lambda j: (0, first + j))]
        + held_specs(2)
        + any_specs((*held, *after)),
        out_specs=[block, block, pl.BlockSpec((8, 128), lambda j: (0, 0))],
        out_shape=[jax.ShapeDtypeStruct((depth, width), BF16)] * 2
        + [jax.ShapeDtypeStruct((8, 128), F32)],
        input_output_aliases={3 + i: i for i in range(len(held))},
        compiler_params=params(40),
        cost_estimate=cost(4 * rows * step * count * width, 4 * step * count * width),
        name="fisher",
    )(x, gg, gu, *held, *after)


def ring_part(tokens, grad_out, wg, wu, wd):
    chips = len(CYCLE)
    far = chips // 2
    row, depth = tokens.shape
    width = wg.shape[1]
    links = [(CYCLE[i], CYCLE[(i + 1) % chips]) for i in range(chips)]
    to_right = [(2 * a + c, 2 * b + c) for a, b in links for c in range(2)]
    to_left = [(b, a) for a, b in to_right]
    across = [(2 * i + c, 2 * i + 1 - c) for i in range(chips) for c in range(2)]

    def right(value):
        return lax.ppermute(value, "hid", to_right)

    def left(value):
        return lax.ppermute(value, "hid", to_left)

    def swap(value):
        return lax.ppermute(value, "hid", across)

    cycle = jnp.array(CYCLE, jnp.int32)
    where = jnp.array([CYCLE.index(c) for c in range(chips)], jnp.int32)
    around = jnp.arange(chips, dtype=jnp.int32)
    chip = cycle[(where[lax.axis_index("hid") // 2] - around) % chips]
    span = chips // SEQS
    spot = (chip // span * 2 * span + chip % span) * row

    def both(r, l, after=(), ends=False):
        (r, l), _ = lax.optimization_barrier(((r, l), after))
        if ends:
            r, l = r[: row // 2], l[row // 2 :]
        return right(r), left(l)

    def blocks(own, rounds):
        return [own] + [r for r, _ in rounds] + [l for _, l in rounds[::-1]]

    lane = tile(width, 256)
    tiles = width // lane
    cuts = [0, 2, 5, 7]

    def piece(i, head, after):
        grant = (30, 28, 28)[i]
        count = cuts[i + 1] - cuts[i]
        a, b, head = gate_up(
            near_x, far_x, head, wg, wu, wd, cuts[i], count, lane, grant, after
        )
        return (a, b), head

    own_x, own_dy, head = bring(tokens, grad_out, wg, wu, lane)
    in_x = [both(tokens, tokens)]
    in_x.append(both(*in_x[-1], (own_x, head)))
    in_dy = [both(own_dy, own_dy, in_x[0])]
    for _ in range(3, far):
        in_x.append(both(*in_x[-1]))
        in_dy.append(both(*in_dy[-1]))
    in_x.append(both(*in_x[-1], in_dy[0], True))
    near_x = pack(blocks(own_x, in_x), (spot, *in_dy[-1]))
    far_x = swap(near_x)

    in_dy.append(both(*in_dy[-1], in_x[-2]))
    some, head = piece(0, head, in_dy[-2])
    factors = [some]
    in_dy.append(both(*in_dy[-1], some, True))
    some, head = piece(1, head, in_dy[-2])
    factors.append(some)
    x = arrange(spot, near_x, far_x, in_dy[-2])
    near_dy = pack_turned(blocks(own_dy, in_dy), (x, *some))
    far_dy = swap(near_dy)
    some, head = piece(2, head, (near_dy,))
    factors.append(some)
    gg, gu, own, sent = back(spot, near_dy, far_dy, head, wg, wu, wd, factors)

    near = swap(sent)
    full, head, tail = pl.ds(0, row), pl.ds(0, row // 2), pl.ds(row // 2, row // 2)
    step = 256
    counts = [4, 2, 4, 4, 2]
    held, first = (), 0
    r = l = None
    ready = ()
    for k in range(far, 0, -1):
        *held, done = fisher(x, gg, gu, first, counts[far - k], step, held, ready)
        first += counts[far - k]
        if k == far:
            sends = [(far, head, None, None), (far, tail, None, None)]
        elif k == far - 1:
            sends = [(chips - k, full, head, r), (k, full, tail, l)]
        else:
            sends = [(chips - k, full, full, r), (k, full, full, l)]
        ready = fold(own, near, row, sends, (done,))
        r, l = right(ready[0]), left(ready[1])
    fg, fu, _ = fisher(x, gg, gu, first, counts[far], step, held, ready)
    mine = last(own, near, r, l)
    return fg, fu, mine


def plain_forward_kernel(x_ref, wg_ref, wu_ref, gate_ref, up_ref):
    x = x_ref[...]
    gate_ref[...] = jnp.dot(x, wg_ref[...], preferred_element_type=jnp.float32)
    up_ref[...] = jnp.dot(x, wu_ref[...], preferred_element_type=jnp.float32)


def plain_forward(x, wg, wu):
    rows, depth = x.shape
    width = wg.shape[1]
    step = tile(width, 256)
    return pl.pallas_call(
        plain_forward_kernel,
        grid=(width // step,),
        in_specs=[
            pl.BlockSpec((rows, depth), lambda j: (0, 0)),
            pl.BlockSpec((depth, step), lambda j: (0, j)),
            pl.BlockSpec((depth, step), lambda j: (0, j)),
        ],
        out_specs=[pl.BlockSpec((rows, step), lambda j: (0, j))] * 2,
        out_shape=[jax.ShapeDtypeStruct((rows, width), jnp.float32)] * 2,
        compiler_params=params(40),
        cost_estimate=cost(4 * rows * depth * width, 4 * depth * width),
        name="gate_up",
    )(x, wg, wu)


def plain_back_kernel(parts, dy_ref, wd_ref, gate_ref, up_ref, gg_ref, gu_ref):
    rows = dy_ref.shape[0] // parts
    for p in range(parts):
        at = pl.ds(p * rows, rows)
        hidden = lax.dot_general(dy_ref[at, :], wd_ref[...], NT, preferred_element_type=jnp.float32)
        gate = gate_ref[at, :]
        sigma = jax.nn.sigmoid(gate)
        both = hidden * sigma
        gg_ref[at, :] = (both * up_ref[at, :] * (1.0 + gate * (1.0 - sigma))).astype(jnp.bfloat16)
        gu_ref[at, :] = (both * gate).astype(jnp.bfloat16)


def plain_back(dy, wd, gate, up):
    rows, depth = dy.shape
    width = wd.shape[0]
    step = tile(width, 256)
    column = pl.BlockSpec((rows, step), lambda j: (0, j))
    return pl.pallas_call(
        functools.partial(plain_back_kernel, 2),
        grid=(width // step,),
        in_specs=[
            pl.BlockSpec((rows, depth), lambda j: (0, 0)),
            pl.BlockSpec((step, depth), lambda j: (j, 0)),
            column,
            column,
        ],
        out_specs=[column, column],
        out_shape=[jax.ShapeDtypeStruct((rows, width), jnp.bfloat16)] * 2,
        compiler_params=params(40),
        cost_estimate=cost(2 * rows * depth * width, 2 * depth * width),
        name="hidden_back",
    )(dy, wd, gate, up)


def plain_input_kernel(gg_ref, gu_ref, wg_ref, wu_ref, out_ref):
    total = lax.dot_general(gg_ref[...], wg_ref[...], NT, preferred_element_type=jnp.float32)
    total += lax.dot_general(gu_ref[...], wu_ref[...], NT, preferred_element_type=jnp.float32)
    out_ref[...] = total.astype(jnp.bfloat16)


def plain_input_terms(gg, gu, wg, wu):
    rows, width = gg.shape
    depth = wg.shape[0]
    step = 512
    held = pl.BlockSpec((rows, width), lambda j: (0, 0))
    return pl.pallas_call(
        plain_input_kernel,
        grid=(depth // step,),
        in_specs=[
            held,
            held,
            pl.BlockSpec((step, width), lambda j: (j, 0)),
            pl.BlockSpec((step, width), lambda j: (j, 0)),
        ],
        out_specs=pl.BlockSpec((rows, step), lambda j: (0, j)),
        out_shape=jax.ShapeDtypeStruct((rows, depth), jnp.bfloat16),
        compiler_params=params(40),
        cost_estimate=cost(4 * rows * depth * width, 4 * depth * width),
        name="input_terms",
    )(gg, gu, wg, wu)


def plain_fisher_kernel(step, x_ref, gg_ref, gu_ref, fg_ref, fu_ref):
    half = x_ref.shape[0] // 2
    span = half // SEQS
    width = gg_ref.shape[1]

    def rows(ref, q, at):
        near = ref[pl.ds(q * span, span), at]
        far = ref[pl.ds(half + q * span, span), at]
        return jnp.concatenate([near, far], axis=0)

    xs = [rows(x_ref, q, slice(None)).T for q in range(SEQS)]
    for g_ref, f_ref in ((gg_ref, fg_ref), (gu_ref, fu_ref)):
        for c in range(width // step):
            at = pl.ds(c * step, step)
            total = None
            for q in range(SEQS):
                seq = jnp.dot(xs[q], rows(g_ref, q, at), preferred_element_type=jnp.float32)
                total = seq * seq if total is None else total + seq * seq
            f_ref[:, at] = (total * (1.0 / SEQS)).astype(jnp.bfloat16)


def plain_fisher(x, gg, gu):
    rows, depth = x.shape
    width = gg.shape[1]
    step = 512
    held = pl.BlockSpec((rows, width), lambda j: (0, 0))
    block = pl.BlockSpec((step, width), lambda j: (j, 0))
    return pl.pallas_call(
        functools.partial(plain_fisher_kernel, tile(width, 256)),
        grid=(depth // step,),
        in_specs=[pl.BlockSpec((rows, step), lambda j: (0, j)), held, held],
        out_specs=[block, block],
        out_shape=[jax.ShapeDtypeStruct((depth, width), jnp.bfloat16)] * 2,
        compiler_params=params(40),
        cost_estimate=cost(4 * rows * depth * width, 4 * depth * width),
        name="fisher",
    )(x, gg, gu)


def plain_part(size, tokens, grad_out, wg, wu, wd):
    chips = size // 2
    across = [[2 * i + c for i in range(chips)] for c in range(2)]
    pairs = [[2 * i, 2 * i + 1] for i in range(chips)]
    block, depth = tokens.shape

    def gather(rows):
        near = lax.all_gather(rows, "hid", axis=0, tiled=True, axis_index_groups=across)
        return lax.all_gather(near, "hid", axis=0, tiled=False, axis_index_groups=pairs)

    x = gather(tokens).reshape(-1, depth)
    dy = gather(grad_out).reshape(-1, depth)
    gate, up = plain_forward(x, wg, wu)
    gg, gu = plain_back(dy, wd, gate, up)
    terms = plain_input_terms(gg, gu, wg, wu).reshape(2, -1, depth)
    mine = lax.psum_scatter(
        terms, "hid", scatter_dimension=0, tiled=False, axis_index_groups=pairs
    )
    mine = lax.psum_scatter(
        mine, "hid", scatter_dimension=0, tiled=True, axis_index_groups=across
    )
    fg, fu = plain_fisher(x, gg, gu)
    return fg, fu, mine


def per_device(size, tokens, grad_out, wg, wu, wd):
    fits = tokens.shape[0] == 32 and wg.shape == (4096, 1792)
    if size == 2 * len(CYCLE) and fits:
        return ring_part(tokens, grad_out, wg, wu, wd)
    return plain_part(size, tokens, grad_out, wg, wu, wd)


def solution(mesh):
    rows = P(("adjust", "hid"), None)
    weights = P("adjust", "hid")
    return jax.shard_map(
        functools.partial(per_device, mesh.shape["hid"]),
        mesh=mesh,
        in_specs=(rows, rows, weights, weights, rows),
        out_specs=(weights, weights, rows),
        check_vma=False,
    )
```

```python
import functools

import jax
import jax.numpy as jnp
from jax import lax
from jax.experimental import pallas as pl
from jax.experimental.pallas import tpu as pltpu
from jax.sharding import PartitionSpec as P

SEQS = 2
MIB = 1 << 20
CYCLE = (0, 2, 4, 6, 7, 5, 3, 1)
NT = (((1,), (1,)), ((), ()))
BF16 = jnp.bfloat16
F32 = jnp.float32


def tile(size, want):
    return want if size % want == 0 else size


def params(mib):
    return pltpu.CompilerParams(vmem_limit_bytes=mib * MIB)


def cost(flops, read):
    return pl.CostEstimate(flops=flops, bytes_accessed=read, transcendentals=0)


def any_specs(values):
    return [pl.BlockSpec(memory_space=pl.ANY)] * len(values)


def hbm_specs(count):
    return [pl.BlockSpec(memory_space=pltpu.HBM)] * count


def held_specs(count):
    return [pl.BlockSpec(memory_space=pltpu.VMEM)] * count


def head_copies(wg_ref, wu_ref, first, step, head_ref, sems):
    cols = pl.ds(first * step, step)
    return [
        pltpu.make_async_copy(ref.at[:, cols], head_ref.at[i], sems.at[i])
        for i, ref in enumerate((wg_ref, wu_ref))
    ]


def bring_kernel(step, x_ref, dy_ref, wg_ref, wu_ref, x_out, dy_out, head_ref, sems):
    copies = head_copies(wg_ref, wu_ref, 0, step, head_ref, sems)
    for copy in copies:
        copy.start()
    x_out[...] = x_ref[...]
    dy_out[...] = dy_ref[...]
    for copy in copies:
        copy.wait()


def bring(x, dy, wg, wu, step):
    return pl.pallas_call(
        functools.partial(bring_kernel, step),
        in_specs=held_specs(2) + hbm_specs(2),
        out_specs=held_specs(3),
        out_shape=[jax.ShapeDtypeStruct(x.shape, BF16)] * 2
        + [jax.ShapeDtypeStruct((2, wg.shape[0], step), BF16)],
        scratch_shapes=[pltpu.SemaphoreType.DMA((2,))],
        compiler_params=params(46),
        cost_estimate=cost(0, 4 * wg.shape[0] * step),
        name="bring",
    )(x, dy, wg, wu)


def relay_kernel(in_ref, *rest):
    rest[-1][...] = in_ref[...]


def relay(value, after):
    return pl.pallas_call(
        relay_kernel,
        in_specs=held_specs(1) + any_specs(after),
        out_specs=pl.BlockSpec(memory_space=pltpu.VMEM),
        out_shape=jax.ShapeDtypeStruct(value.shape, value.dtype),
        compiler_params=params(4),
        cost_estimate=cost(0, 4 * value.size),
        name="relay",
    )(value, *after)


def pack_kernel(count, *refs):
    out_ref = refs[-1]
    start = 0
    for piece in refs[:count]:
        out_ref[pl.ds(start, piece.shape[0]), :] = piece[...]
        start += piece.shape[0]


def pack(pieces, after):
    depth = pieces[0].shape[1]
    rows = sum(piece.shape[0] for piece in pieces)
    whole = pl.BlockSpec(memory_space=pltpu.VMEM)
    return pl.pallas_call(
        functools.partial(pack_kernel, len(pieces)),
        in_specs=[whole] * len(pieces) + any_specs(after),
        out_specs=whole,
        out_shape=jax.ShapeDtypeStruct((rows, depth), BF16),
        compiler_params=params(8),
        cost_estimate=cost(0, 4 * rows * depth),
        name="pack",
    )(*pieces, *after)


def pack_turned_kernel(count, *refs):
    pieces, out_ref = refs[:count], refs[-1]
    step = 512
    for c in range(0, out_ref.shape[0], step):
        block = jnp.concatenate([piece[:, c : c + step] for piece in pieces], axis=0)
        out_ref[c : c + step, :] = block.T


def pack_turned(pieces, after):
    depth = pieces[0].shape[1]
    rows = sum(piece.shape[0] for piece in pieces)
    return pl.pallas_call(
        functools.partial(pack_turned_kernel, len(pieces)),
        in_specs=held_specs(len(pieces)) + any_specs(after),
        out_specs=pl.BlockSpec(memory_space=pltpu.VMEM),
        out_shape=jax.ShapeDtypeStruct((depth, rows), BF16),
        compiler_params=params(8),
        cost_estimate=cost(0, 4 * rows * depth),
        name="pack_turned",
    )(*pieces, *after)


def put_rows(spot_ref, side, value, out_ref, cols):
    chips = spot_ref.shape[0]
    row = value.shape[0] // chips
    for p in range(chips):
        start = pl.multiple_of(spot_ref[p] + side * chips // SEQS * row, row)
        out_ref[pl.ds(start, row), cols] = value[p * row : (p + 1) * row, :]


def arrange_kernel(spot_ref, near_ref, far_ref, *rest):
    for side, ref in enumerate((near_ref, far_ref)):
        put_rows(spot_ref, side, ref[...], rest[-1], slice(None))


def arrange(spot, near, far, after):
    rows, depth = near.shape
    return pl.pallas_call(
        arrange_kernel,
        in_specs=[pl.BlockSpec(memory_space=pltpu.SMEM)] + held_specs(2) + any_specs(after),
        out_specs=pl.BlockSpec(memory_space=pltpu.VMEM),
        out_shape=jax.ShapeDtypeStruct((2 * rows, depth), BF16),
        compiler_params=params(6),
        cost_estimate=cost(0, 8 * rows * depth),
        name="arrange",
    )(spot, near, far, *after)


def gate_up_kernel(first, step, near_ref, far_ref, head_ref, wg_ref, wu_ref, wd_ref, *rest):
    a_ref, b_ref, next_ref, w_buf, out_buf, sems, out_sems, next_sems = rest[-8:]
    rows = near_ref.shape[0]
    tiles = a_ref.shape[0] // step

    def fetch(t):
        slot = t % 2
        return head_copies(wg_ref, wu_ref, first + t, step, w_buf.at[slot], sems.at[slot])

    def fetch_next():
        if next_ref.shape[0] == 2:
            return head_copies(wg_ref, wu_ref, first + tiles, step, next_ref, next_sems)
        return [pltpu.make_async_copy(wd_ref.at[pl.ds(0, step), :], next_ref, next_sems.at[0])]

    def store(t):
        to = pl.ds(t * step, step)
        return [
            pltpu.make_async_copy(out_buf.at[t % 2, i], ref.at[to, :], out_sems.at[t % 2, i])
            for i, ref in enumerate((a_ref, b_ref))
        ]

    def begin(copies):
        for copy in copies:
            copy.start()

    def finish(copies):
        for copy in copies:
            copy.wait()

    for t in range(1, min(3, tiles)):
        begin(fetch(t))
    for t in range(tiles):
        if t:
            finish(fetch(t))
        if t == tiles - 1:
            begin(fetch_next())
        w_ref = w_buf.at[t % 2] if t else head_ref
        if t > 1:
            finish(store(t - 2))
        for side, x_ref in enumerate((near_ref, far_ref)):
            gate = jnp.dot(x_ref[...], w_ref[0], preferred_element_type=F32)
            up = jnp.dot(x_ref[...], w_ref[1], preferred_element_type=F32)
            at = pl.ds(side * rows, rows)
            sigma = jax.nn.sigmoid(gate)
            out_buf[t % 2, 0, :, at] = (up * sigma * (1.0 + gate * (1.0 - sigma))).T
            out_buf[t % 2, 1, :, at] = (gate * sigma).T
        if t and t + 2 < tiles:
            begin(fetch(t + 2))
        begin(store(t))
    for t in range(max(tiles - 2, 0), tiles):
        finish(store(t))
    finish(fetch_next())


def gate_up(near, far, head, wg, wu, wd, first, count, step, grant, after):
    rows, depth = near.shape
    last = (first + count) * step == wg.shape[1]
    return pl.pallas_call(
        functools.partial(gate_up_kernel, first, step),
        in_specs=held_specs(3) + hbm_specs(3) + any_specs(after),
        out_specs=hbm_specs(2) + held_specs(1),
        out_shape=[jax.ShapeDtypeStruct((count * step, 2 * rows), F32)] * 2
        + [jax.ShapeDtypeStruct((step, depth) if last else (2, depth, step), BF16)],
        scratch_shapes=[
            pltpu.VMEM((2, 2, depth, step), BF16),
            pltpu.VMEM((2, 2, step, 2 * rows), F32),
            pltpu.SemaphoreType.DMA((2, 2)),
            pltpu.SemaphoreType.DMA((2, 2)),
            pltpu.SemaphoreType.DMA((2,)),
        ],
        compiler_params=params(grant),
        cost_estimate=cost(8 * rows * depth * count * step, 4 * depth * count * step),
        name="gate_up",
    )(near, far, head, wg, wu, wd, *after)


def back_kernel(
    step, deep, pieces, spot_ref, near_ref, far_ref, head_ref, wg_ref, wu_ref, wd_ref, *refs
):
    a_refs, b_refs = refs[:pieces], refs[pieces : 2 * pieces]
    ggs_ref, gus_ref, own_ref, sent_ref, g_ref = refs[2 * pieces : 2 * pieces + 5]
    wd_buf, w_buf, factor_buf, sems, w_sems, factor_sems = refs[2 * pieces + 5 :]
    width = wg_ref.shape[1]
    rows = near_ref.shape[1]
    tiles = wd_ref.shape[0] // step

    def fetch(t):
        at = pl.ds(pl.multiple_of(t * step, step), step)
        slot = lax.rem(t, 2)
        return pltpu.make_async_copy(wd_ref.at[at, :], wd_buf.at[slot], sems.at[slot])

    def fetch_rows(i):
        at = pl.ds(pl.multiple_of(i * deep, deep), deep)
        slot = lax.rem(i, 2)
        return [
            pltpu.make_async_copy(
                w_ref.at[at, :], w_buf.at[slot, :, pl.ds(k * width, width)], w_sems.at[slot, k]
            )
            for k, w_ref in enumerate((wg_ref, wu_ref))
        ]

    starts = [0]
    for a_ref in a_refs:
        starts.append(starts[-1] + a_ref.shape[0])

    def fetch_factors(p):
        at = pl.ds(starts[p], starts[p + 1] - starts[p])
        return [
            pltpu.make_async_copy(ref, factor_buf.at[k, at, :], factor_sems.at[k, p])
            for k, ref in enumerate((a_refs[p], b_refs[p]))
        ]

    def hidden_tile(t, wd):
        cols = pl.ds(pl.multiple_of(t * step, step), step)
        for side, dy_ref in enumerate((near_ref, far_ref)):
            hidden = jnp.dot(wd, dy_ref[...], preferred_element_type=F32)
            at = pl.ds(side * rows, rows)
            for f, gs_ref in enumerate((ggs_ref, gus_ref)):
                grad = (hidden * factor_buf[f, cols, at]).astype(BF16)
                to = pl.multiple_of(t * step + f * width, step)
                g_ref[pl.ds(to, step), at] = grad
                put_rows(spot_ref, side, grad.T, gs_ref, cols)

    blocks = wg_ref.shape[0] // deep
    for copy in fetch_factors(0):
        copy.start()
    for t in range(1, min(3, tiles)):
        fetch(jnp.int32(t)).start()
    for p in range(pieces):
        if p + 1 < pieces:
            for copy in fetch_factors(p + 1):
                copy.start()
        else:
            for i in range(2):
                for copy in fetch_rows(jnp.int32(i)):
                    copy.start()
        for copy in fetch_factors(p):
            copy.wait()

        if p == 0:
            hidden_tile(0, head_ref[...])

        @pl.loop(max(starts[p] // step, 1), starts[p + 1] // step)
        def _(t):
            fetch(t).wait()
            hidden_tile(t, wd_buf[lax.rem(t, 2)])

            @pl.when(t + 2 < tiles)
            def _():
                fetch(t + 2).start()

    @pl.loop(0, blocks)
    def _(i):
        at = pl.ds(pl.multiple_of(i * deep, deep), deep)
        slot = lax.rem(i, 2)
        for copy in fetch_rows(i):
            copy.wait()
        for side, out_ref in enumerate((own_ref, sent_ref)):
            of = pl.ds(side * rows, rows)
            total = jnp.dot(w_buf[slot], g_ref[:, of], preferred_element_type=F32)
            out_ref[:, at] = total.astype(BF16).T

        @pl.when(i + 2 < blocks)
        def _():
            for copy in fetch_rows(i + 2):
                copy.start()


def back(spot, near, far, head, wg, wu, wd, factors):
    depth, rows = near.shape
    width = wd.shape[0]
    step = tile(width, 256)
    a = [pair[0] for pair in factors]
    b = [pair[1] for pair in factors]
    return pl.pallas_call(
        functools.partial(back_kernel, step, 512, len(a)),
        in_specs=[pl.BlockSpec(memory_space=pltpu.SMEM)]
        + held_specs(3)
        + hbm_specs(3)
        + any_specs(a + b),
        out_specs=held_specs(4),
        out_shape=[jax.ShapeDtypeStruct((2 * rows, width), BF16)] * 2
        + [jax.ShapeDtypeStruct((rows, depth), BF16)] * 2,
        scratch_shapes=[
            pltpu.VMEM((2 * width, 2 * rows), BF16),
            pltpu.VMEM((2, step, depth), BF16),
            pltpu.VMEM((2, 512, 2 * width), BF16),
            pltpu.VMEM((2, width, 2 * rows), F32),
            pltpu.SemaphoreType.DMA((2,)),
            pltpu.SemaphoreType.DMA((2, 2)),
            pltpu.SemaphoreType.DMA((2, len(a))),
        ],
        compiler_params=params(26),
        cost_estimate=cost(12 * rows * depth * width, 6 * depth * width),
        name="hidden_back",
    )(spot, near, far, head, wg, wu, wd, *a, *b)


def fold_kernel(cuts, *refs):
    count = len(cuts)
    outs = refs[-count:]
    for i, (at, got_at) in enumerate(cuts):
        own_ref, near_ref, got_ref = refs[3 * i : 3 * i + 3]
        out_ref = outs[i]
        out_ref[...] = (own_ref[at, :].astype(F32) + near_ref[at, :].astype(F32)).astype(BF16)
        if got_at is not None:
            total = own_ref[got_at, :].astype(F32) + near_ref[got_at, :].astype(F32)
            out_ref[got_at, :] = (total + got_ref[...].astype(F32)).astype(BF16)


def fold(own, near, row, sends, after):
    depth = own.shape[1]
    operands, specs, shapes, cuts = [], [], [], []
    for p, at, got_at, got in sends:
        block = pl.BlockSpec((row, depth), lambda i, p=p: (p, 0))
        got = near if got is None else got
        size = got.shape[0] if got_at is not None else row
        operands += [own, near, got]
        specs += [block, block, pl.BlockSpec((size, depth), lambda i: (0, 0))]
        shapes.append(jax.ShapeDtypeStruct((at.size, depth), BF16))
        cuts.append((at, got_at))
    return pl.pallas_call(
        functools.partial(fold_kernel, cuts),
        grid=(1,),
        in_specs=specs + any_specs(after),
        out_specs=[pl.BlockSpec(shape.shape, lambda i: (0, 0)) for shape in shapes],
        out_shape=shapes,
        compiler_params=params(24),
        cost_estimate=cost(0, 16 * row * depth),
        name="fold",
    )(*operands, *after)


def last_kernel(own_ref, near_ref, r_ref, l_ref, out_ref):
    total = own_ref[...].astype(F32) + near_ref[...].astype(F32)
    out_ref[...] = (total + r_ref[...].astype(F32) + l_ref[...].astype(F32)).astype(BF16)


def last(own, near, r, l):
    block = pl.BlockSpec(r.shape, lambda i: (0, 0))
    return pl.pallas_call(
        last_kernel,
        grid=(1,),
        in_specs=[block] * 4,
        out_specs=block,
        out_shape=jax.ShapeDtypeStruct(r.shape, BF16),
        compiler_params=params(24),
        cost_estimate=cost(0, 12 * r.size),
        name="last",
    )(own, near, r, l)


def fisher_kernel(step, x_ref, gg_ref, gu_ref, *rest):
    fg_ref, fu_ref, done_ref = rest[-3:]
    done_ref[...] = jnp.zeros_like(done_ref)
    span = x_ref.shape[0] // SEQS
    seqs = [pl.ds(q * span, span) for q in range(SEQS)]
    cols = [x_ref[at, :].T for at in seqs]
    for g_ref, f_ref in ((gg_ref, fg_ref), (gu_ref, fu_ref)):
        for c in range(g_ref.shape[1] // step):
            at = pl.ds(c * step, step)
            total = None
            for q in range(SEQS):
                seq = jnp.dot(cols[q], g_ref[seqs[q], at], preferred_element_type=F32)
                total = seq * seq if total is None else total + seq * seq
            f_ref[:, at] = (total * (1.0 / SEQS)).astype(BF16)


def fisher(x, gg, gu, first, count, step, held, after):
    rows, depth = x.shape
    width = gg.shape[1]
    block = pl.BlockSpec((step, width), lambda j: (first + j, 0))
    return pl.pallas_call(
        functools.partial(fisher_kernel, tile(width, 256)),
        grid=(count,),
        in_specs=[pl.BlockSpec((rows, step), lambda j: (0, first + j))]
        + held_specs(2)
        + any_specs((*held, *after)),
        out_specs=[block, block, pl.BlockSpec((8, 128), lambda j: (0, 0))],
        out_shape=[jax.ShapeDtypeStruct((depth, width), BF16)] * 2
        + [jax.ShapeDtypeStruct((8, 128), F32)],
        input_output_aliases={3 + i: i for i in range(len(held))},
        compiler_params=params(40),
        cost_estimate=cost(4 * rows * step * count * width, 4 * step * count * width),
        name="fisher",
    )(x, gg, gu, *held, *after)


def ring_part(tokens, grad_out, wg, wu, wd):
    chips = len(CYCLE)
    far = chips // 2
    row, depth = tokens.shape
    width = wg.shape[1]
    links = [(CYCLE[i], CYCLE[(i + 1) % chips]) for i in range(chips)]
    to_right = [(2 * a + c, 2 * b + c) for a, b in links for c in range(2)]
    to_left = [(b, a) for a, b in to_right]
    across = [(2 * i + c, 2 * i + 1 - c) for i in range(chips) for c in range(2)]

    def right(value):
        return lax.ppermute(value, "hid", to_right)

    def left(value):
        return lax.ppermute(value, "hid", to_left)

    def swap(value):
        return lax.ppermute(value, "hid", across)

    cycle = jnp.array(CYCLE, jnp.int32)
    where = jnp.array([CYCLE.index(c) for c in range(chips)], jnp.int32)
    around = jnp.arange(chips, dtype=jnp.int32)
    chip = cycle[(where[lax.axis_index("hid") // 2] - around) % chips]
    span = chips // SEQS
    spot = (chip // span * 2 * span + chip % span) * row

    def both(r, l, after=(), ends=False):
        (r, l), _ = lax.optimization_barrier(((r, l), after))
        if ends:
            r, l = r[: row // 2], l[row // 2 :]
        return right(r), left(l)

    def blocks(own, rounds):
        return [own] + [r for r, _ in rounds] + [l for _, l in rounds[::-1]]

    lane = tile(width, 256)
    own_x, own_dy, head = bring(tokens, grad_out, wg, wu, lane)
    in_x = [both(tokens, tokens)]
    in_dy = [both(grad_out, grad_out)]
    in_x.append(both(*in_x[-1], (own_x, head)))
    in_dy.append(both(*in_dy[-1], in_x[0]))
    in_x.append(both(*in_x[-1], in_dy[0]))
    in_dy.append(both(*in_dy[-1], in_x[1]))
    in_x.append(both(*in_x[-1], in_dy[1], True))
    near_x = pack(blocks(own_x, in_x), (spot, *in_dy[2]))
    far_x = swap(near_x)
    in_dy.append(both(*in_dy[-1], in_x[2], True))
    near_dy = pack_turned(blocks(own_dy, in_dy), ())
    far_dy = swap(near_dy)
    a, b, head = gate_up(
        near_x, far_x, head, wg, wu, wd, 0, width // lane, lane, 26, (near_dy,)
    )
    gg, gu, own, sent = back(spot, near_dy, far_dy, head, wg, wu, wd, [(a, b)])
    x = arrange(spot, near_x, far_x, (own,))

    near = swap(sent)
    full, head, tail = pl.ds(0, row), pl.ds(0, row // 2), pl.ds(row // 2, row // 2)
    step = 256
    counts = [3, 3, 4, 4, 2]
    held, first = (), 0
    r = l = None
    ready = ()
    for k in range(far, 0, -1):
        *held, done = fisher(x, gg, gu, first, counts[far - k], step, held, ready)
        first += counts[far - k]
        if k == far:
            sends = [(far, head, None, None), (far, tail, None, None)]
        elif k == far - 1:
            sends = [(chips - k, full, head, r), (k, full, tail, l)]
        else:
            sends = [(chips - k, full, full, r), (k, full, full, l)]
        ready = fold(own, near, row, sends, (done,))
        r, l = right(ready[0]), left(ready[1])
    fg, fu, _ = fisher(x, gg, gu, first, counts[far], step, held, ready)
    mine = last(own, near, r, l)
    return fg, fu, mine


def plain_forward_kernel(x_ref, wg_ref, wu_ref, gate_ref, up_ref):
    x = x_ref[...]
    gate_ref[...] = jnp.dot(x, wg_ref[...], preferred_element_type=jnp.float32)
    up_ref[...] = jnp.dot(x, wu_ref[...], preferred_element_type=jnp.float32)


def plain_forward(x, wg, wu):
    rows, depth = x.shape
    width = wg.shape[1]
    step = tile(width, 256)
    return pl.pallas_call(
        plain_forward_kernel,
        grid=(width // step,),
        in_specs=[
            pl.BlockSpec((rows, depth), lambda j: (0, 0)),
            pl.BlockSpec((depth, step), lambda j: (0, j)),
            pl.BlockSpec((depth, step), lambda j: (0, j)),
        ],
        out_specs=[pl.BlockSpec((rows, step), lambda j: (0, j))] * 2,
        out_shape=[jax.ShapeDtypeStruct((rows, width), jnp.float32)] * 2,
        compiler_params=params(40),
        cost_estimate=cost(4 * rows * depth * width, 4 * depth * width),
        name="gate_up",
    )(x, wg, wu)


def plain_back_kernel(parts, dy_ref, wd_ref, gate_ref, up_ref, gg_ref, gu_ref):
    rows = dy_ref.shape[0] // parts
    for p in range(parts):
        at = pl.ds(p * rows, rows)
        hidden = lax.dot_general(dy_ref[at, :], wd_ref[...], NT, preferred_element_type=jnp.float32)
        gate = gate_ref[at, :]
        sigma = jax.nn.sigmoid(gate)
        both = hidden * sigma
        gg_ref[at, :] = (both * up_ref[at, :] * (1.0 + gate * (1.0 - sigma))).astype(jnp.bfloat16)
        gu_ref[at, :] = (both * gate).astype(jnp.bfloat16)


def plain_back(dy, wd, gate, up):
    rows, depth = dy.shape
    width = wd.shape[0]
    step = tile(width, 256)
    column = pl.BlockSpec((rows, step), lambda j: (0, j))
    return pl.pallas_call(
        functools.partial(plain_back_kernel, 2),
        grid=(width // step,),
        in_specs=[
            pl.BlockSpec((rows, depth), lambda j: (0, 0)),
            pl.BlockSpec((step, depth), lambda j: (j, 0)),
            column,
            column,
        ],
        out_specs=[column, column],
        out_shape=[jax.ShapeDtypeStruct((rows, width), jnp.bfloat16)] * 2,
        compiler_params=params(40),
        cost_estimate=cost(2 * rows * depth * width, 2 * depth * width),
        name="hidden_back",
    )(dy, wd, gate, up)


def plain_input_kernel(gg_ref, gu_ref, wg_ref, wu_ref, out_ref):
    total = lax.dot_general(gg_ref[...], wg_ref[...], NT, preferred_element_type=jnp.float32)
    total += lax.dot_general(gu_ref[...], wu_ref[...], NT, preferred_element_type=jnp.float32)
    out_ref[...] = total.astype(jnp.bfloat16)


def plain_input_terms(gg, gu, wg, wu):
    rows, width = gg.shape
    depth = wg.shape[0]
    step = 512
    held = pl.BlockSpec((rows, width), lambda j: (0, 0))
    return pl.pallas_call(
        plain_input_kernel,
        grid=(depth // step,),
        in_specs=[
            held,
            held,
            pl.BlockSpec((step, width), lambda j: (j, 0)),
            pl.BlockSpec((step, width), lambda j: (j, 0)),
        ],
        out_specs=pl.BlockSpec((rows, step), lambda j: (0, j)),
        out_shape=jax.ShapeDtypeStruct((rows, depth), jnp.bfloat16),
        compiler_params=params(40),
        cost_estimate=cost(4 * rows * depth * width, 4 * depth * width),
        name="input_terms",
    )(gg, gu, wg, wu)


def plain_fisher_kernel(step, x_ref, gg_ref, gu_ref, fg_ref, fu_ref):
    half = x_ref.shape[0] // 2
    span = half // SEQS
    width = gg_ref.shape[1]

    def rows(ref, q, at):
        near = ref[pl.ds(q * span, span), at]
        far = ref[pl.ds(half + q * span, span), at]
        return jnp.concatenate([near, far], axis=0)

    xs = [rows(x_ref, q, slice(None)).T for q in range(SEQS)]
    for g_ref, f_ref in ((gg_ref, fg_ref), (gu_ref, fu_ref)):
        for c in range(width // step):
            at = pl.ds(c * step, step)
            total = None
            for q in range(SEQS):
                seq = jnp.dot(xs[q], rows(g_ref, q, at), preferred_element_type=jnp.float32)
                total = seq * seq if total is None else total + seq * seq
            f_ref[:, at] = (total * (1.0 / SEQS)).astype(jnp.bfloat16)


def plain_fisher(x, gg, gu):
    rows, depth = x.shape
    width = gg.shape[1]
    step = 512
    held = pl.BlockSpec((rows, width), lambda j: (0, 0))
    block = pl.BlockSpec((step, width), lambda j: (j, 0))
    return pl.pallas_call(
        functools.partial(plain_fisher_kernel, tile(width, 256)),
        grid=(depth // step,),
        in_specs=[pl.BlockSpec((rows, step), lambda j: (0, j)), held, held],
        out_specs=[block, block],
        out_shape=[jax.ShapeDtypeStruct((depth, width), jnp.bfloat16)] * 2,
        compiler_params=params(40),
        cost_estimate=cost(4 * rows * depth * width, 4 * depth * width),
        name="fisher",
    )(x, gg, gu)


def plain_part(size, tokens, grad_out, wg, wu, wd):
    chips = size // 2
    across = [[2 * i + c for i in range(chips)] for c in range(2)]
    pairs = [[2 * i, 2 * i + 1] for i in range(chips)]
    block, depth = tokens.shape

    def gather(rows):
        near = lax.all_gather(rows, "hid", axis=0, tiled=True, axis_index_groups=across)
        return lax.all_gather(near, "hid", axis=0, tiled=False, axis_index_groups=pairs)

    x = gather(tokens).reshape(-1, depth)
    dy = gather(grad_out).reshape(-1, depth)
    gate, up = plain_forward(x, wg, wu)
    gg, gu = plain_back(dy, wd, gate, up)
    terms = plain_input_terms(gg, gu, wg, wu).reshape(2, -1, depth)
    mine = lax.psum_scatter(
        terms, "hid", scatter_dimension=0, tiled=False, axis_index_groups=pairs
    )
    mine = lax.psum_scatter(
        mine, "hid", scatter_dimension=0, tiled=True, axis_index_groups=across
    )
    fg, fu = plain_fisher(x, gg, gu)
    return fg, fu, mine


def per_device(size, tokens, grad_out, wg, wu, wd):
    fits = tokens.shape[0] == 32 and wg.shape == (4096, 1792)
    if size == 2 * len(CYCLE) and fits:
        return ring_part(tokens, grad_out, wg, wu, wd)
    return plain_part(size, tokens, grad_out, wg, wu, wd)


def solution(mesh):
    rows = P(("adjust", "hid"), None)
    weights = P("adjust", "hid")
    return jax.shard_map(
        functools.partial(per_device, mesh.shape["hid"]),
        mesh=mesh,
        in_specs=(rows, rows, weights, weights, rows),
        out_specs=(weights, weights, rows),
        check_vma=False,
    )
```

```python
import functools

import jax
import jax.numpy as jnp
from jax import lax
from jax.experimental import pallas as pl
from jax.experimental.pallas import tpu as pltpu
from jax.sharding import PartitionSpec as P

SEQS = 2
MIB = 1 << 20
CYCLE = (0, 2, 4, 6, 7, 5, 3, 1)
NT = (((1,), (1,)), ((), ()))
BF16 = jnp.bfloat16
F32 = jnp.float32


def tile(size, want):
    return want if size % want == 0 else size


def params(mib):
    return pltpu.CompilerParams(vmem_limit_bytes=mib * MIB)


def cost(flops, read):
    return pl.CostEstimate(flops=flops, bytes_accessed=read, transcendentals=0)


def any_specs(values):
    return [pl.BlockSpec(memory_space=pl.ANY)] * len(values)


def hbm_specs(count):
    return [pl.BlockSpec(memory_space=pltpu.HBM)] * count


def held_specs(count):
    return [pl.BlockSpec(memory_space=pltpu.VMEM)] * count


def head_copies(wg_ref, wu_ref, first, step, head_ref, sems):
    cols = pl.ds(first * step, step)
    return [
        pltpu.make_async_copy(ref.at[:, cols], head_ref.at[i], sems.at[i])
        for i, ref in enumerate((wg_ref, wu_ref))
    ]


def bring_kernel(step, x_ref, dy_ref, wg_ref, wu_ref, x_out, dy_out, head_ref, sems):
    copies = head_copies(wg_ref, wu_ref, 0, step, head_ref, sems)
    for copy in copies:
        copy.start()
    x_out[...] = x_ref[...]
    dy_out[...] = dy_ref[...]
    for copy in copies:
        copy.wait()


def bring(x, dy, wg, wu, step):
    return pl.pallas_call(
        functools.partial(bring_kernel, step),
        in_specs=held_specs(2) + hbm_specs(2),
        out_specs=held_specs(3),
        out_shape=[jax.ShapeDtypeStruct(x.shape, BF16)] * 2
        + [jax.ShapeDtypeStruct((2, wg.shape[0], step), BF16)],
        scratch_shapes=[pltpu.SemaphoreType.DMA((2,))],
        compiler_params=params(46),
        cost_estimate=cost(0, 4 * wg.shape[0] * step),
        name="bring",
    )(x, dy, wg, wu)


def relay_kernel(in_ref, *rest):
    rest[-1][...] = in_ref[...]


def relay(value, after):
    return pl.pallas_call(
        relay_kernel,
        in_specs=held_specs(1) + any_specs(after),
        out_specs=pl.BlockSpec(memory_space=pltpu.VMEM),
        out_shape=jax.ShapeDtypeStruct(value.shape, value.dtype),
        compiler_params=params(4),
        cost_estimate=cost(0, 4 * value.size),
        name="relay",
    )(value, *after)


def pack_kernel(count, *refs):
    out_ref = refs[-1]
    start = 0
    for piece in refs[:count]:
        out_ref[pl.ds(start, piece.shape[0]), :] = piece[...]
        start += piece.shape[0]


def pack(pieces, after):
    depth = pieces[0].shape[1]
    rows = sum(piece.shape[0] for piece in pieces)
    whole = pl.BlockSpec(memory_space=pltpu.VMEM)
    return pl.pallas_call(
        functools.partial(pack_kernel, len(pieces)),
        in_specs=[whole] * len(pieces) + any_specs(after),
        out_specs=whole,
        out_shape=jax.ShapeDtypeStruct((rows, depth), BF16),
        compiler_params=params(8),
        cost_estimate=cost(0, 4 * rows * depth),
        name="pack",
    )(*pieces, *after)


def pack_turned_kernel(count, *refs):
    pieces, out_ref = refs[:count], refs[-1]
    step = 512
    for c in range(0, out_ref.shape[0], step):
        block = jnp.concatenate([piece[:, c : c + step] for piece in pieces], axis=0)
        out_ref[c : c + step, :] = block.T


def pack_turned(pieces, after):
    depth = pieces[0].shape[1]
    rows = sum(piece.shape[0] for piece in pieces)
    return pl.pallas_call(
        functools.partial(pack_turned_kernel, len(pieces)),
        in_specs=held_specs(len(pieces)) + any_specs(after),
        out_specs=pl.BlockSpec(memory_space=pltpu.VMEM),
        out_shape=jax.ShapeDtypeStruct((depth, rows), BF16),
        compiler_params=params(8),
        cost_estimate=cost(0, 4 * rows * depth),
        name="pack_turned",
    )(*pieces, *after)


def put_rows(spot_ref, side, value, out_ref, cols):
    chips = spot_ref.shape[0]
    row = value.shape[0] // chips
    for p in range(chips):
        start = pl.multiple_of(spot_ref[p] + side * chips // SEQS * row, row)
        out_ref[pl.ds(start, row), cols] = value[p * row : (p + 1) * row, :]


def arrange_kernel(spot_ref, near_ref, far_ref, *rest):
    for side, ref in enumerate((near_ref, far_ref)):
        put_rows(spot_ref, side, ref[...], rest[-1], slice(None))


def arrange(spot, near, far, after):
    rows, depth = near.shape
    return pl.pallas_call(
        arrange_kernel,
        in_specs=[pl.BlockSpec(memory_space=pltpu.SMEM)] + held_specs(2) + any_specs(after),
        out_specs=pl.BlockSpec(memory_space=pltpu.VMEM),
        out_shape=jax.ShapeDtypeStruct((2 * rows, depth), BF16),
        compiler_params=params(6),
        cost_estimate=cost(0, 8 * rows * depth),
        name="arrange",
    )(spot, near, far, *after)


def gate_up_kernel(first, step, near_ref, far_ref, head_ref, wg_ref, wu_ref, wd_ref, *rest):
    a_ref, b_ref, next_ref, w_buf, out_buf, sems, out_sems, next_sems = rest[-8:]
    rows = near_ref.shape[0]
    tiles = a_ref.shape[0] // step

    def fetch(t):
        slot = t % 2
        return head_copies(wg_ref, wu_ref, first + t, step, w_buf.at[slot], sems.at[slot])

    def fetch_next():
        if next_ref.shape[0] == 2:
            return head_copies(wg_ref, wu_ref, first + tiles, step, next_ref, next_sems)
        return [pltpu.make_async_copy(wd_ref.at[pl.ds(0, step), :], next_ref, next_sems.at[0])]

    def store(t):
        to = pl.ds(t * step, step)
        return [
            pltpu.make_async_copy(out_buf.at[t, i], ref.at[to, :], out_sems.at[t, i])
            for i, ref in enumerate((a_ref, b_ref))
        ]

    def begin(copies):
        for copy in copies:
            copy.start()

    def finish(copies):
        for copy in copies:
            copy.wait()

    for t in range(1, min(3, tiles)):
        begin(fetch(t))
    for t in range(tiles):
        if t:
            finish(fetch(t))
        if t == tiles - 1:
            begin(fetch_next())
        w_ref = w_buf.at[t % 2] if t else head_ref
        for side, x_ref in enumerate((near_ref, far_ref)):
            gate = jnp.dot(x_ref[...], w_ref[0], preferred_element_type=F32)
            up = jnp.dot(x_ref[...], w_ref[1], preferred_element_type=F32)
            at = pl.ds(side * rows, rows)
            sigma = jax.nn.sigmoid(gate)
            out_buf[t, 0, :, at] = (up * sigma * (1.0 + gate * (1.0 - sigma))).T
            out_buf[t, 1, :, at] = (gate * sigma).T
        if t and t + 2 < tiles:
            begin(fetch(t + 2))
        begin(store(t))
    for t in range(tiles):
        finish(store(t))
    finish(fetch_next())


def gate_up(near, far, head, wg, wu, wd, first, count, step, grant, after):
    rows, depth = near.shape
    last = (first + count) * step == wg.shape[1]
    return pl.pallas_call(
        functools.partial(gate_up_kernel, first, step),
        in_specs=held_specs(3) + hbm_specs(3) + any_specs(after),
        out_specs=hbm_specs(2) + held_specs(1),
        out_shape=[jax.ShapeDtypeStruct((count * step, 2 * rows), F32)] * 2
        + [jax.ShapeDtypeStruct((step, depth) if last else (2, depth, step), BF16)],
        scratch_shapes=[
            pltpu.VMEM((2, 2, depth, step), BF16),
            pltpu.VMEM((count, 2, step, 2 * rows), F32),
            pltpu.SemaphoreType.DMA((2, 2)),
            pltpu.SemaphoreType.DMA((count, 2)),
            pltpu.SemaphoreType.DMA((2,)),
        ],
        compiler_params=params(grant),
        cost_estimate=cost(8 * rows * depth * count * step, 4 * depth * count * step),
        name="gate_up",
    )(near, far, head, wg, wu, wd, *after)


def back_kernel(
    step, deep, pieces, spot_ref, near_ref, far_ref, head_ref, wg_ref, wu_ref, wd_ref, *refs
):
    a_refs, b_refs = refs[:pieces], refs[pieces : 2 * pieces]
    ggs_ref, gus_ref, own_ref, sent_ref, g_ref = refs[2 * pieces : 2 * pieces + 5]
    wd_buf, w_buf, factor_buf, sems, w_sems, factor_sems = refs[2 * pieces + 5 :]
    width = wg_ref.shape[1]
    rows = near_ref.shape[1]
    tiles = wd_ref.shape[0] // step

    def fetch(t):
        at = pl.ds(pl.multiple_of(t * step, step), step)
        slot = lax.rem(t, 2)
        return pltpu.make_async_copy(wd_ref.at[at, :], wd_buf.at[slot], sems.at[slot])

    def fetch_rows(i):
        at = pl.ds(pl.multiple_of(i * deep, deep), deep)
        slot = lax.rem(i, 2)
        return [
            pltpu.make_async_copy(
                w_ref.at[at, :], w_buf.at[slot, :, pl.ds(k * width, width)], w_sems.at[slot, k]
            )
            for k, w_ref in enumerate((wg_ref, wu_ref))
        ]

    starts = [0]
    for a_ref in a_refs:
        starts.append(starts[-1] + a_ref.shape[0])

    def fetch_factors(p):
        at = pl.ds(starts[p], starts[p + 1] - starts[p])
        return [
            pltpu.make_async_copy(ref, factor_buf.at[k, at, :], factor_sems.at[k, p])
            for k, ref in enumerate((a_refs[p], b_refs[p]))
        ]

    def hidden_tile(t, wd):
        cols = pl.ds(pl.multiple_of(t * step, step), step)
        for side, dy_ref in enumerate((near_ref, far_ref)):
            hidden = jnp.dot(wd, dy_ref[...], preferred_element_type=F32)
            at = pl.ds(side * rows, rows)
            for f, gs_ref in enumerate((ggs_ref, gus_ref)):
                grad = (hidden * factor_buf[f, cols, at]).astype(BF16)
                to = pl.multiple_of(t * step + f * width, step)
                g_ref[pl.ds(to, step), at] = grad
                put_rows(spot_ref, side, grad.T, gs_ref, cols)

    blocks = wg_ref.shape[0] // deep
    for copy in fetch_factors(0):
        copy.start()
    for t in range(1, min(3, tiles)):
        fetch(jnp.int32(t)).start()
    for p in range(pieces):
        if p + 1 < pieces:
            for copy in fetch_factors(p + 1):
                copy.start()
        else:
            for i in range(2):
                for copy in fetch_rows(jnp.int32(i)):
                    copy.start()
        for copy in fetch_factors(p):
            copy.wait()

        if p == 0:
            hidden_tile(0, head_ref[...])

        @pl.loop(max(starts[p] // step, 1), starts[p + 1] // step)
        def _(t):
            fetch(t).wait()
            hidden_tile(t, wd_buf[lax.rem(t, 2)])

            @pl.when(t + 2 < tiles)
            def _():
                fetch(t + 2).start()

    @pl.loop(0, blocks)
    def _(i):
        at = pl.ds(pl.multiple_of(i * deep, deep), deep)
        slot = lax.rem(i, 2)
        for copy in fetch_rows(i):
            copy.wait()
        for side, out_ref in enumerate((own_ref, sent_ref)):
            of = pl.ds(side * rows, rows)
            total = jnp.dot(w_buf[slot], g_ref[:, of], preferred_element_type=F32)
            out_ref[:, at] = total.astype(BF16).T

        @pl.when(i + 2 < blocks)
        def _():
            for copy in fetch_rows(i + 2):
                copy.start()


def back(spot, near, far, head, wg, wu, wd, factors):
    depth, rows = near.shape
    width = wd.shape[0]
    step = tile(width, 256)
    a = [pair[0] for pair in factors]
    b = [pair[1] for pair in factors]
    return pl.pallas_call(
        functools.partial(back_kernel, step, 512, len(a)),
        in_specs=[pl.BlockSpec(memory_space=pltpu.SMEM)]
        + held_specs(3)
        + hbm_specs(3)
        + any_specs(a + b),
        out_specs=held_specs(4),
        out_shape=[jax.ShapeDtypeStruct((2 * rows, width), BF16)] * 2
        + [jax.ShapeDtypeStruct((rows, depth), BF16)] * 2,
        scratch_shapes=[
            pltpu.VMEM((2 * width, 2 * rows), BF16),
            pltpu.VMEM((2, step, depth), BF16),
            pltpu.VMEM((2, 512, 2 * width), BF16),
            pltpu.VMEM((2, width, 2 * rows), F32),
            pltpu.SemaphoreType.DMA((2,)),
            pltpu.SemaphoreType.DMA((2, 2)),
            pltpu.SemaphoreType.DMA((2, len(a))),
        ],
        compiler_params=params(26),
        cost_estimate=cost(12 * rows * depth * width, 6 * depth * width),
        name="hidden_back",
    )(spot, near, far, head, wg, wu, wd, *a, *b)


def fold_kernel(cuts, *refs):
    count = len(cuts)
    outs = refs[-count:]
    for i, (at, got_at) in enumerate(cuts):
        own_ref, near_ref, got_ref = refs[3 * i : 3 * i + 3]
        out_ref = outs[i]
        out_ref[...] = (own_ref[at, :].astype(F32) + near_ref[at, :].astype(F32)).astype(BF16)
        if got_at is not None:
            total = own_ref[got_at, :].astype(F32) + near_ref[got_at, :].astype(F32)
            out_ref[got_at, :] = (total + got_ref[...].astype(F32)).astype(BF16)


def fold(own, near, row, sends, after):
    depth = own.shape[1]
    operands, specs, shapes, cuts = [], [], [], []
    for p, at, got_at, got in sends:
        block = pl.BlockSpec((row, depth), lambda i, p=p: (p, 0))
        got = near if got is None else got
        size = got.shape[0] if got_at is not None else row
        operands += [own, near, got]
        specs += [block, block, pl.BlockSpec((size, depth), lambda i: (0, 0))]
        shapes.append(jax.ShapeDtypeStruct((at.size, depth), BF16))
        cuts.append((at, got_at))
    return pl.pallas_call(
        functools.partial(fold_kernel, cuts),
        grid=(1,),
        in_specs=specs + any_specs(after),
        out_specs=[pl.BlockSpec(shape.shape, lambda i: (0, 0)) for shape in shapes],
        out_shape=shapes,
        compiler_params=params(24),
        cost_estimate=cost(0, 16 * row * depth),
        name="fold",
    )(*operands, *after)


def last_kernel(own_ref, near_ref, r_ref, l_ref, out_ref):
    total = own_ref[...].astype(F32) + near_ref[...].astype(F32)
    out_ref[...] = (total + r_ref[...].astype(F32) + l_ref[...].astype(F32)).astype(BF16)


def last(own, near, r, l):
    block = pl.BlockSpec(r.shape, lambda i: (0, 0))
    return pl.pallas_call(
        last_kernel,
        grid=(1,),
        in_specs=[block] * 4,
        out_specs=block,
        out_shape=jax.ShapeDtypeStruct(r.shape, BF16),
        compiler_params=params(24),
        cost_estimate=cost(0, 12 * r.size),
        name="last",
    )(own, near, r, l)


def fisher_kernel(step, x_ref, gg_ref, gu_ref, *rest):
    fg_ref, fu_ref, done_ref = rest[-3:]
    done_ref[...] = jnp.zeros_like(done_ref)
    span = x_ref.shape[0] // SEQS
    seqs = [pl.ds(q * span, span) for q in range(SEQS)]
    cols = [x_ref[at, :].T for at in seqs]
    for g_ref, f_ref in ((gg_ref, fg_ref), (gu_ref, fu_ref)):
        for c in range(g_ref.shape[1] // step):
            at = pl.ds(c * step, step)
            total = None
            for q in range(SEQS):
                seq = jnp.dot(cols[q], g_ref[seqs[q], at], preferred_element_type=F32)
                total = seq * seq if total is None else total + seq * seq
            f_ref[:, at] = (total * (1.0 / SEQS)).astype(BF16)


def fisher(x, gg, gu, first, count, step, held, after):
    rows, depth = x.shape
    width = gg.shape[1]
    block = pl.BlockSpec((step, width), lambda j: (first + j, 0))
    return pl.pallas_call(
        functools.partial(fisher_kernel, tile(width, 256)),
        grid=(count,),
        in_specs=[pl.BlockSpec((rows, step), lambda j: (0, first + j))]
        + held_specs(2)
        + any_specs((*held, *after)),
        out_specs=[block, block, pl.BlockSpec((8, 128), lambda j: (0, 0))],
        out_shape=[jax.ShapeDtypeStruct((depth, width), BF16)] * 2
        + [jax.ShapeDtypeStruct((8, 128), F32)],
        input_output_aliases={3 + i: i for i in range(len(held))},
        compiler_params=params(40),
        cost_estimate=cost(4 * rows * step * count * width, 4 * step * count * width),
        name="fisher",
    )(x, gg, gu, *held, *after)


def ring_part(tokens, grad_out, wg, wu, wd):
    chips = len(CYCLE)
    far = chips // 2
    row, depth = tokens.shape
    width = wg.shape[1]
    links = [(CYCLE[i], CYCLE[(i + 1) % chips]) for i in range(chips)]
    to_right = [(2 * a + c, 2 * b + c) for a, b in links for c in range(2)]
    to_left = [(b, a) for a, b in to_right]
    across = [(2 * i + c, 2 * i + 1 - c) for i in range(chips) for c in range(2)]

    def right(value):
        return lax.ppermute(value, "hid", to_right)

    def left(value):
        return lax.ppermute(value, "hid", to_left)

    def swap(value):
        return lax.ppermute(value, "hid", across)

    cycle = jnp.array(CYCLE, jnp.int32)
    where = jnp.array([CYCLE.index(c) for c in range(chips)], jnp.int32)
    around = jnp.arange(chips, dtype=jnp.int32)
    chip = cycle[(where[lax.axis_index("hid") // 2] - around) % chips]
    span = chips // SEQS
    spot = (chip // span * 2 * span + chip % span) * row

    def both(r, l, after=(), ends=False):
        (r, l), _ = lax.optimization_barrier(((r, l), after))
        if ends:
            r, l = r[: row // 2], l[row // 2 :]
        return right(r), left(l)

    def blocks(own, rounds):
        return [own] + [r for r, _ in rounds] + [l for _, l in rounds[::-1]]

    lane = tile(width, 256)
    tiles = width // lane
    cuts = [0, 2, 5, 7]

    def piece(i, head, after):
        grant = (30, 28, 26)[i]
        count = cuts[i + 1] - cuts[i]
        a, b, head = gate_up(
            near_x, far_x, head, wg, wu, wd, cuts[i], count, lane, grant, after
        )
        return (a, b), head

    own_x, own_dy, head = bring(tokens, grad_out, wg, wu, lane)
    in_x = [both(tokens, tokens)]
    in_x.append(both(*in_x[-1], (own_x, head)))
    in_dy = [both(own_dy, own_dy, in_x[0])]
    for _ in range(3, far):
        in_x.append(both(*in_x[-1]))
        in_dy.append(both(*in_dy[-1]))
    in_x.append(both(*in_x[-1], in_dy[0], True))
    near_x = pack(blocks(own_x, in_x), (spot, *in_dy[-1]))
    far_x = swap(near_x)

    in_dy.append(both(*in_dy[-1], in_x[-2]))
    some, head = piece(0, head, in_dy[-2])
    factors = [some]
    in_dy.append(both(*in_dy[-1], some, True))
    some, head = piece(1, head, in_dy[-2])
    factors.append(some)
    near_dy = pack_turned(blocks(own_dy, in_dy), some)
    far_dy = swap(near_dy)
    some, head = piece(2, head, (near_dy,))
    factors.append(some)
    gg, gu, own, sent = back(spot, near_dy, far_dy, head, wg, wu, wd, factors)
    x = arrange(spot, near_x, far_x, (own,))

    near = swap(sent)
    full, head, tail = pl.ds(0, row), pl.ds(0, row // 2), pl.ds(row // 2, row // 2)
    step = 256
    counts = [2, 3, 4, 4, 3]
    held, first = (), 0
    r = l = None
    ready = ()
    for k in range(far, 0, -1):
        *held, done = fisher(x, gg, gu, first, counts[far - k], step, held, ready)
        first += counts[far - k]
        if k == far:
            sends = [(far, head, None, None), (far, tail, None, None)]
        elif k == far - 1:
            sends = [(chips - k, full, head, r), (k, full, tail, l)]
        else:
            sends = [(chips - k, full, full, r), (k, full, full, l)]
        ready = fold(own, near, row, sends, (done,))
        r, l = right(ready[0]), left(ready[1])
    fg, fu, _ = fisher(x, gg, gu, first, counts[far], step, held, ready)
    mine = last(own, near, r, l)
    return fg, fu, mine


def plain_forward_kernel(x_ref, wg_ref, wu_ref, gate_ref, up_ref):
    x = x_ref[...]
    gate_ref[...] = jnp.dot(x, wg_ref[...], preferred_element_type=jnp.float32)
    up_ref[...] = jnp.dot(x, wu_ref[...], preferred_element_type=jnp.float32)


def plain_forward(x, wg, wu):
    rows, depth = x.shape
    width = wg.shape[1]
    step = tile(width, 256)
    return pl.pallas_call(
        plain_forward_kernel,
        grid=(width // step,),
        in_specs=[
            pl.BlockSpec((rows, depth), lambda j: (0, 0)),
            pl.BlockSpec((depth, step), lambda j: (0, j)),
            pl.BlockSpec((depth, step), lambda j: (0, j)),
        ],
        out_specs=[pl.BlockSpec((rows, step), lambda j: (0, j))] * 2,
        out_shape=[jax.ShapeDtypeStruct((rows, width), jnp.float32)] * 2,
        compiler_params=params(40),
        cost_estimate=cost(4 * rows * depth * width, 4 * depth * width),
        name="gate_up",
    )(x, wg, wu)


def plain_back_kernel(parts, dy_ref, wd_ref, gate_ref, up_ref, gg_ref, gu_ref):
    rows = dy_ref.shape[0] // parts
    for p in range(parts):
        at = pl.ds(p * rows, rows)
        hidden = lax.dot_general(dy_ref[at, :], wd_ref[...], NT, preferred_element_type=jnp.float32)
        gate = gate_ref[at, :]
        sigma = jax.nn.sigmoid(gate)
        both = hidden * sigma
        gg_ref[at, :] = (both * up_ref[at, :] * (1.0 + gate * (1.0 - sigma))).astype(jnp.bfloat16)
        gu_ref[at, :] = (both * gate).astype(jnp.bfloat16)


def plain_back(dy, wd, gate, up):
    rows, depth = dy.shape
    width = wd.shape[0]
    step = tile(width, 256)
    column = pl.BlockSpec((rows, step), lambda j: (0, j))
    return pl.pallas_call(
        functools.partial(plain_back_kernel, 2),
        grid=(width // step,),
        in_specs=[
            pl.BlockSpec((rows, depth), lambda j: (0, 0)),
            pl.BlockSpec((step, depth), lambda j: (j, 0)),
            column,
            column,
        ],
        out_specs=[column, column],
        out_shape=[jax.ShapeDtypeStruct((rows, width), jnp.bfloat16)] * 2,
        compiler_params=params(40),
        cost_estimate=cost(2 * rows * depth * width, 2 * depth * width),
        name="hidden_back",
    )(dy, wd, gate, up)


def plain_input_kernel(gg_ref, gu_ref, wg_ref, wu_ref, out_ref):
    total = lax.dot_general(gg_ref[...], wg_ref[...], NT, preferred_element_type=jnp.float32)
    total += lax.dot_general(gu_ref[...], wu_ref[...], NT, preferred_element_type=jnp.float32)
    out_ref[...] = total.astype(jnp.bfloat16)


def plain_input_terms(gg, gu, wg, wu):
    rows, width = gg.shape
    depth = wg.shape[0]
    step = 512
    held = pl.BlockSpec((rows, width), lambda j: (0, 0))
    return pl.pallas_call(
        plain_input_kernel,
        grid=(depth // step,),
        in_specs=[
            held,
            held,
            pl.BlockSpec((step, width), lambda j: (j, 0)),
            pl.BlockSpec((step, width), lambda j: (j, 0)),
        ],
        out_specs=pl.BlockSpec((rows, step), lambda j: (0, j)),
        out_shape=jax.ShapeDtypeStruct((rows, depth), jnp.bfloat16),
        compiler_params=params(40),
        cost_estimate=cost(4 * rows * depth * width, 4 * depth * width),
        name="input_terms",
    )(gg, gu, wg, wu)


def plain_fisher_kernel(step, x_ref, gg_ref, gu_ref, fg_ref, fu_ref):
    half = x_ref.shape[0] // 2
    span = half // SEQS
    width = gg_ref.shape[1]

    def rows(ref, q, at):
        near = ref[pl.ds(q * span, span), at]
        far = ref[pl.ds(half + q * span, span), at]
        return jnp.concatenate([near, far], axis=0)

    xs = [rows(x_ref, q, slice(None)).T for q in range(SEQS)]
    for g_ref, f_ref in ((gg_ref, fg_ref), (gu_ref, fu_ref)):
        for c in range(width // step):
            at = pl.ds(c * step, step)
            total = None
            for q in range(SEQS):
                seq = jnp.dot(xs[q], rows(g_ref, q, at), preferred_element_type=jnp.float32)
                total = seq * seq if total is None else total + seq * seq
            f_ref[:, at] = (total * (1.0 / SEQS)).astype(jnp.bfloat16)


def plain_fisher(x, gg, gu):
    rows, depth = x.shape
    width = gg.shape[1]
    step = 512
    held = pl.BlockSpec((rows, width), lambda j: (0, 0))
    block = pl.BlockSpec((step, width), lambda j: (j, 0))
    return pl.pallas_call(
        functools.partial(plain_fisher_kernel, tile(width, 256)),
        grid=(depth // step,),
        in_specs=[pl.BlockSpec((rows, step), lambda j: (0, j)), held, held],
        out_specs=[block, block],
        out_shape=[jax.ShapeDtypeStruct((depth, width), jnp.bfloat16)] * 2,
        compiler_params=params(40),
        cost_estimate=cost(4 * rows * depth * width, 4 * depth * width),
        name="fisher",
    )(x, gg, gu)


def plain_part(size, tokens, grad_out, wg, wu, wd):
    chips = size // 2
    across = [[2 * i + c for i in range(chips)] for c in range(2)]
    pairs = [[2 * i, 2 * i + 1] for i in range(chips)]
    block, depth = tokens.shape

    def gather(rows):
        near = lax.all_gather(rows, "hid", axis=0, tiled=True, axis_index_groups=across)
        return lax.all_gather(near, "hid", axis=0, tiled=False, axis_index_groups=pairs)

    x = gather(tokens).reshape(-1, depth)
    dy = gather(grad_out).reshape(-1, depth)
    gate, up = plain_forward(x, wg, wu)
    gg, gu = plain_back(dy, wd, gate, up)
    terms = plain_input_terms(gg, gu, wg, wu).reshape(2, -1, depth)
    mine = lax.psum_scatter(
        terms, "hid", scatter_dimension=0, tiled=False, axis_index_groups=pairs
    )
    mine = lax.psum_scatter(
        mine, "hid", scatter_dimension=0, tiled=True, axis_index_groups=across
    )
    fg, fu = plain_fisher(x, gg, gu)
    return fg, fu, mine


def per_device(size, tokens, grad_out, wg, wu, wd):
    fits = tokens.shape[0] == 32 and wg.shape == (4096, 1792)
    if size == 2 * len(CYCLE) and fits:
        return ring_part(tokens, grad_out, wg, wu, wd)
    return plain_part(size, tokens, grad_out, wg, wu, wd)


def solution(mesh):
    rows = P(("adjust", "hid"), None)
    weights = P("adjust", "hid")
    return jax.shard_map(
        functools.partial(per_device, mesh.shape["hid"]),
        mesh=mesh,
        in_specs=(rows, rows, weights, weights, rows),
        out_specs=(weights, weights, rows),
        check_vma=False,
    )
```

```python
import functools

import jax
import jax.numpy as jnp
from jax import lax
from jax.experimental import pallas as pl
from jax.experimental.pallas import tpu as pltpu
from jax.sharding import PartitionSpec as P

SEQS = 2
MIB = 1 << 20
CYCLE = (0, 2, 4, 6, 7, 5, 3, 1)
NT = (((1,), (1,)), ((), ()))
BF16 = jnp.bfloat16
F32 = jnp.float32


def tile(size, want):
    return want if size % want == 0 else size


def params(mib):
    return pltpu.CompilerParams(vmem_limit_bytes=mib * MIB)


def cost(flops, read):
    return pl.CostEstimate(flops=flops, bytes_accessed=read, transcendentals=0)


def any_specs(values):
    return [pl.BlockSpec(memory_space=pl.ANY)] * len(values)


def hbm_specs(count):
    return [pl.BlockSpec(memory_space=pltpu.HBM)] * count


def held_specs(count):
    return [pl.BlockSpec(memory_space=pltpu.VMEM)] * count


def head_copies(wg_ref, wu_ref, first, step, head_ref, sems):
    cols = pl.ds(first * step, step)
    return [
        pltpu.make_async_copy(
            ref.at[:, cols], head_ref.at[:, pl.ds(i * step, step)], sems.at[i]
        )
        for i, ref in enumerate((wg_ref, wu_ref))
    ]


def bring_kernel(step, x_ref, dy_ref, wg_ref, wu_ref, x_out, dy_out, head_ref, sems):
    copies = head_copies(wg_ref, wu_ref, 0, step, head_ref, sems)
    for copy in copies:
        copy.start()
    x_out[...] = x_ref[...]
    dy_out[...] = dy_ref[...]
    for copy in copies:
        copy.wait()


def bring(x, dy, wg, wu, step):
    return pl.pallas_call(
        functools.partial(bring_kernel, step),
        in_specs=held_specs(2) + hbm_specs(2),
        out_specs=held_specs(3),
        out_shape=[jax.ShapeDtypeStruct(x.shape, BF16)] * 2
        + [jax.ShapeDtypeStruct((wg.shape[0], 2 * step), BF16)],
        scratch_shapes=[pltpu.SemaphoreType.DMA((2,))],
        compiler_params=params(46),
        cost_estimate=cost(0, 4 * wg.shape[0] * step),
        name="bring",
    )(x, dy, wg, wu)


def relay_kernel(in_ref, *rest):
    rest[-1][...] = in_ref[...]


def relay(value, after):
    return pl.pallas_call(
        relay_kernel,
        in_specs=held_specs(1) + any_specs(after),
        out_specs=pl.BlockSpec(memory_space=pltpu.VMEM),
        out_shape=jax.ShapeDtypeStruct(value.shape, value.dtype),
        compiler_params=params(4),
        cost_estimate=cost(0, 4 * value.size),
        name="relay",
    )(value, *after)


def pack_kernel(count, *refs):
    out_ref = refs[-1]
    start = 0
    for piece in refs[:count]:
        out_ref[pl.ds(start, piece.shape[0]), :] = piece[...]
        start += piece.shape[0]


def pack(pieces, after):
    depth = pieces[0].shape[1]
    rows = sum(piece.shape[0] for piece in pieces)
    whole = pl.BlockSpec(memory_space=pltpu.VMEM)
    return pl.pallas_call(
        functools.partial(pack_kernel, len(pieces)),
        in_specs=[whole] * len(pieces) + any_specs(after),
        out_specs=whole,
        out_shape=jax.ShapeDtypeStruct((rows, depth), BF16),
        compiler_params=params(8),
        cost_estimate=cost(0, 4 * rows * depth),
        name="pack",
    )(*pieces, *after)


def pack_turned_kernel(count, *refs):
    pieces, out_ref = refs[:count], refs[-1]
    step = 512
    for c in range(0, out_ref.shape[0], step):
        block = jnp.concatenate([piece[:, c : c + step] for piece in pieces], axis=0)
        out_ref[c : c + step, :] = block.T


def pack_turned(pieces, after):
    depth = pieces[0].shape[1]
    rows = sum(piece.shape[0] for piece in pieces)
    return pl.pallas_call(
        functools.partial(pack_turned_kernel, len(pieces)),
        in_specs=held_specs(len(pieces)) + any_specs(after),
        out_specs=pl.BlockSpec(memory_space=pltpu.VMEM),
        out_shape=jax.ShapeDtypeStruct((depth, rows), BF16),
        compiler_params=params(8),
        cost_estimate=cost(0, 4 * rows * depth),
        name="pack_turned",
    )(*pieces, *after)


def put_rows(spot_ref, side, value, out_ref, cols):
    chips = spot_ref.shape[0]
    row = value.shape[0] // chips
    for p in range(chips):
        start = pl.multiple_of(spot_ref[p] + side * chips // SEQS * row, row)
        out_ref[pl.ds(start, row), cols] = value[p * row : (p + 1) * row, :]


def arrange_kernel(spot_ref, near_ref, far_ref, *rest):
    for side, ref in enumerate((near_ref, far_ref)):
        put_rows(spot_ref, side, ref[...], rest[-1], slice(None))


def arrange(spot, near, far, after):
    rows, depth = near.shape
    return pl.pallas_call(
        arrange_kernel,
        in_specs=[pl.BlockSpec(memory_space=pltpu.SMEM)] + held_specs(2) + any_specs(after),
        out_specs=pl.BlockSpec(memory_space=pltpu.VMEM),
        out_shape=jax.ShapeDtypeStruct((2 * rows, depth), BF16),
        compiler_params=params(6),
        cost_estimate=cost(0, 8 * rows * depth),
        name="arrange",
    )(spot, near, far, *after)


def gate_up_kernel(first, step, near_ref, far_ref, head_ref, wg_ref, wu_ref, wd_ref, *rest):
    a_ref, b_ref, next_ref, w_buf, out_buf, sems, out_sems, next_sems = rest[-8:]
    rows = near_ref.shape[0]
    tiles = a_ref.shape[0] // step

    def fetch(t):
        slot = t % 2
        return head_copies(wg_ref, wu_ref, first + t, step, w_buf.at[slot], sems.at[slot])

    def fetch_next():
        if next_ref.shape[0] == near_ref.shape[1]:
            return head_copies(wg_ref, wu_ref, first + tiles, step, next_ref, next_sems)
        return [pltpu.make_async_copy(wd_ref.at[pl.ds(0, step), :], next_ref, next_sems.at[0])]

    def store(t):
        to = pl.ds(t * step, step)
        return [
            pltpu.make_async_copy(out_buf.at[t, i], ref.at[to, :], out_sems.at[t, i])
            for i, ref in enumerate((a_ref, b_ref))
        ]

    def begin(copies):
        for copy in copies:
            copy.start()

    def finish(copies):
        for copy in copies:
            copy.wait()

    for t in range(1, min(3, tiles)):
        begin(fetch(t))
    for t in range(tiles):
        if t:
            finish(fetch(t))
        if t == max(tiles - 2, 0):
            begin(fetch_next())
        w_ref = w_buf.at[t % 2] if t else head_ref
        for side, x_ref in enumerate((near_ref, far_ref)):
            both = jnp.dot(x_ref[...], w_ref[...], preferred_element_type=F32)
            gate, up = both[:, :step], both[:, step:]
            at = pl.ds(side * rows, rows)
            sigma = jax.nn.sigmoid(gate)
            out_buf[t, 0, :, at] = (up * sigma * (1.0 + gate * (1.0 - sigma))).T
            out_buf[t, 1, :, at] = (gate * sigma).T
        if t and t + 2 < tiles:
            begin(fetch(t + 2))
        begin(store(t))
    for t in range(tiles):
        finish(store(t))
    finish(fetch_next())


def gate_up(near, far, head, wg, wu, wd, first, count, step, grant, after):
    rows, depth = near.shape
    last = (first + count) * step == wg.shape[1]
    return pl.pallas_call(
        functools.partial(gate_up_kernel, first, step),
        in_specs=held_specs(3) + hbm_specs(3) + any_specs(after),
        out_specs=hbm_specs(2) + held_specs(1),
        out_shape=[jax.ShapeDtypeStruct((count * step, 2 * rows), F32)] * 2
        + [jax.ShapeDtypeStruct((step, depth) if last else (depth, 2 * step), BF16)],
        scratch_shapes=[
            pltpu.VMEM((2, depth, 2 * step), BF16),
            pltpu.VMEM((count, 2, step, 2 * rows), F32),
            pltpu.SemaphoreType.DMA((2, 2)),
            pltpu.SemaphoreType.DMA((count, 2)),
            pltpu.SemaphoreType.DMA((2,)),
        ],
        compiler_params=params(grant),
        cost_estimate=cost(8 * rows * depth * count * step, 4 * depth * count * step),
        name="gate_up",
    )(near, far, head, wg, wu, wd, *after)


def back_kernel(
    step, deep, pieces, spot_ref, near_ref, far_ref, head_ref, wg_ref, wu_ref, wd_ref, *refs
):
    a_refs, b_refs = refs[:pieces], refs[pieces : 2 * pieces]
    ggs_ref, gus_ref, own_ref, sent_ref, g_ref = refs[2 * pieces : 2 * pieces + 5]
    wd_buf, w_buf, factor_buf, sems, w_sems, factor_sems = refs[2 * pieces + 5 :]
    width = wg_ref.shape[1]
    rows = near_ref.shape[1]
    tiles = wd_ref.shape[0] // step

    def fetch(t):
        at = pl.ds(pl.multiple_of(t * step, step), step)
        slot = lax.rem(t, 2)
        return pltpu.make_async_copy(wd_ref.at[at, :], wd_buf.at[slot], sems.at[slot])

    def fetch_rows(i):
        at = pl.ds(pl.multiple_of(i * deep, deep), deep)
        slot = lax.rem(i, 2)
        return [
            pltpu.make_async_copy(
                w_ref.at[at, :], w_buf.at[slot, :, pl.ds(k * width, width)], w_sems.at[slot, k]
            )
            for k, w_ref in enumerate((wg_ref, wu_ref))
        ]

    starts = [0]
    for a_ref in a_refs:
        starts.append(starts[-1] + a_ref.shape[0])

    def fetch_factors(p):
        at = pl.ds(starts[p], starts[p + 1] - starts[p])
        return [
            pltpu.make_async_copy(ref, factor_buf.at[k, at, :], factor_sems.at[k, p])
            for k, ref in enumerate((a_refs[p], b_refs[p]))
        ]

    def hidden_tile(t, wd):
        cols = pl.ds(pl.multiple_of(t * step, step), step)
        for side, dy_ref in enumerate((near_ref, far_ref)):
            hidden = jnp.dot(wd, dy_ref[...], preferred_element_type=F32)
            at = pl.ds(side * rows, rows)
            for f, gs_ref in enumerate((ggs_ref, gus_ref)):
                grad = (hidden * factor_buf[f, cols, at]).astype(BF16)
                to = pl.multiple_of(t * step + f * width, step)
                g_ref[pl.ds(to, step), at] = grad
                put_rows(spot_ref, side, grad.T, gs_ref, cols)

    blocks = wg_ref.shape[0] // deep
    for copy in fetch_factors(0):
        copy.start()
    for t in range(1, min(3, tiles)):
        fetch(jnp.int32(t)).start()
    for p in range(pieces):
        if p + 1 < pieces:
            for copy in fetch_factors(p + 1):
                copy.start()
        else:
            for i in range(2):
                for copy in fetch_rows(jnp.int32(i)):
                    copy.start()
        for copy in fetch_factors(p):
            copy.wait()

        if p == 0:
            hidden_tile(0, head_ref[...])

        @pl.loop(max(starts[p] // step, 1), starts[p + 1] // step)
        def _(t):
            fetch(t).wait()
            hidden_tile(t, wd_buf[lax.rem(t, 2)])

            @pl.when(t + 2 < tiles)
            def _():
                fetch(t + 2).start()

    @pl.loop(0, blocks)
    def _(i):
        at = pl.ds(pl.multiple_of(i * deep, deep), deep)
        slot = lax.rem(i, 2)
        for copy in fetch_rows(i):
            copy.wait()
        total = jnp.dot(w_buf[slot], g_ref[...], preferred_element_type=F32)
        own_ref[:, at] = total[:, :rows].astype(BF16).T
        sent_ref[:, at] = total[:, rows:].astype(BF16).T

        @pl.when(i + 2 < blocks)
        def _():
            for copy in fetch_rows(i + 2):
                copy.start()


def back(spot, near, far, head, wg, wu, wd, factors):
    depth, rows = near.shape
    width = wd.shape[0]
    step = tile(width, 256)
    a = [pair[0] for pair in factors]
    b = [pair[1] for pair in factors]
    return pl.pallas_call(
        functools.partial(back_kernel, step, 512, len(a)),
        in_specs=[pl.BlockSpec(memory_space=pltpu.SMEM)]
        + held_specs(3)
        + hbm_specs(3)
        + any_specs(a + b),
        out_specs=held_specs(4),
        out_shape=[jax.ShapeDtypeStruct((2 * rows, width), BF16)] * 2
        + [jax.ShapeDtypeStruct((rows, depth), BF16)] * 2,
        scratch_shapes=[
            pltpu.VMEM((2 * width, 2 * rows), BF16),
            pltpu.VMEM((2, step, depth), BF16),
            pltpu.VMEM((2, 512, 2 * width), BF16),
            pltpu.VMEM((2, width, 2 * rows), F32),
            pltpu.SemaphoreType.DMA((2,)),
            pltpu.SemaphoreType.DMA((2, 2)),
            pltpu.SemaphoreType.DMA((2, len(a))),
        ],
        compiler_params=params(26),
        cost_estimate=cost(12 * rows * depth * width, 6 * depth * width),
        name="hidden_back",
    )(spot, near, far, head, wg, wu, wd, *a, *b)


def fold_kernel(cuts, *refs):
    count = len(cuts)
    outs = refs[-count:]
    for i, (at, got_at) in enumerate(cuts):
        own_ref, near_ref, got_ref = refs[3 * i : 3 * i + 3]
        out_ref = outs[i]
        out_ref[...] = (own_ref[at, :].astype(F32) + near_ref[at, :].astype(F32)).astype(BF16)
        if got_at is not None:
            total = own_ref[got_at, :].astype(F32) + near_ref[got_at, :].astype(F32)
            out_ref[got_at, :] = (total + got_ref[...].astype(F32)).astype(BF16)


def fold(own, near, row, sends, after):
    depth = own.shape[1]
    operands, specs, shapes, cuts = [], [], [], []
    for p, at, got_at, got in sends:
        block = pl.BlockSpec((row, depth), lambda i, p=p: (p, 0))
        got = near if got is None else got
        size = got.shape[0] if got_at is not None else row
        operands += [own, near, got]
        specs += [block, block, pl.BlockSpec((size, depth), lambda i: (0, 0))]
        shapes.append(jax.ShapeDtypeStruct((at.size, depth), BF16))
        cuts.append((at, got_at))
    return pl.pallas_call(
        functools.partial(fold_kernel, cuts),
        grid=(1,),
        in_specs=specs + any_specs(after),
        out_specs=[pl.BlockSpec(shape.shape, lambda i: (0, 0)) for shape in shapes],
        out_shape=shapes,
        compiler_params=params(24),
        cost_estimate=cost(0, 16 * row * depth),
        name="fold",
    )(*operands, *after)


def last_kernel(own_ref, near_ref, r_ref, l_ref, out_ref):
    total = own_ref[...].astype(F32) + near_ref[...].astype(F32)
    out_ref[...] = (total + r_ref[...].astype(F32) + l_ref[...].astype(F32)).astype(BF16)


def last(own, near, r, l):
    block = pl.BlockSpec(r.shape, lambda i: (0, 0))
    return pl.pallas_call(
        last_kernel,
        grid=(1,),
        in_specs=[block] * 4,
        out_specs=block,
        out_shape=jax.ShapeDtypeStruct(r.shape, BF16),
        compiler_params=params(24),
        cost_estimate=cost(0, 12 * r.size),
        name="last",
    )(own, near, r, l)


def fisher_kernel(step, x_ref, gg_ref, gu_ref, *rest):
    fg_ref, fu_ref, done_ref = rest[-3:]
    done_ref[...] = jnp.zeros_like(done_ref)
    span = x_ref.shape[0] // SEQS
    seqs = [pl.ds(q * span, span) for q in range(SEQS)]
    cols = [x_ref[at, :].T for at in seqs]
    for g_ref, f_ref in ((gg_ref, fg_ref), (gu_ref, fu_ref)):
        for c in range(g_ref.shape[1] // step):
            at = pl.ds(c * step, step)
            total = None
            for q in range(SEQS):
                seq = jnp.dot(cols[q], g_ref[seqs[q], at], preferred_element_type=F32)
                total = seq * seq if total is None else total + seq * seq
            f_ref[:, at] = (total * (1.0 / SEQS)).astype(BF16)


def fisher(x, gg, gu, first, count, step, held, after):
    rows, depth = x.shape
    width = gg.shape[1]
    block = pl.BlockSpec((step, width), lambda j: (first + j, 0))
    return pl.pallas_call(
        functools.partial(fisher_kernel, tile(width, 256)),
        grid=(count,),
        in_specs=[pl.BlockSpec((rows, step), lambda j: (0, first + j))]
        + held_specs(2)
        + any_specs((*held, *after)),
        out_specs=[block, block, pl.BlockSpec((8, 128), lambda j: (0, 0))],
        out_shape=[jax.ShapeDtypeStruct((depth, width), BF16)] * 2
        + [jax.ShapeDtypeStruct((8, 128), F32)],
        input_output_aliases={3 + i: i for i in range(len(held))},
        compiler_params=params(40),
        cost_estimate=cost(4 * rows * step * count * width, 4 * step * count * width),
        name="fisher",
    )(x, gg, gu, *held, *after)


def ring_part(tokens, grad_out, wg, wu, wd):
    chips = len(CYCLE)
    far = chips // 2
    row, depth = tokens.shape
    width = wg.shape[1]
    links = [(CYCLE[i], CYCLE[(i + 1) % chips]) for i in range(chips)]
    to_right = [(2 * a + c, 2 * b + c) for a, b in links for c in range(2)]
    to_left = [(b, a) for a, b in to_right]
    across = [(2 * i + c, 2 * i + 1 - c) for i in range(chips) for c in range(2)]

    def right(value):
        return lax.ppermute(value, "hid", to_right)

    def left(value):
        return lax.ppermute(value, "hid", to_left)

    def swap(value):
        return lax.ppermute(value, "hid", across)

    cycle = jnp.array(CYCLE, jnp.int32)
    where = jnp.array([CYCLE.index(c) for c in range(chips)], jnp.int32)
    around = jnp.arange(chips, dtype=jnp.int32)
    chip = cycle[(where[lax.axis_index("hid") // 2] - around) % chips]
    span = chips // SEQS
    spot = (chip // span * 2 * span + chip % span) * row

    def both(r, l, after=(), ends=False):
        (r, l), _ = lax.optimization_barrier(((r, l), after))
        if ends:
            r, l = r[: row // 2], l[row // 2 :]
        return right(r), left(l)

    def blocks(own, rounds):
        return [own] + [r for r, _ in rounds] + [l for _, l in rounds[::-1]]

    lane = tile(width, 256)
    tiles = width // lane
    cuts = [0, 2, 5, 7]

    def piece(i, head, after):
        grant = (30, 28, 26)[i]
        count = cuts[i + 1] - cuts[i]
        a, b, head = gate_up(
            near_x, far_x, head, wg, wu, wd, cuts[i], count, lane, grant, after
        )
        return (a, b), head

    own_x, own_dy, head = bring(tokens, grad_out, wg, wu, lane)
    in_x = [both(tokens, tokens)]
    in_x.append(both(*in_x[-1], (own_x, head)))
    in_dy = [both(own_dy, own_dy, in_x[0])]
    for _ in range(3, far):
        in_x.append(both(*in_x[-1]))
        in_dy.append(both(*in_dy[-1]))
    in_x.append(both(*in_x[-1], in_dy[0], True))
    near_x = pack(blocks(own_x, in_x), (spot, *in_dy[-1]))
    far_x = swap(near_x)

    in_dy.append(both(*in_dy[-1], in_x[-2]))
    some, head = piece(0, head, in_dy[-2])
    factors = [some]
    in_dy.append(both(*in_dy[-1], some, True))
    some, head = piece(1, head, in_dy[-2])
    factors.append(some)
    near_dy = pack_turned(blocks(own_dy, in_dy), some)
    far_dy = swap(near_dy)
    some, head = piece(2, head, (near_dy,))
    factors.append(some)
    gg, gu, own, sent = back(spot, near_dy, far_dy, head, wg, wu, wd, factors)
    x = arrange(spot, near_x, far_x, (own,))

    near = swap(sent)
    full, head, tail = pl.ds(0, row), pl.ds(0, row // 2), pl.ds(row // 2, row // 2)
    step = 256
    counts = [2, 3, 4, 4, 3]
    held, first = (), 0
    r = l = None
    ready = ()
    for k in range(far, 0, -1):
        *held, done = fisher(x, gg, gu, first, counts[far - k], step, held, ready)
        first += counts[far - k]
        if k == far:
            sends = [(far, head, None, None), (far, tail, None, None)]
        elif k == far - 1:
            sends = [(chips - k, full, head, r), (k, full, tail, l)]
        else:
            sends = [(chips - k, full, full, r), (k, full, full, l)]
        ready = fold(own, near, row, sends, (done,))
        r, l = right(ready[0]), left(ready[1])
    fg, fu, _ = fisher(x, gg, gu, first, counts[far], step, held, ready)
    mine = last(own, near, r, l)
    return fg, fu, mine


def plain_forward_kernel(x_ref, wg_ref, wu_ref, gate_ref, up_ref):
    x = x_ref[...]
    gate_ref[...] = jnp.dot(x, wg_ref[...], preferred_element_type=jnp.float32)
    up_ref[...] = jnp.dot(x, wu_ref[...], preferred_element_type=jnp.float32)


def plain_forward(x, wg, wu):
    rows, depth = x.shape
    width = wg.shape[1]
    step = tile(width, 256)
    return pl.pallas_call(
        plain_forward_kernel,
        grid=(width // step,),
        in_specs=[
            pl.BlockSpec((rows, depth), lambda j: (0, 0)),
            pl.BlockSpec((depth, step), lambda j: (0, j)),
            pl.BlockSpec((depth, step), lambda j: (0, j)),
        ],
        out_specs=[pl.BlockSpec((rows, step), lambda j: (0, j))] * 2,
        out_shape=[jax.ShapeDtypeStruct((rows, width), jnp.float32)] * 2,
        compiler_params=params(40),
        cost_estimate=cost(4 * rows * depth * width, 4 * depth * width),
        name="gate_up",
    )(x, wg, wu)


def plain_back_kernel(parts, dy_ref, wd_ref, gate_ref, up_ref, gg_ref, gu_ref):
    rows = dy_ref.shape[0] // parts
    for p in range(parts):
        at = pl.ds(p * rows, rows)
        hidden = lax.dot_general(dy_ref[at, :], wd_ref[...], NT, preferred_element_type=jnp.float32)
        gate = gate_ref[at, :]
        sigma = jax.nn.sigmoid(gate)
        both = hidden * sigma
        gg_ref[at, :] = (both * up_ref[at, :] * (1.0 + gate * (1.0 - sigma))).astype(jnp.bfloat16)
        gu_ref[at, :] = (both * gate).astype(jnp.bfloat16)


def plain_back(dy, wd, gate, up):
    rows, depth = dy.shape
    width = wd.shape[0]
    step = tile(width, 256)
    column = pl.BlockSpec((rows, step), lambda j: (0, j))
    return pl.pallas_call(
        functools.partial(plain_back_kernel, 2),
        grid=(width // step,),
        in_specs=[
            pl.BlockSpec((rows, depth), lambda j: (0, 0)),
            pl.BlockSpec((step, depth), lambda j: (j, 0)),
            column,
            column,
        ],
        out_specs=[column, column],
        out_shape=[jax.ShapeDtypeStruct((rows, width), jnp.bfloat16)] * 2,
        compiler_params=params(40),
        cost_estimate=cost(2 * rows * depth * width, 2 * depth * width),
        name="hidden_back",
    )(dy, wd, gate, up)


def plain_input_kernel(gg_ref, gu_ref, wg_ref, wu_ref, out_ref):
    total = lax.dot_general(gg_ref[...], wg_ref[...], NT, preferred_element_type=jnp.float32)
    total += lax.dot_general(gu_ref[...], wu_ref[...], NT, preferred_element_type=jnp.float32)
    out_ref[...] = total.astype(jnp.bfloat16)


def plain_input_terms(gg, gu, wg, wu):
    rows, width = gg.shape
    depth = wg.shape[0]
    step = 512
    held = pl.BlockSpec((rows, width), lambda j: (0, 0))
    return pl.pallas_call(
        plain_input_kernel,
        grid=(depth // step,),
        in_specs=[
            held,
            held,
            pl.BlockSpec((step, width), lambda j: (j, 0)),
            pl.BlockSpec((step, width), lambda j: (j, 0)),
        ],
        out_specs=pl.BlockSpec((rows, step), lambda j: (0, j)),
        out_shape=jax.ShapeDtypeStruct((rows, depth), jnp.bfloat16),
        compiler_params=params(40),
        cost_estimate=cost(4 * rows * depth * width, 4 * depth * width),
        name="input_terms",
    )(gg, gu, wg, wu)


def plain_fisher_kernel(step, x_ref, gg_ref, gu_ref, fg_ref, fu_ref):
    half = x_ref.shape[0] // 2
    span = half // SEQS
    width = gg_ref.shape[1]

    def rows(ref, q, at):
        near = ref[pl.ds(q * span, span), at]
        far = ref[pl.ds(half + q * span, span), at]
        return jnp.concatenate([near, far], axis=0)

    xs = [rows(x_ref, q, slice(None)).T for q in range(SEQS)]
    for g_ref, f_ref in ((gg_ref, fg_ref), (gu_ref, fu_ref)):
        for c in range(width // step):
            at = pl.ds(c * step, step)
            total = None
            for q in range(SEQS):
                seq = jnp.dot(xs[q], rows(g_ref, q, at), preferred_element_type=jnp.float32)
                total = seq * seq if total is None else total + seq * seq
            f_ref[:, at] = (total * (1.0 / SEQS)).astype(jnp.bfloat16)


def plain_fisher(x, gg, gu):
    rows, depth = x.shape
    width = gg.shape[1]
    step = 512
    held = pl.BlockSpec((rows, width), lambda j: (0, 0))
    block = pl.BlockSpec((step, width), lambda j: (j, 0))
    return pl.pallas_call(
        functools.partial(plain_fisher_kernel, tile(width, 256)),
        grid=(depth // step,),
        in_specs=[pl.BlockSpec((rows, step), lambda j: (0, j)), held, held],
        out_specs=[block, block],
        out_shape=[jax.ShapeDtypeStruct((depth, width), jnp.bfloat16)] * 2,
        compiler_params=params(40),
        cost_estimate=cost(4 * rows * depth * width, 4 * depth * width),
        name="fisher",
    )(x, gg, gu)


def plain_part(size, tokens, grad_out, wg, wu, wd):
    chips = size // 2
    across = [[2 * i + c for i in range(chips)] for c in range(2)]
    pairs = [[2 * i, 2 * i + 1] for i in range(chips)]
    block, depth = tokens.shape

    def gather(rows):
        near = lax.all_gather(rows, "hid", axis=0, tiled=True, axis_index_groups=across)
        return lax.all_gather(near, "hid", axis=0, tiled=False, axis_index_groups=pairs)

    x = gather(tokens).reshape(-1, depth)
    dy = gather(grad_out).reshape(-1, depth)
    gate, up = plain_forward(x, wg, wu)
    gg, gu = plain_back(dy, wd, gate, up)
    terms = plain_input_terms(gg, gu, wg, wu).reshape(2, -1, depth)
    mine = lax.psum_scatter(
        terms, "hid", scatter_dimension=0, tiled=False, axis_index_groups=pairs
    )
    mine = lax.psum_scatter(
        mine, "hid", scatter_dimension=0, tiled=True, axis_index_groups=across
    )
    fg, fu = plain_fisher(x, gg, gu)
    return fg, fu, mine


def per_device(size, tokens, grad_out, wg, wu, wd):
    fits = tokens.shape[0] == 32 and wg.shape == (4096, 1792)
    if size == 2 * len(CYCLE) and fits:
        return ring_part(tokens, grad_out, wg, wu, wd)
    return plain_part(size, tokens, grad_out, wg, wu, wd)


def solution(mesh):
    rows = P(("adjust", "hid"), None)
    weights = P("adjust", "hid")
    return jax.shard_map(
        functools.partial(per_device, mesh.shape["hid"]),
        mesh=mesh,
        in_specs=(rows, rows, weights, weights, rows),
        out_specs=(weights, weights, rows),
        check_vma=False,
    )
```

```python
import functools

import jax
import jax.numpy as jnp
from jax import lax
from jax.experimental import pallas as pl
from jax.experimental.pallas import tpu as pltpu
from jax.sharding import PartitionSpec as P

SEQS = 2
MIB = 1 << 20
CYCLE = (0, 2, 4, 6, 7, 5, 3, 1)
NT = (((1,), (1,)), ((), ()))
BF16 = jnp.bfloat16
F32 = jnp.float32


def tile(size, want):
    return want if size % want == 0 else size


def params(mib):
    return pltpu.CompilerParams(vmem_limit_bytes=mib * MIB)


def cost(flops, read):
    return pl.CostEstimate(flops=flops, bytes_accessed=read, transcendentals=0)


def any_specs(values):
    return [pl.BlockSpec(memory_space=pl.ANY)] * len(values)


def hbm_specs(count):
    return [pl.BlockSpec(memory_space=pltpu.HBM)] * count


def held_specs(count):
    return [pl.BlockSpec(memory_space=pltpu.VMEM)] * count


def head_copies(wg_ref, wu_ref, first, step, head_ref, sems):
    cols = pl.ds(first * step, step)
    return [
        pltpu.make_async_copy(ref.at[:, cols], head_ref.at[i], sems.at[i])
        for i, ref in enumerate((wg_ref, wu_ref))
    ]


def bring_kernel(step, x_ref, dy_ref, wg_ref, wu_ref, x_out, dy_out, head_ref, sems):
    copies = head_copies(wg_ref, wu_ref, 0, step, head_ref, sems)
    for copy in copies:
        copy.start()
    x_out[...] = x_ref[...]
    dy_out[...] = dy_ref[...]
    for copy in copies:
        copy.wait()


def bring(x, dy, wg, wu, step):
    return pl.pallas_call(
        functools.partial(bring_kernel, step),
        in_specs=held_specs(2) + hbm_specs(2),
        out_specs=held_specs(3),
        out_shape=[jax.ShapeDtypeStruct(x.shape, BF16)] * 2
        + [jax.ShapeDtypeStruct((2, wg.shape[0], step), BF16)],
        scratch_shapes=[pltpu.SemaphoreType.DMA((2,))],
        compiler_params=params(46),
        cost_estimate=cost(0, 4 * wg.shape[0] * step),
        name="bring",
    )(x, dy, wg, wu)


def relay_kernel(in_ref, *rest):
    rest[-1][...] = in_ref[...]


def relay(value, after):
    return pl.pallas_call(
        relay_kernel,
        in_specs=held_specs(1) + any_specs(after),
        out_specs=pl.BlockSpec(memory_space=pltpu.VMEM),
        out_shape=jax.ShapeDtypeStruct(value.shape, value.dtype),
        compiler_params=params(4),
        cost_estimate=cost(0, 4 * value.size),
        name="relay",
    )(value, *after)


def pack_kernel(count, *refs):
    out_ref = refs[-1]
    start = 0
    for piece in refs[:count]:
        out_ref[pl.ds(start, piece.shape[0]), :] = piece[...]
        start += piece.shape[0]


def pack(pieces, after):
    depth = pieces[0].shape[1]
    rows = sum(piece.shape[0] for piece in pieces)
    whole = pl.BlockSpec(memory_space=pltpu.VMEM)
    return pl.pallas_call(
        functools.partial(pack_kernel, len(pieces)),
        in_specs=[whole] * len(pieces) + any_specs(after),
        out_specs=whole,
        out_shape=jax.ShapeDtypeStruct((rows, depth), BF16),
        compiler_params=params(8),
        cost_estimate=cost(0, 4 * rows * depth),
        name="pack",
    )(*pieces, *after)


def pack_turned_kernel(count, *refs):
    pieces, out_ref = refs[:count], refs[-1]
    step = 512
    for c in range(0, out_ref.shape[0], step):
        block = jnp.concatenate([piece[:, c : c + step] for piece in pieces], axis=0)
        out_ref[c : c + step, :] = block.T


def pack_turned(pieces, after):
    depth = pieces[0].shape[1]
    rows = sum(piece.shape[0] for piece in pieces)
    return pl.pallas_call(
        functools.partial(pack_turned_kernel, len(pieces)),
        in_specs=held_specs(len(pieces)) + any_specs(after),
        out_specs=pl.BlockSpec(memory_space=pltpu.VMEM),
        out_shape=jax.ShapeDtypeStruct((depth, rows), BF16),
        compiler_params=params(8),
        cost_estimate=cost(0, 4 * rows * depth),
        name="pack_turned",
    )(*pieces, *after)


def put_rows(spot_ref, side, value, out_ref, cols):
    chips = spot_ref.shape[0]
    row = value.shape[0] // chips
    for p in range(chips):
        start = pl.multiple_of(spot_ref[p] + side * chips // SEQS * row, row)
        out_ref[pl.ds(start, row), cols] = value[p * row : (p + 1) * row, :]


def arrange_kernel(spot_ref, near_ref, far_ref, *rest):
    for side, ref in enumerate((near_ref, far_ref)):
        put_rows(spot_ref, side, ref[...], rest[-1], slice(None))


def arrange(spot, near, far, after):
    rows, depth = near.shape
    return pl.pallas_call(
        arrange_kernel,
        in_specs=[pl.BlockSpec(memory_space=pltpu.SMEM)] + held_specs(2) + any_specs(after),
        out_specs=pl.BlockSpec(memory_space=pltpu.VMEM),
        out_shape=jax.ShapeDtypeStruct((2 * rows, depth), BF16),
        compiler_params=params(6),
        cost_estimate=cost(0, 8 * rows * depth),
        name="arrange",
    )(spot, near, far, *after)


def gate_up_kernel(first, step, near_ref, far_ref, head_ref, wg_ref, wu_ref, wd_ref, *rest):
    a_ref, b_ref, next_ref, w_buf, out_buf, sems, out_sems, next_sems = rest[-8:]
    rows = near_ref.shape[0]
    tiles = a_ref.shape[0] // step

    def fetch(t):
        slot = t % 2
        return head_copies(wg_ref, wu_ref, first + t, step, w_buf.at[slot], sems.at[slot])

    def fetch_next():
        if next_ref.shape[0] == 2:
            return head_copies(wg_ref, wu_ref, first + tiles, step, next_ref, next_sems)
        return [pltpu.make_async_copy(wd_ref.at[pl.ds(0, step), :], next_ref, next_sems.at[0])]

    def store(t):
        to = pl.ds(t * step, step)
        return [
            pltpu.make_async_copy(out_buf.at[t, i], ref.at[to, :], out_sems.at[t, i])
            for i, ref in enumerate((a_ref, b_ref))
        ]

    def begin(copies):
        for copy in copies:
            copy.start()

    def finish(copies):
        for copy in copies:
            copy.wait()

    for t in range(1, min(3, tiles)):
        begin(fetch(t))
    for t in range(tiles):
        if t:
            finish(fetch(t))
        if t == (max(tiles - 2, 0) if next_ref.shape[0] == 2 else tiles - 1):
            begin(fetch_next())
        w_ref = w_buf.at[t % 2] if t else head_ref
        for side, x_ref in enumerate((near_ref, far_ref)):
            gate = jnp.dot(x_ref[...], w_ref[0], preferred_element_type=F32)
            up = jnp.dot(x_ref[...], w_ref[1], preferred_element_type=F32)
            at = pl.ds(side * rows, rows)
            sigma = jax.nn.sigmoid(gate)
            out_buf[t, 0, :, at] = (up * sigma * (1.0 + gate * (1.0 - sigma))).T
            out_buf[t, 1, :, at] = (gate * sigma).T
        if t and t + 2 < tiles:
            begin(fetch(t + 2))
        begin(store(t))
    for t in range(tiles):
        finish(store(t))
    finish(fetch_next())


def gate_up(near, far, head, wg, wu, wd, first, count, step, grant, after):
    rows, depth = near.shape
    last = (first + count) * step == wg.shape[1]
    return pl.pallas_call(
        functools.partial(gate_up_kernel, first, step),
        in_specs=held_specs(3) + hbm_specs(3) + any_specs(after),
        out_specs=hbm_specs(2) + held_specs(1),
        out_shape=[jax.ShapeDtypeStruct((count * step, 2 * rows), F32)] * 2
        + [jax.ShapeDtypeStruct((step, depth) if last else (2, depth, step), BF16)],
        scratch_shapes=[
            pltpu.VMEM((2, 2, depth, step), BF16),
            pltpu.VMEM((count, 2, step, 2 * rows), F32),
            pltpu.SemaphoreType.DMA((2, 2)),
            pltpu.SemaphoreType.DMA((count, 2)),
            pltpu.SemaphoreType.DMA((2,)),
        ],
        compiler_params=params(grant),
        cost_estimate=cost(8 * rows * depth * count * step, 4 * depth * count * step),
        name="gate_up",
    )(near, far, head, wg, wu, wd, *after)


def back_kernel(
    step, deep, pieces, spot_ref, near_ref, far_ref, head_ref, wg_ref, wu_ref, wd_ref, *refs
):
    a_refs, b_refs = refs[:pieces], refs[pieces : 2 * pieces]
    ggs_ref, gus_ref, own_ref, sent_ref, g_ref = refs[2 * pieces : 2 * pieces + 5]
    wd_buf, w_buf, factor_buf, sems, w_sems, factor_sems = refs[2 * pieces + 5 :]
    width = wg_ref.shape[1]
    rows = near_ref.shape[1]
    tiles = wd_ref.shape[0] // step

    def fetch(t):
        at = pl.ds(pl.multiple_of(t * step, step), step)
        slot = lax.rem(t, 2)
        return pltpu.make_async_copy(wd_ref.at[at, :], wd_buf.at[slot], sems.at[slot])

    def fetch_rows(i):
        at = pl.ds(pl.multiple_of(i * deep, deep), deep)
        slot = lax.rem(i, 2)
        return [
            pltpu.make_async_copy(
                w_ref.at[at, :], w_buf.at[slot, :, pl.ds(k * width, width)], w_sems.at[slot, k]
            )
            for k, w_ref in enumerate((wg_ref, wu_ref))
        ]

    starts = [0]
    for a_ref in a_refs:
        starts.append(starts[-1] + a_ref.shape[0])

    def fetch_factors(p):
        at = pl.ds(starts[p], starts[p + 1] - starts[p])
        return [
            pltpu.make_async_copy(ref, factor_buf.at[k, at, :], factor_sems.at[k, p])
            for k, ref in enumerate((a_refs[p], b_refs[p]))
        ]

    def hidden_tile(t, wd):
        cols = pl.ds(pl.multiple_of(t * step, step), step)
        for side, dy_ref in enumerate((near_ref, far_ref)):
            hidden = jnp.dot(wd, dy_ref[...], preferred_element_type=F32)
            at = pl.ds(side * rows, rows)
            for f, gs_ref in enumerate((ggs_ref, gus_ref)):
                grad = (hidden * factor_buf[f, cols, at]).astype(BF16)
                to = pl.multiple_of(t * step + f * width, step)
                g_ref[pl.ds(to, step), at] = grad
                put_rows(spot_ref, side, grad.T, gs_ref, cols)

    blocks = wg_ref.shape[0] // deep
    for copy in fetch_factors(0):
        copy.start()
    for t in range(1, min(3, tiles)):
        fetch(jnp.int32(t)).start()
    for p in range(pieces):
        if p + 1 < pieces:
            for copy in fetch_factors(p + 1):
                copy.start()
        else:
            for i in range(2):
                for copy in fetch_rows(jnp.int32(i)):
                    copy.start()
        for copy in fetch_factors(p):
            copy.wait()

        if p == 0:
            hidden_tile(0, head_ref[...])

        @pl.loop(max(starts[p] // step, 1), starts[p + 1] // step)
        def _(t):
            fetch(t).wait()
            hidden_tile(t, wd_buf[lax.rem(t, 2)])

            @pl.when(t + 2 < tiles)
            def _():
                fetch(t + 2).start()

    @pl.loop(0, blocks)
    def _(i):
        at = pl.ds(pl.multiple_of(i * deep, deep), deep)
        slot = lax.rem(i, 2)
        for copy in fetch_rows(i):
            copy.wait()
        for side, out_ref in enumerate((own_ref, sent_ref)):
            of = pl.ds(side * rows, rows)
            total = jnp.dot(w_buf[slot], g_ref[:, of], preferred_element_type=F32)
            out_ref[:, at] = total.astype(BF16).T

        @pl.when(i + 2 < blocks)
        def _():
            for copy in fetch_rows(i + 2):
                copy.start()


def back(spot, near, far, head, wg, wu, wd, factors):
    depth, rows = near.shape
    width = wd.shape[0]
    step = tile(width, 256)
    a = [pair[0] for pair in factors]
    b = [pair[1] for pair in factors]
    return pl.pallas_call(
        functools.partial(back_kernel, step, 512, len(a)),
        in_specs=[pl.BlockSpec(memory_space=pltpu.SMEM)]
        + held_specs(3)
        + hbm_specs(3)
        + any_specs(a + b),
        out_specs=held_specs(4),
        out_shape=[jax.ShapeDtypeStruct((2 * rows, width), BF16)] * 2
        + [jax.ShapeDtypeStruct((rows, depth), BF16)] * 2,
        scratch_shapes=[
            pltpu.VMEM((2 * width, 2 * rows), BF16),
            pltpu.VMEM((2, step, depth), BF16),
            pltpu.VMEM((2, 512, 2 * width), BF16),
            pltpu.VMEM((2, width, 2 * rows), F32),
            pltpu.SemaphoreType.DMA((2,)),
            pltpu.SemaphoreType.DMA((2, 2)),
            pltpu.SemaphoreType.DMA((2, len(a))),
        ],
        compiler_params=params(26),
        cost_estimate=cost(12 * rows * depth * width, 6 * depth * width),
        name="hidden_back",
    )(spot, near, far, head, wg, wu, wd, *a, *b)


def fold_kernel(cuts, *refs):
    count = len(cuts)
    outs = refs[-count:]
    for i, (at, got_at) in enumerate(cuts):
        own_ref, near_ref, got_ref = refs[3 * i : 3 * i + 3]
        out_ref = outs[i]
        out_ref[...] = (own_ref[at, :].astype(F32) + near_ref[at, :].astype(F32)).astype(BF16)
        if got_at is not None:
            total = own_ref[got_at, :].astype(F32) + near_ref[got_at, :].astype(F32)
            out_ref[got_at, :] = (total + got_ref[...].astype(F32)).astype(BF16)


def fold(own, near, row, sends, after):
    depth = own.shape[1]
    operands, specs, shapes, cuts = [], [], [], []
    for p, at, got_at, got in sends:
        block = pl.BlockSpec((row, depth), lambda i, p=p: (p, 0))
        got = near if got is None else got
        size = got.shape[0] if got_at is not None else row
        operands += [own, near, got]
        specs += [block, block, pl.BlockSpec((size, depth), lambda i: (0, 0))]
        shapes.append(jax.ShapeDtypeStruct((at.size, depth), BF16))
        cuts.append((at, got_at))
    return pl.pallas_call(
        functools.partial(fold_kernel, cuts),
        grid=(1,),
        in_specs=specs + any_specs(after),
        out_specs=[pl.BlockSpec(shape.shape, lambda i: (0, 0)) for shape in shapes],
        out_shape=shapes,
        compiler_params=params(24),
        cost_estimate=cost(0, 16 * row * depth),
        name="fold",
    )(*operands, *after)


def last_kernel(own_ref, near_ref, r_ref, l_ref, out_ref):
    total = own_ref[...].astype(F32) + near_ref[...].astype(F32)
    out_ref[...] = (total + r_ref[...].astype(F32) + l_ref[...].astype(F32)).astype(BF16)


def last(own, near, r, l):
    block = pl.BlockSpec(r.shape, lambda i: (0, 0))
    return pl.pallas_call(
        last_kernel,
        grid=(1,),
        in_specs=[block] * 4,
        out_specs=block,
        out_shape=jax.ShapeDtypeStruct(r.shape, BF16),
        compiler_params=params(24),
        cost_estimate=cost(0, 12 * r.size),
        name="last",
    )(own, near, r, l)


def fisher_kernel(step, x_ref, gg_ref, gu_ref, *rest):
    fg_ref, fu_ref, done_ref = rest[-3:]
    done_ref[...] = jnp.zeros_like(done_ref)
    span = x_ref.shape[0] // SEQS
    seqs = [pl.ds(q * span, span) for q in range(SEQS)]
    cols = [x_ref[at, :].T for at in seqs]
    for g_ref, f_ref in ((gg_ref, fg_ref), (gu_ref, fu_ref)):
        for c in range(g_ref.shape[1] // step):
            at = pl.ds(c * step, step)
            total = None
            for q in range(SEQS):
                seq = jnp.dot(cols[q], g_ref[seqs[q], at], preferred_element_type=F32)
                total = seq * seq if total is None else total + seq * seq
            f_ref[:, at] = (total * (1.0 / SEQS)).astype(BF16)


def fisher(x, gg, gu, first, count, step, held, after):
    rows, depth = x.shape
    width = gg.shape[1]
    block = pl.BlockSpec((step, width), lambda j: (first + j, 0))
    return pl.pallas_call(
        functools.partial(fisher_kernel, tile(width, 256)),
        grid=(count,),
        in_specs=[pl.BlockSpec((rows, step), lambda j: (0, first + j))]
        + held_specs(2)
        + any_specs((*held, *after)),
        out_specs=[block, block, pl.BlockSpec((8, 128), lambda j: (0, 0))],
        out_shape=[jax.ShapeDtypeStruct((depth, width), BF16)] * 2
        + [jax.ShapeDtypeStruct((8, 128), F32)],
        input_output_aliases={3 + i: i for i in range(len(held))},
        compiler_params=params(40),
        cost_estimate=cost(4 * rows * step * count * width, 4 * step * count * width),
        name="fisher",
    )(x, gg, gu, *held, *after)


def ring_part(tokens, grad_out, wg, wu, wd):
    chips = len(CYCLE)
    far = chips // 2
    row, depth = tokens.shape
    width = wg.shape[1]
    links = [(CYCLE[i], CYCLE[(i + 1) % chips]) for i in range(chips)]
    to_right = [(2 * a + c, 2 * b + c) for a, b in links for c in range(2)]
    to_left = [(b, a) for a, b in to_right]
    across = [(2 * i + c, 2 * i + 1 - c) for i in range(chips) for c in range(2)]

    def right(value):
        return lax.ppermute(value, "hid", to_right)

    def left(value):
        return lax.ppermute(value, "hid", to_left)

    def swap(value):
        return lax.ppermute(value, "hid", across)

    cycle = jnp.array(CYCLE, jnp.int32)
    where = jnp.array([CYCLE.index(c) for c in range(chips)], jnp.int32)
    around = jnp.arange(chips, dtype=jnp.int32)
    chip = cycle[(where[lax.axis_index("hid") // 2] - around) % chips]
    span = chips // SEQS
    spot = (chip // span * 2 * span + chip % span) * row

    def both(r, l, after=(), ends=False):
        (r, l), _ = lax.optimization_barrier(((r, l), after))
        if ends:
            r, l = r[: row // 2], l[row // 2 :]
        return right(r), left(l)

    def blocks(own, rounds):
        return [own] + [r for r, _ in rounds] + [l for _, l in rounds[::-1]]

    lane = tile(width, 256)
    tiles = width // lane
    cuts = [0, 2, 5, 7]

    def piece(i, head, after):
        grant = (30, 26, 26)[i]
        count = cuts[i + 1] - cuts[i]
        a, b, head = gate_up(
            near_x, far_x, head, wg, wu, wd, cuts[i], count, lane, grant, after
        )
        return (a, b), head

    own_x, own_dy, head = bring(tokens, grad_out, wg, wu, lane)
    in_x = [both(tokens, tokens)]
    in_x.append(both(*in_x[-1], (own_x, head)))
    in_dy = [both(own_dy, own_dy, in_x[0])]
    for _ in range(3, far):
        in_x.append(both(*in_x[-1]))
        in_dy.append(both(*in_dy[-1]))
    in_x.append(both(*in_x[-1], in_dy[0], True))
    near_x = pack(blocks(own_x, in_x), (spot, *in_dy[-1]))
    far_x = swap(near_x)

    in_dy.append(both(*in_dy[-1], in_x[-2]))
    some, head = piece(0, head, in_dy[-2])
    factors = [some]
    in_dy.append(both(*in_dy[-1], some, True))
    some, head = piece(1, head, in_dy[-2])
    factors.append(some)
    near_dy = pack_turned(blocks(own_dy, in_dy), some)
    far_dy = swap(near_dy)
    some, head = piece(2, head, (near_dy,))
    factors.append(some)
    gg, gu, own, sent = back(spot, near_dy, far_dy, head, wg, wu, wd, factors)
    x = arrange(spot, near_x, far_x, (own,))

    near = swap(sent)
    full, head, tail = pl.ds(0, row), pl.ds(0, row // 2), pl.ds(row // 2, row // 2)
    step = 256
    counts = [2, 3, 4, 4, 3]
    held, first = (), 0
    r = l = None
    ready = ()
    for k in range(far, 0, -1):
        *held, done = fisher(x, gg, gu, first, counts[far - k], step, held, ready)
        first += counts[far - k]
        if k == far:
            sends = [(far, head, None, None), (far, tail, None, None)]
        elif k == far - 1:
            sends = [(chips - k, full, head, r), (k, full, tail, l)]
        else:
            sends = [(chips - k, full, full, r), (k, full, full, l)]
        ready = fold(own, near, row, sends, (done,))
        r, l = right(ready[0]), left(ready[1])
    fg, fu, _ = fisher(x, gg, gu, first, counts[far], step, held, ready)
    mine = last(own, near, r, l)
    return fg, fu, mine


def plain_forward_kernel(x_ref, wg_ref, wu_ref, gate_ref, up_ref):
    x = x_ref[...]
    gate_ref[...] = jnp.dot(x, wg_ref[...], preferred_element_type=jnp.float32)
    up_ref[...] = jnp.dot(x, wu_ref[...], preferred_element_type=jnp.float32)


def plain_forward(x, wg, wu):
    rows, depth = x.shape
    width = wg.shape[1]
    step = tile(width, 256)
    return pl.pallas_call(
        plain_forward_kernel,
        grid=(width // step,),
        in_specs=[
            pl.BlockSpec((rows, depth), lambda j: (0, 0)),
            pl.BlockSpec((depth, step), lambda j: (0, j)),
            pl.BlockSpec((depth, step), lambda j: (0, j)),
        ],
        out_specs=[pl.BlockSpec((rows, step), lambda j: (0, j))] * 2,
        out_shape=[jax.ShapeDtypeStruct((rows, width), jnp.float32)] * 2,
        compiler_params=params(40),
        cost_estimate=cost(4 * rows * depth * width, 4 * depth * width),
        name="gate_up",
    )(x, wg, wu)


def plain_back_kernel(parts, dy_ref, wd_ref, gate_ref, up_ref, gg_ref, gu_ref):
    rows = dy_ref.shape[0] // parts
    for p in range(parts):
        at = pl.ds(p * rows, rows)
        hidden = lax.dot_general(dy_ref[at, :], wd_ref[...], NT, preferred_element_type=jnp.float32)
        gate = gate_ref[at, :]
        sigma = jax.nn.sigmoid(gate)
        both = hidden * sigma
        gg_ref[at, :] = (both * up_ref[at, :] * (1.0 + gate * (1.0 - sigma))).astype(jnp.bfloat16)
        gu_ref[at, :] = (both * gate).astype(jnp.bfloat16)


def plain_back(dy, wd, gate, up):
    rows, depth = dy.shape
    width = wd.shape[0]
    step = tile(width, 256)
    column = pl.BlockSpec((rows, step), lambda j: (0, j))
    return pl.pallas_call(
        functools.partial(plain_back_kernel, 2),
        grid=(width // step,),
        in_specs=[
            pl.BlockSpec((rows, depth), lambda j: (0, 0)),
            pl.BlockSpec((step, depth), lambda j: (j, 0)),
            column,
            column,
        ],
        out_specs=[column, column],
        out_shape=[jax.ShapeDtypeStruct((rows, width), jnp.bfloat16)] * 2,
        compiler_params=params(40),
        cost_estimate=cost(2 * rows * depth * width, 2 * depth * width),
        name="hidden_back",
    )(dy, wd, gate, up)


def plain_input_kernel(gg_ref, gu_ref, wg_ref, wu_ref, out_ref):
    total = lax.dot_general(gg_ref[...], wg_ref[...], NT, preferred_element_type=jnp.float32)
    total += lax.dot_general(gu_ref[...], wu_ref[...], NT, preferred_element_type=jnp.float32)
    out_ref[...] = total.astype(jnp.bfloat16)


def plain_input_terms(gg, gu, wg, wu):
    rows, width = gg.shape
    depth = wg.shape[0]
    step = 512
    held = pl.BlockSpec((rows, width), lambda j: (0, 0))
    return pl.pallas_call(
        plain_input_kernel,
        grid=(depth // step,),
        in_specs=[
            held,
            held,
            pl.BlockSpec((step, width), lambda j: (j, 0)),
            pl.BlockSpec((step, width), lambda j: (j, 0)),
        ],
        out_specs=pl.BlockSpec((rows, step), lambda j: (0, j)),
        out_shape=jax.ShapeDtypeStruct((rows, depth), jnp.bfloat16),
        compiler_params=params(40),
        cost_estimate=cost(4 * rows * depth * width, 4 * depth * width),
        name="input_terms",
    )(gg, gu, wg, wu)


def plain_fisher_kernel(step, x_ref, gg_ref, gu_ref, fg_ref, fu_ref):
    half = x_ref.shape[0] // 2
    span = half // SEQS
    width = gg_ref.shape[1]

    def rows(ref, q, at):
        near = ref[pl.ds(q * span, span), at]
        far = ref[pl.ds(half + q * span, span), at]
        return jnp.concatenate([near, far], axis=0)

    xs = [rows(x_ref, q, slice(None)).T for q in range(SEQS)]
    for g_ref, f_ref in ((gg_ref, fg_ref), (gu_ref, fu_ref)):
        for c in range(width // step):
            at = pl.ds(c * step, step)
            total = None
            for q in range(SEQS):
                seq = jnp.dot(xs[q], rows(g_ref, q, at), preferred_element_type=jnp.float32)
                total = seq * seq if total is None else total + seq * seq
            f_ref[:, at] = (total * (1.0 / SEQS)).astype(jnp.bfloat16)


def plain_fisher(x, gg, gu):
    rows, depth = x.shape
    width = gg.shape[1]
    step = 512
    held = pl.BlockSpec((rows, width), lambda j: (0, 0))
    block = pl.BlockSpec((step, width), lambda j: (j, 0))
    return pl.pallas_call(
        functools.partial(plain_fisher_kernel, tile(width, 256)),
        grid=(depth // step,),
        in_specs=[pl.BlockSpec((rows, step), lambda j: (0, j)), held, held],
        out_specs=[block, block],
        out_shape=[jax.ShapeDtypeStruct((depth, width), jnp.bfloat16)] * 2,
        compiler_params=params(40),
        cost_estimate=cost(4 * rows * depth * width, 4 * depth * width),
        name="fisher",
    )(x, gg, gu)


def plain_part(size, tokens, grad_out, wg, wu, wd):
    chips = size // 2
    across = [[2 * i + c for i in range(chips)] for c in range(2)]
    pairs = [[2 * i, 2 * i + 1] for i in range(chips)]
    block, depth = tokens.shape

    def gather(rows):
        near = lax.all_gather(rows, "hid", axis=0, tiled=True, axis_index_groups=across)
        return lax.all_gather(near, "hid", axis=0, tiled=False, axis_index_groups=pairs)

    x = gather(tokens).reshape(-1, depth)
    dy = gather(grad_out).reshape(-1, depth)
    gate, up = plain_forward(x, wg, wu)
    gg, gu = plain_back(dy, wd, gate, up)
    terms = plain_input_terms(gg, gu, wg, wu).reshape(2, -1, depth)
    mine = lax.psum_scatter(
        terms, "hid", scatter_dimension=0, tiled=False, axis_index_groups=pairs
    )
    mine = lax.psum_scatter(
        mine, "hid", scatter_dimension=0, tiled=True, axis_index_groups=across
    )
    fg, fu = plain_fisher(x, gg, gu)
    return fg, fu, mine


def per_device(size, tokens, grad_out, wg, wu, wd):
    fits = tokens.shape[0] == 32 and wg.shape == (4096, 1792)
    if size == 2 * len(CYCLE) and fits:
        return ring_part(tokens, grad_out, wg, wu, wd)
    return plain_part(size, tokens, grad_out, wg, wu, wd)


def solution(mesh):
    rows = P(("adjust", "hid"), None)
    weights = P("adjust", "hid")
    return jax.shard_map(
        functools.partial(per_device, mesh.shape["hid"]),
        mesh=mesh,
        in_specs=(rows, rows, weights, weights, rows),
        out_specs=(weights, weights, rows),
        check_vma=False,
    )
```

```python
import functools

import jax
import jax.numpy as jnp
from jax import lax
from jax.experimental import pallas as pl
from jax.experimental.pallas import tpu as pltpu
from jax.sharding import PartitionSpec as P

SEQS = 2
MIB = 1 << 20
CYCLE = (0, 2, 4, 6, 7, 5, 3, 1)
NT = (((1,), (1,)), ((), ()))
BF16 = jnp.bfloat16
F32 = jnp.float32


def tile(size, want):
    return want if size % want == 0 else size


def params(mib):
    return pltpu.CompilerParams(vmem_limit_bytes=mib * MIB)


def cost(flops, read):
    return pl.CostEstimate(flops=flops, bytes_accessed=read, transcendentals=0)


def any_specs(values):
    return [pl.BlockSpec(memory_space=pl.ANY)] * len(values)


def hbm_specs(count):
    return [pl.BlockSpec(memory_space=pltpu.HBM)] * count


def held_specs(count):
    return [pl.BlockSpec(memory_space=pltpu.VMEM)] * count


def head_copies(wg_ref, wu_ref, first, step, head_ref, sems):
    cols = pl.ds(first * step, step)
    return [
        pltpu.make_async_copy(ref.at[:, cols], head_ref.at[i], sems.at[i])
        for i, ref in enumerate((wg_ref, wu_ref))
    ]


def bring_kernel(step, x_ref, dy_ref, wg_ref, wu_ref, x_out, dy_out, head_ref, sems):
    copies = head_copies(wg_ref, wu_ref, 0, step, head_ref, sems)
    for copy in copies:
        copy.start()
    x_out[...] = x_ref[...]
    dy_out[...] = dy_ref[...]
    for copy in copies:
        copy.wait()


def bring(x, dy, wg, wu, step):
    return pl.pallas_call(
        functools.partial(bring_kernel, step),
        in_specs=held_specs(2) + hbm_specs(2),
        out_specs=held_specs(3),
        out_shape=[jax.ShapeDtypeStruct(x.shape, BF16)] * 2
        + [jax.ShapeDtypeStruct((2, wg.shape[0], step), BF16)],
        scratch_shapes=[pltpu.SemaphoreType.DMA((2,))],
        compiler_params=params(46),
        cost_estimate=cost(0, 4 * wg.shape[0] * step),
        name="bring",
    )(x, dy, wg, wu)


def relay_kernel(in_ref, *rest):
    rest[-1][...] = in_ref[...]


def relay(value, after):
    return pl.pallas_call(
        relay_kernel,
        in_specs=held_specs(1) + any_specs(after),
        out_specs=pl.BlockSpec(memory_space=pltpu.VMEM),
        out_shape=jax.ShapeDtypeStruct(value.shape, value.dtype),
        compiler_params=params(4),
        cost_estimate=cost(0, 4 * value.size),
        name="relay",
    )(value, *after)


def pack_kernel(count, *refs):
    out_ref = refs[-1]
    start = 0
    for piece in refs[:count]:
        out_ref[pl.ds(start, piece.shape[0]), :] = piece[...]
        start += piece.shape[0]


def pack(pieces, after):
    depth = pieces[0].shape[1]
    rows = sum(piece.shape[0] for piece in pieces)
    whole = pl.BlockSpec(memory_space=pltpu.VMEM)
    return pl.pallas_call(
        functools.partial(pack_kernel, len(pieces)),
        in_specs=[whole] * len(pieces) + any_specs(after),
        out_specs=whole,
        out_shape=jax.ShapeDtypeStruct((rows, depth), BF16),
        compiler_params=params(8),
        cost_estimate=cost(0, 4 * rows * depth),
        name="pack",
    )(*pieces, *after)


def pack_turned_kernel(count, *refs):
    pieces, out_ref = refs[:count], refs[-1]
    step = 512
    for c in range(0, out_ref.shape[0], step):
        block = jnp.concatenate([piece[:, c : c + step] for piece in pieces], axis=0)
        out_ref[c : c + step, :] = block.T


def pack_turned(pieces, after):
    depth = pieces[0].shape[1]
    rows = sum(piece.shape[0] for piece in pieces)
    return pl.pallas_call(
        functools.partial(pack_turned_kernel, len(pieces)),
        in_specs=held_specs(len(pieces)) + any_specs(after),
        out_specs=pl.BlockSpec(memory_space=pltpu.VMEM),
        out_shape=jax.ShapeDtypeStruct((depth, rows), BF16),
        compiler_params=params(8),
        cost_estimate=cost(0, 4 * rows * depth),
        name="pack_turned",
    )(*pieces, *after)


def put_rows(spot_ref, side, value, out_ref, cols):
    chips = spot_ref.shape[0]
    row = value.shape[0] // chips
    for p in range(chips):
        start = pl.multiple_of(spot_ref[p] + side * chips // SEQS * row, row)
        out_ref[pl.ds(start, row), cols] = value[p * row : (p + 1) * row, :]


def arrange_kernel(spot_ref, near_ref, far_ref, *rest):
    for side, ref in enumerate((near_ref, far_ref)):
        put_rows(spot_ref, side, ref[...], rest[-1], slice(None))


def arrange(spot, near, far, after):
    rows, depth = near.shape
    return pl.pallas_call(
        arrange_kernel,
        in_specs=[pl.BlockSpec(memory_space=pltpu.SMEM)] + held_specs(2) + any_specs(after),
        out_specs=pl.BlockSpec(memory_space=pltpu.VMEM),
        out_shape=jax.ShapeDtypeStruct((2 * rows, depth), BF16),
        compiler_params=params(6),
        cost_estimate=cost(0, 8 * rows * depth),
        name="arrange",
    )(spot, near, far, *after)


def gate_up_kernel(first, step, near_ref, far_ref, head_ref, wg_ref, wu_ref, wd_ref, *rest):
    a_ref, b_ref, next_ref, w_buf, out_buf, sems, out_sems, next_sems = rest[-8:]
    rows = near_ref.shape[0]
    tiles = a_ref.shape[0] // step

    def fetch(t):
        slot = t % 2
        return head_copies(wg_ref, wu_ref, first + t, step, w_buf.at[slot], sems.at[slot])

    def fetch_next():
        if next_ref.shape[0] == 2:
            return head_copies(wg_ref, wu_ref, first + tiles, step, next_ref, next_sems)
        return [pltpu.make_async_copy(wd_ref.at[pl.ds(0, step), :], next_ref, next_sems.at[0])]

    def store(t):
        to = pl.ds(t * step, step)
        return [
            pltpu.make_async_copy(out_buf.at[t, i], ref.at[to, :], out_sems.at[t, i])
            for i, ref in enumerate((a_ref, b_ref))
        ]

    def begin(copies):
        for copy in copies:
            copy.start()

    def finish(copies):
        for copy in copies:
            copy.wait()

    for t in range(1, min(3, tiles)):
        begin(fetch(t))
    for t in range(tiles):
        if t:
            finish(fetch(t))
        if t == (max(tiles - 2, 0) if next_ref.shape[0] == 2 else tiles - 1):
            begin(fetch_next())
        w_ref = w_buf.at[t % 2] if t else head_ref
        for side, x_ref in enumerate((near_ref, far_ref)):
            gate = jnp.dot(x_ref[...], w_ref[0], preferred_element_type=F32)
            up = jnp.dot(x_ref[...], w_ref[1], preferred_element_type=F32)
            at = pl.ds(side * rows, rows)
            sigma = jax.nn.sigmoid(gate)
            out_buf[t, 0, :, at] = (up * sigma * (1.0 + gate * (1.0 - sigma))).T
            out_buf[t, 1, :, at] = (gate * sigma).T
        if t and t + 2 < tiles:
            begin(fetch(t + 2))
        begin(store(t))
    for t in range(tiles):
        finish(store(t))
    finish(fetch_next())


def gate_up(near, far, head, wg, wu, wd, first, count, step, grant, after):
    rows, depth = near.shape
    last = (first + count) * step == wg.shape[1]
    return pl.pallas_call(
        functools.partial(gate_up_kernel, first, step),
        in_specs=held_specs(3) + hbm_specs(3) + any_specs(after),
        out_specs=hbm_specs(2) + held_specs(1),
        out_shape=[jax.ShapeDtypeStruct((count * step, 2 * rows), F32)] * 2
        + [jax.ShapeDtypeStruct((step, depth) if last else (2, depth, step), BF16)],
        scratch_shapes=[
            pltpu.VMEM((2, 2, depth, step), BF16),
            pltpu.VMEM((count, 2, step, 2 * rows), F32),
            pltpu.SemaphoreType.DMA((2, 2)),
            pltpu.SemaphoreType.DMA((count, 2)),
            pltpu.SemaphoreType.DMA((2,)),
        ],
        compiler_params=params(grant),
        cost_estimate=cost(8 * rows * depth * count * step, 4 * depth * count * step),
        name="gate_up",
    )(near, far, head, wg, wu, wd, *after)


def back_kernel(
    step, deep, pieces, spot_ref, near_ref, far_ref, head_ref, wg_ref, wu_ref, wd_ref, *refs
):
    a_refs, b_refs = refs[:pieces], refs[pieces : 2 * pieces]
    ggs_ref, gus_ref, own_ref, sent_ref, g_ref = refs[2 * pieces : 2 * pieces + 5]
    wd_buf, w_buf, factor_buf, sems, w_sems, factor_sems = refs[2 * pieces + 5 :]
    width = wg_ref.shape[1]
    rows = near_ref.shape[1]
    tiles = wd_ref.shape[0] // step

    def fetch(t):
        at = pl.ds(pl.multiple_of(t * step, step), step)
        slot = lax.rem(t, 2)
        return pltpu.make_async_copy(wd_ref.at[at, :], wd_buf.at[slot], sems.at[slot])

    def fetch_rows(i):
        at = pl.ds(pl.multiple_of(i * deep, deep), deep)
        slot = lax.rem(i, 2)
        return [
            pltpu.make_async_copy(
                w_ref.at[at, :], w_buf.at[slot, :, pl.ds(k * width, width)], w_sems.at[slot, k]
            )
            for k, w_ref in enumerate((wg_ref, wu_ref))
        ]

    starts = [0]
    for a_ref in a_refs:
        starts.append(starts[-1] + a_ref.shape[0])

    def fetch_factors(p):
        at = pl.ds(starts[p], starts[p + 1] - starts[p])
        return [
            pltpu.make_async_copy(ref, factor_buf.at[k, at, :], factor_sems.at[k, p])
            for k, ref in enumerate((a_refs[p], b_refs[p]))
        ]

    def hidden_tile(t, wd):
        cols = pl.ds(pl.multiple_of(t * step, step), step)
        for side, dy_ref in enumerate((near_ref, far_ref)):
            hidden = jnp.dot(wd, dy_ref[...], preferred_element_type=F32)
            at = pl.ds(side * rows, rows)
            for f, gs_ref in enumerate((ggs_ref, gus_ref)):
                grad = (hidden * factor_buf[f, cols, at]).astype(BF16)
                to = pl.multiple_of(t * step + f * width, step)
                g_ref[pl.ds(to, step), at] = grad
                put_rows(spot_ref, side, grad.T, gs_ref, cols)

    blocks = wg_ref.shape[0] // deep
    for copy in fetch_factors(0):
        copy.start()
    for t in range(1, min(3, tiles)):
        fetch(jnp.int32(t)).start()
    for p in range(pieces):
        if p + 1 < pieces:
            for copy in fetch_factors(p + 1):
                copy.start()
        else:
            for i in range(2):
                for copy in fetch_rows(jnp.int32(i)):
                    copy.start()
        for copy in fetch_factors(p):
            copy.wait()

        if p == 0:
            hidden_tile(0, head_ref[...])

        @pl.loop(max(starts[p] // step, 1), starts[p + 1] // step)
        def _(t):
            fetch(t).wait()
            hidden_tile(t, wd_buf[lax.rem(t, 2)])

            @pl.when(t + 2 < tiles)
            def _():
                fetch(t + 2).start()

    @pl.loop(0, blocks)
    def _(i):
        at = pl.ds(pl.multiple_of(i * deep, deep), deep)
        slot = lax.rem(i, 2)
        for copy in fetch_rows(i):
            copy.wait()
        for side, out_ref in enumerate((own_ref, sent_ref)):
            of = pl.ds(side * rows, rows)
            total = jnp.dot(w_buf[slot], g_ref[:, of], preferred_element_type=F32)
            out_ref[:, at] = total.astype(BF16).T

        @pl.when(i + 2 < blocks)
        def _():
            for copy in fetch_rows(i + 2):
                copy.start()


def back(spot, near, far, head, wg, wu, wd, factors):
    depth, rows = near.shape
    width = wd.shape[0]
    step = tile(width, 256)
    a = [pair[0] for pair in factors]
    b = [pair[1] for pair in factors]
    return pl.pallas_call(
        functools.partial(back_kernel, step, 512, len(a)),
        in_specs=[pl.BlockSpec(memory_space=pltpu.SMEM)]
        + held_specs(3)
        + hbm_specs(3)
        + any_specs(a + b),
        out_specs=held_specs(4),
        out_shape=[jax.ShapeDtypeStruct((2 * rows, width), BF16)] * 2
        + [jax.ShapeDtypeStruct((rows, depth), BF16)] * 2,
        scratch_shapes=[
            pltpu.VMEM((2 * width, 2 * rows), BF16),
            pltpu.VMEM((2, step, depth), BF16),
            pltpu.VMEM((2, 512, 2 * width), BF16),
            pltpu.VMEM((2, width, 2 * rows), F32),
            pltpu.SemaphoreType.DMA((2,)),
            pltpu.SemaphoreType.DMA((2, 2)),
            pltpu.SemaphoreType.DMA((2, len(a))),
        ],
        compiler_params=params(26),
        cost_estimate=cost(12 * rows * depth * width, 6 * depth * width),
        name="hidden_back",
    )(spot, near, far, head, wg, wu, wd, *a, *b)


def fold_kernel(cuts, *refs):
    count = len(cuts)
    outs = refs[-count:]
    for i, (at, got_at) in enumerate(cuts):
        own_ref, near_ref, got_ref = refs[3 * i : 3 * i + 3]
        out_ref = outs[i]
        out_ref[...] = (own_ref[at, :].astype(F32) + near_ref[at, :].astype(F32)).astype(BF16)
        if got_at is not None:
            total = own_ref[got_at, :].astype(F32) + near_ref[got_at, :].astype(F32)
            out_ref[got_at, :] = (total + got_ref[...].astype(F32)).astype(BF16)


def fold(own, near, row, sends, after):
    depth = own.shape[1]
    operands, specs, shapes, cuts = [], [], [], []
    for p, at, got_at, got in sends:
        block = pl.BlockSpec((row, depth), lambda i, p=p: (p, 0))
        got = near if got is None else got
        size = got.shape[0] if got_at is not None else row
        operands += [own, near, got]
        specs += [block, block, pl.BlockSpec((size, depth), lambda i: (0, 0))]
        shapes.append(jax.ShapeDtypeStruct((at.size, depth), BF16))
        cuts.append((at, got_at))
    return pl.pallas_call(
        functools.partial(fold_kernel, cuts),
        grid=(1,),
        in_specs=specs + any_specs(after),
        out_specs=[pl.BlockSpec(shape.shape, lambda i: (0, 0)) for shape in shapes],
        out_shape=shapes,
        compiler_params=params(24),
        cost_estimate=cost(0, 16 * row * depth),
        name="fold",
    )(*operands, *after)


def last_kernel(own_ref, near_ref, r_ref, l_ref, out_ref):
    total = own_ref[...].astype(F32) + near_ref[...].astype(F32)
    out_ref[...] = (total + r_ref[...].astype(F32) + l_ref[...].astype(F32)).astype(BF16)


def last(own, near, r, l):
    block = pl.BlockSpec(r.shape, lambda i: (0, 0))
    return pl.pallas_call(
        last_kernel,
        grid=(1,),
        in_specs=[block] * 4,
        out_specs=block,
        out_shape=jax.ShapeDtypeStruct(r.shape, BF16),
        compiler_params=params(24),
        cost_estimate=cost(0, 12 * r.size),
        name="last",
    )(own, near, r, l)


def fisher_kernel(step, x_ref, gg_ref, gu_ref, *rest):
    fg_ref, fu_ref, done_ref = rest[-3:]
    done_ref[...] = jnp.zeros_like(done_ref)
    span = x_ref.shape[0] // SEQS
    seqs = [pl.ds(q * span, span) for q in range(SEQS)]
    cols = [x_ref[at, :].T for at in seqs]
    for g_ref, f_ref in ((gg_ref, fg_ref), (gu_ref, fu_ref)):
        for c in range(g_ref.shape[1] // step):
            at = pl.ds(c * step, step)
            total = None
            for q in range(SEQS):
                seq = jnp.dot(cols[q], g_ref[seqs[q], at], preferred_element_type=F32)
                total = seq * seq if total is None else total + seq * seq
            f_ref[:, at] = (total * (1.0 / SEQS)).astype(BF16)


def fisher(x, gg, gu, first, count, step, held, after):
    rows, depth = x.shape
    width = gg.shape[1]
    block = pl.BlockSpec((step, width), lambda j: (first + j, 0))
    return pl.pallas_call(
        functools.partial(fisher_kernel, tile(width, 896)),
        grid=(count,),
        in_specs=[pl.BlockSpec((rows, step), lambda j: (0, first + j))]
        + held_specs(2)
        + any_specs((*held, *after)),
        out_specs=[block, block, pl.BlockSpec((8, 128), lambda j: (0, 0))],
        out_shape=[jax.ShapeDtypeStruct((depth, width), BF16)] * 2
        + [jax.ShapeDtypeStruct((8, 128), F32)],
        input_output_aliases={3 + i: i for i in range(len(held))},
        compiler_params=params(40),
        cost_estimate=cost(4 * rows * step * count * width, 4 * step * count * width),
        name="fisher",
    )(x, gg, gu, *held, *after)


def ring_part(tokens, grad_out, wg, wu, wd):
    chips = len(CYCLE)
    far = chips // 2
    row, depth = tokens.shape
    width = wg.shape[1]
    links = [(CYCLE[i], CYCLE[(i + 1) % chips]) for i in range(chips)]
    to_right = [(2 * a + c, 2 * b + c) for a, b in links for c in range(2)]
    to_left = [(b, a) for a, b in to_right]
    across = [(2 * i + c, 2 * i + 1 - c) for i in range(chips) for c in range(2)]

    def right(value):
        return lax.ppermute(value, "hid", to_right)

    def left(value):
        return lax.ppermute(value, "hid", to_left)

    def swap(value):
        return lax.ppermute(value, "hid", across)

    cycle = jnp.array(CYCLE, jnp.int32)
    where = jnp.array([CYCLE.index(c) for c in range(chips)], jnp.int32)
    around = jnp.arange(chips, dtype=jnp.int32)
    chip = cycle[(where[lax.axis_index("hid") // 2] - around) % chips]
    span = chips // SEQS
    spot = (chip // span * 2 * span + chip % span) * row

    def both(r, l, after=(), ends=False):
        (r, l), _ = lax.optimization_barrier(((r, l), after))
        if ends:
            r, l = r[: row // 2], l[row // 2 :]
        return right(r), left(l)

    def blocks(own, rounds):
        return [own] + [r for r, _ in rounds] + [l for _, l in rounds[::-1]]

    lane = tile(width, 256)
    tiles = width // lane
    cuts = [0, 2, 5, 7]

    def piece(i, head, after):
        grant = (30, 26, 26)[i]
        count = cuts[i + 1] - cuts[i]
        a, b, head = gate_up(
            near_x, far_x, head, wg, wu, wd, cuts[i], count, lane, grant, after
        )
        return (a, b), head

    own_x, own_dy, head = bring(tokens, grad_out, wg, wu, lane)
    in_x = [both(tokens, tokens)]
    in_x.append(both(*in_x[-1], (own_x, head)))
    in_dy = [both(own_dy, own_dy, in_x[0])]
    for _ in range(3, far):
        in_x.append(both(*in_x[-1]))
        in_dy.append(both(*in_dy[-1]))
    in_x.append(both(*in_x[-1], in_dy[0], True))
    near_x = pack(blocks(own_x, in_x), (spot, *in_dy[-1]))
    far_x = swap(near_x)

    in_dy.append(both(*in_dy[-1], in_x[-2]))
    some, head = piece(0, head, in_dy[-2])
    factors = [some]
    in_dy.append(both(*in_dy[-1], some, True))
    some, head = piece(1, head, in_dy[-2])
    factors.append(some)
    near_dy = pack_turned(blocks(own_dy, in_dy), some)
    far_dy = swap(near_dy)
    some, head = piece(2, head, (near_dy,))
    factors.append(some)
    gg, gu, own, sent = back(spot, near_dy, far_dy, head, wg, wu, wd, factors)
    x = arrange(spot, near_x, far_x, (own,))

    near = swap(sent)
    full, head, tail = pl.ds(0, row), pl.ds(0, row // 2), pl.ds(row // 2, row // 2)
    step = 256
    counts = [2, 3, 4, 4, 3]
    held, first = (), 0
    r = l = None
    ready = ()
    for k in range(far, 0, -1):
        *held, done = fisher(x, gg, gu, first, counts[far - k], step, held, ready)
        first += counts[far - k]
        if k == far:
            sends = [(far, head, None, None), (far, tail, None, None)]
        elif k == far - 1:
            sends = [(chips - k, full, head, r), (k, full, tail, l)]
        else:
            sends = [(chips - k, full, full, r), (k, full, full, l)]
        ready = fold(own, near, row, sends, (done,))
        r, l = right(ready[0]), left(ready[1])
    fg, fu, _ = fisher(x, gg, gu, first, counts[far], step, held, ready)
    mine = last(own, near, r, l)
    return fg, fu, mine


def plain_forward_kernel(x_ref, wg_ref, wu_ref, gate_ref, up_ref):
    x = x_ref[...]
    gate_ref[...] = jnp.dot(x, wg_ref[...], preferred_element_type=jnp.float32)
    up_ref[...] = jnp.dot(x, wu_ref[...], preferred_element_type=jnp.float32)


def plain_forward(x, wg, wu):
    rows, depth = x.shape
    width = wg.shape[1]
    step = tile(width, 256)
    return pl.pallas_call(
        plain_forward_kernel,
        grid=(width // step,),
        in_specs=[
            pl.BlockSpec((rows, depth), lambda j: (0, 0)),
            pl.BlockSpec((depth, step), lambda j: (0, j)),
            pl.BlockSpec((depth, step), lambda j: (0, j)),
        ],
        out_specs=[pl.BlockSpec((rows, step), lambda j: (0, j))] * 2,
        out_shape=[jax.ShapeDtypeStruct((rows, width), jnp.float32)] * 2,
        compiler_params=params(40),
        cost_estimate=cost(4 * rows * depth * width, 4 * depth * width),
        name="gate_up",
    )(x, wg, wu)


def plain_back_kernel(parts, dy_ref, wd_ref, gate_ref, up_ref, gg_ref, gu_ref):
    rows = dy_ref.shape[0] // parts
    for p in range(parts):
        at = pl.ds(p * rows, rows)
        hidden = lax.dot_general(dy_ref[at, :], wd_ref[...], NT, preferred_element_type=jnp.float32)
        gate = gate_ref[at, :]
        sigma = jax.nn.sigmoid(gate)
        both = hidden * sigma
        gg_ref[at, :] = (both * up_ref[at, :] * (1.0 + gate * (1.0 - sigma))).astype(jnp.bfloat16)
        gu_ref[at, :] = (both * gate).astype(jnp.bfloat16)


def plain_back(dy, wd, gate, up):
    rows, depth = dy.shape
    width = wd.shape[0]
    step = tile(width, 256)
    column = pl.BlockSpec((rows, step), lambda j: (0, j))
    return pl.pallas_call(
        functools.partial(plain_back_kernel, 2),
        grid=(width // step,),
        in_specs=[
            pl.BlockSpec((rows, depth), lambda j: (0, 0)),
            pl.BlockSpec((step, depth), lambda j: (j, 0)),
            column,
            column,
        ],
        out_specs=[column, column],
        out_shape=[jax.ShapeDtypeStruct((rows, width), jnp.bfloat16)] * 2,
        compiler_params=params(40),
        cost_estimate=cost(2 * rows * depth * width, 2 * depth * width),
        name="hidden_back",
    )(dy, wd, gate, up)


def plain_input_kernel(gg_ref, gu_ref, wg_ref, wu_ref, out_ref):
    total = lax.dot_general(gg_ref[...], wg_ref[...], NT, preferred_element_type=jnp.float32)
    total += lax.dot_general(gu_ref[...], wu_ref[...], NT, preferred_element_type=jnp.float32)
    out_ref[...] = total.astype(jnp.bfloat16)


def plain_input_terms(gg, gu, wg, wu):
    rows, width = gg.shape
    depth = wg.shape[0]
    step = 512
    held = pl.BlockSpec((rows, width), lambda j: (0, 0))
    return pl.pallas_call(
        plain_input_kernel,
        grid=(depth // step,),
        in_specs=[
            held,
            held,
            pl.BlockSpec((step, width), lambda j: (j, 0)),
            pl.BlockSpec((step, width), lambda j: (j, 0)),
        ],
        out_specs=pl.BlockSpec((rows, step), lambda j: (0, j)),
        out_shape=jax.ShapeDtypeStruct((rows, depth), jnp.bfloat16),
        compiler_params=params(40),
        cost_estimate=cost(4 * rows * depth * width, 4 * depth * width),
        name="input_terms",
    )(gg, gu, wg, wu)


def plain_fisher_kernel(step, x_ref, gg_ref, gu_ref, fg_ref, fu_ref):
    half = x_ref.shape[0] // 2
    span = half // SEQS
    width = gg_ref.shape[1]

    def rows(ref, q, at):
        near = ref[pl.ds(q * span, span), at]
        far = ref[pl.ds(half + q * span, span), at]
        return jnp.concatenate([near, far], axis=0)

    xs = [rows(x_ref, q, slice(None)).T for q in range(SEQS)]
    for g_ref, f_ref in ((gg_ref, fg_ref), (gu_ref, fu_ref)):
        for c in range(width // step):
            at = pl.ds(c * step, step)
            total = None
            for q in range(SEQS):
                seq = jnp.dot(xs[q], rows(g_ref, q, at), preferred_element_type=jnp.float32)
                total = seq * seq if total is None else total + seq * seq
            f_ref[:, at] = (total * (1.0 / SEQS)).astype(jnp.bfloat16)


def plain_fisher(x, gg, gu):
    rows, depth = x.shape
    width = gg.shape[1]
    step = 512
    held = pl.BlockSpec((rows, width), lambda j: (0, 0))
    block = pl.BlockSpec((step, width), lambda j: (j, 0))
    return pl.pallas_call(
        functools.partial(plain_fisher_kernel, tile(width, 256)),
        grid=(depth // step,),
        in_specs=[pl.BlockSpec((rows, step), lambda j: (0, j)), held, held],
        out_specs=[block, block],
        out_shape=[jax.ShapeDtypeStruct((depth, width), jnp.bfloat16)] * 2,
        compiler_params=params(40),
        cost_estimate=cost(4 * rows * depth * width, 4 * depth * width),
        name="fisher",
    )(x, gg, gu)


def plain_part(size, tokens, grad_out, wg, wu, wd):
    chips = size // 2
    across = [[2 * i + c for i in range(chips)] for c in range(2)]
    pairs = [[2 * i, 2 * i + 1] for i in range(chips)]
    block, depth = tokens.shape

    def gather(rows):
        near = lax.all_gather(rows, "hid", axis=0, tiled=True, axis_index_groups=across)
        return lax.all_gather(near, "hid", axis=0, tiled=False, axis_index_groups=pairs)

    x = gather(tokens).reshape(-1, depth)
    dy = gather(grad_out).reshape(-1, depth)
    gate, up = plain_forward(x, wg, wu)
    gg, gu = plain_back(dy, wd, gate, up)
    terms = plain_input_terms(gg, gu, wg, wu).reshape(2, -1, depth)
    mine = lax.psum_scatter(
        terms, "hid", scatter_dimension=0, tiled=False, axis_index_groups=pairs
    )
    mine = lax.psum_scatter(
        mine, "hid", scatter_dimension=0, tiled=True, axis_index_groups=across
    )
    fg, fu = plain_fisher(x, gg, gu)
    return fg, fu, mine


def per_device(size, tokens, grad_out, wg, wu, wd):
    fits = tokens.shape[0] == 32 and wg.shape == (4096, 1792)
    if size == 2 * len(CYCLE) and fits:
        return ring_part(tokens, grad_out, wg, wu, wd)
    return plain_part(size, tokens, grad_out, wg, wu, wd)


def solution(mesh):
    rows = P(("adjust", "hid"), None)
    weights = P("adjust", "hid")
    return jax.shard_map(
        functools.partial(per_device, mesh.shape["hid"]),
        mesh=mesh,
        in_specs=(rows, rows, weights, weights, rows),
        out_specs=(weights, weights, rows),
        check_vma=False,
    )
```
